32 devices in a mesh: groups: 2 (over y), seq: 4 (over z), batch: 2 (over x), chan: 2 (over core).
Axes of the slice: x: 2, y: 2, z: 4, core: 2. Of those that a mesh axis runs over, the one named last changes fastest.
Arguments:
- query_vectors: bfloat16 [16, 256, 768], P(('groups', 'batch'), 'seq', 'chan'), parts along dimension 0, may hold values from -6 to 6
- key_vectors: bfloat16 [16, 256, 768], P(('groups', 'batch'), 'seq', 'chan'), parts along dimension 0, may hold values from -6 to 6
- value_vectors: bfloat16 [16, 256, 768], P(('groups', 'batch'), 'seq', 'chan'), parts along dimension 0, may hold values from -6 to 6
- hidden: bfloat16 [16, 256, 768], P(('groups', 'batch'), 'seq', 'chan'), parts along dimension 0, may hold values from -6 to 6
- cotangent: bfloat16 [16, 256, 768], P(('groups', 'batch'), 'seq', 'chan'), parts along dimension 0, may hold values from -6 to 6
- conv_weight: bfloat16 [768, 3, 768], P(None, None, 'chan'), may hold values from -0.125 to 0.125
Outputs:
- query_grad: bfloat16 [16, 256, 768], P(('groups', 'batch'), 'seq', 'chan'), parts along dimension 0
- key_grad: bfloat16 [16, 256, 768], P(('groups', 'batch'), 'seq', 'chan'), parts along dimension 0
- value_grad: bfloat16 [16, 256, 768], P(('groups', 'batch'), 'seq', 'chan'), parts along dimension 0
- hidden_grad: bfloat16 [16, 256, 768], P(('groups', 'batch'), 'seq', 'chan'), parts along dimension 0
- weight_grad: float32 [1536, 3, 768], P(('groups', 'seq', 'batch'), None, 'chan'), parts along dimension 0
The draws below stay inside these ranges and needn't reach their ends.
There are 2 independent parts, one for each index of `groups`. The reference program is written for one: setup_inputs(seed, part) draws one part's arguments, and reference() takes and returns one part's arrays. A program takes and returns all parts, laid end to end along the dimension named above; an argument that names none is the same for every part. Nothing has to cross between parts.
All inputs are finite; a program needn't handle non-finite values.
Results may differ from the reference program's by a relative error of at most 0.025.
Values may be sent and summed in bfloat16 or wider, within the bound.
No kernel may reach another device: no remote copies, remote signals or barrier semaphores. Data moves between devices by JAX's collectives and lax.ppermute only.
A program may use at most 64 MiB of HBM per device.

```python
import math
import jax
import jax.numpy as jnp
from jax import lax

HD = 96
HEADS = 8
C = 768
TAPS = 3
BATCH = 8
LEN = 256
DILATION = 64
N_CHAN = 2


def drawn_pair(key):
    shape = (BATCH, LEN, C)
    query_key = jax.random.fold_in(key, 101)
    key_key = jax.random.fold_in(key, 202)
    query_arr = jnp.clip(jax.random.normal(query_key, shape, jnp.float32), -6.0, 6.0)
    key_arr = jnp.clip(jax.random.normal(key_key, shape, jnp.float32), -6.0, 6.0)
    return (query_arr, key_arr)


def draw_query_vectors(key, part):
    return drawn_pair(key)[0].astype(jnp.bfloat16)


def draw_key_vectors(key, part):
    return drawn_pair(key)[1].astype(jnp.bfloat16)


def steps_of(rng, dims, pieces, smallest, largest):
    gain = 1.0
    for position, parts in pieces:
        heights = jax.random.uniform(jax.random.fold_in(jax.random.fold_in(rng, 6), position), (parts,), jnp.float32, smallest / len(pieces), largest / len(pieces))
        gain = gain * jnp.repeat(jnp.exp(heights), dims[position] // parts).reshape((-1,) + (1,) * (len(dims) - 1 - position))
    return gain


def gaussian(key, dims, scale, bound, split=(), dtype=jnp.bfloat16):
    values = jax.random.normal(key, dims, jnp.float32) * scale
    if len(split) > 0:
        values = steps_of(key, dims, split, -0.22, 0.18) * values
    return jnp.clip(values, min=-bound, max=bound).astype(dtype)


def setup_inputs(seed: int = 0, part: int = 0) -> dict:
    streams_of = jax.random.split(jax.random.key(seed), 7)
    part_keys = jax.random.split(jax.random.fold_in(streams_of[6], part), 7)
    query_vectors = draw_query_vectors(jax.random.fold_in(jax.random.fold_in(streams_of[6], part), 71), part)
    key_vectors = draw_key_vectors(jax.random.fold_in(jax.random.fold_in(streams_of[6], part), 71), part)
    value_vectors = gaussian(part_keys[2], (BATCH, LEN, C), 1.0, 6.0, ((0, 2), (1, 4), (2, 2)))
    hidden = gaussian(part_keys[3], (BATCH, LEN, C), 1.0, 6.0, ((0, 2), (1, 4), (2, 2)))
    cotangent = gaussian(part_keys[4], (BATCH, LEN, C), 1.0, 6.0, ((0, 2), (1, 4), (2, 2)))
    conv_weight = gaussian(streams_of[5], (C, TAPS, C), (TAPS * C) ** -0.5, 0.125, ((2, 2),))
    return {"query_vectors": query_vectors, "key_vectors": key_vectors, "value_vectors": value_vectors, "hidden": hidden, "cotangent": cotangent, "conv_weight": conv_weight}


def tanh_gelu(signal):
    inner_arg = 0.7978845608 * (signal + 0.044715 * signal * signal * signal)
    return 0.5 * signal * (1.0 + jnp.tanh(inner_arg))

def gelu_slope(signal):
    inner_arg = 0.7978845608 * (signal + 0.044715 * signal * signal * signal)
    hyper = jnp.tanh(inner_arg)
    return 0.5 * (1.0 + hyper) + 0.5 * signal * (1.0 - hyper * hyper) * 0.7978845608 * (1.0 + 3.0 * 0.044715 * signal * signal)

def move_rows(signal, offset):
    filler = jnp.zeros_like(signal[:, :abs(offset)])
    if offset > 0:
        return jnp.concatenate([signal[:, offset:], filler], axis=1)
    return jnp.concatenate([filler, signal[:, :offset]], axis=1)

def head_backward(operands):
    query_rows, key_rows, value_rows, grad_rows = operands
    score_scale = 1.0 / math.sqrt(HD)
    scores = jnp.dot(query_rows, key_rows.T, preferred_element_type=jnp.float32) * score_scale
    row_max = lax.optimization_barrier(jnp.max(scores, axis=-1, keepdims=True))
    raised = jnp.exp(scores - row_max)
    probability = raised / lax.optimization_barrier(jnp.sum(raised, axis=-1, keepdims=True))
    prob_b = probability.astype(jnp.bfloat16)
    value_grad = jnp.dot(prob_b.T, grad_rows, preferred_element_type=jnp.float32).astype(jnp.bfloat16)
    d_prob = jnp.dot(grad_rows, value_rows.T, preferred_element_type=jnp.float32)
    row_total = lax.optimization_barrier(jnp.sum(probability * d_prob, axis=-1, keepdims=True))
    d_score = (probability * (d_prob - row_total)).astype(jnp.bfloat16)
    query_grad = (score_scale * jnp.dot(d_score, key_rows, preferred_element_type=jnp.float32)).astype(jnp.bfloat16)
    key_grad = (score_scale * jnp.dot(d_score.T, query_rows, preferred_element_type=jnp.float32)).astype(jnp.bfloat16)
    return (query_grad, key_grad, value_grad)

def split_heads(signal):
    return signal.reshape(BATCH, LEN, HEADS, HD).transpose(0, 2, 1, 3).reshape(BATCH * HEADS, LEN, HD)

def merge_heads(signal):
    return signal.reshape(BATCH, HEADS, LEN, HD).transpose(0, 2, 1, 3).reshape(BATCH, LEN, C)

def reference(query_vectors, key_vectors, value_vectors, hidden, cotangent, conv_weight):
    hidden_f = hidden.astype(jnp.float32)
    activation = tanh_gelu(hidden_f).astype(jnp.bfloat16)
    cot_after = move_rows(cotangent, DILATION)
    cot_before = move_rows(cotangent, -DILATION)
    shifted_taps = [cot_after, cotangent, cot_before]
    flat_act = activation.reshape(-1, C)
    factor = 1.0 / math.sqrt(BATCH * LEN)
    weight_grad = jnp.stack([factor * jnp.dot(flat_act.T, shifted.reshape(-1, C), preferred_element_type=jnp.float32) for shifted in shifted_taps], axis=1)
    half_width = C // N_CHAN
    back_sum = jnp.zeros((BATCH * LEN, C), jnp.float32)
    for portion in range(N_CHAN):
        first_col = portion * half_width
        term = jnp.zeros((BATCH * LEN, C), jnp.float32)
        for tap_index in range(TAPS):
            shifted = shifted_taps[tap_index][:, :, first_col:first_col + half_width].reshape(-1, half_width)
            weight_part = conv_weight[:, tap_index, first_col:first_col + half_width]
            term = term + jnp.dot(shifted, weight_part.T, preferred_element_type=jnp.float32)
        rounded = lax.optimization_barrier(term.astype(jnp.bfloat16))
        back_sum = back_sum + rounded.astype(jnp.float32)
    back_sum = back_sum.reshape(BATCH, LEN, C)
    hidden_grad = (cotangent.astype(jnp.float32) + back_sum * gelu_slope(hidden_f)).astype(jnp.bfloat16)
    query_grad, key_grad, value_grad = lax.map(head_backward, (split_heads(query_vectors), split_heads(key_vectors), split_heads(value_vectors), split_heads(hidden_grad)))
    return (merge_heads(query_grad), merge_heads(key_grad), merge_heads(value_grad), hidden_grad, weight_grad)
```

```python
import functools
import math

import jax
import jax.numpy as jnp
from jax import lax
from jax.experimental import pallas as pl
from jax.experimental.pallas import tpu as pltpu
from jax.sharding import PartitionSpec as P

HD = 96
BF = jnp.bfloat16
F32 = jnp.float32
VMEM_LIMIT = 40 * 1024 * 1024


def tanh_gelu(signal):
    inner_arg = 0.7978845608 * (signal + 0.044715 * signal * signal * signal)
    return 0.5 * signal * (1.0 + jnp.tanh(inner_arg))


def gelu_slope(signal):
    inner_arg = 0.7978845608 * (signal + 0.044715 * signal * signal * signal)
    hyper = jnp.tanh(inner_arg)
    return 0.5 * (1.0 + hyper) + 0.5 * signal * (1.0 - hyper * hyper) * 0.7978845608 * (
        1.0 + 3.0 * 0.044715 * signal * signal
    )


def kernel_call(body, outs, flops=0, transcendentals=0, name=None, scratch=()):
    vmem = pl.BlockSpec(memory_space=pltpu.VMEM)

    def call(*args):
        moved = sum(math.prod(a.shape) * a.dtype.itemsize for a in args)
        moved += sum(math.prod(o.shape) * o.dtype.itemsize for o in outs)
        return pl.pallas_call(
            body,
            out_shape=list(outs),
            in_specs=[vmem] * len(args),
            out_specs=[vmem] * len(outs),
            scratch_shapes=list(scratch),
            compiler_params=pltpu.CompilerParams(vmem_limit_bytes=VMEM_LIMIT),
            cost_estimate=pl.CostEstimate(
                flops=flops, bytes_accessed=moved, transcendentals=transcendentals
            ),
            name=name,
        )(*args)

    return call


def shape(dims, dtype=BF):
    return jax.ShapeDtypeStruct(dims, dtype)


def prepare_kernel(count, q_ref, k_ref, v_ref, h_ref, *outs):
    s = lax.axis_index("seq")
    for d in range(count):
        b = lax.rem(s + d, count)
        for j, ref in enumerate((q_ref, k_ref, v_ref)):
            outs[d][j] = ref[b]
    act_refs = outs[count : count + 2]
    blocks, rows, width = h_ref.shape
    act = tanh_gelu(h_ref[...].astype(F32)).reshape(blocks * rows, width)
    act_t = act.T.astype(BF)
    half = width // 2
    first = lax.rem(s, 2) == 0
    low, high = act_t[:half], act_t[half:]
    act_refs[0][...] = jnp.where(first, low, high)
    act_refs[1][...] = jnp.where(first, high, low)


def conv_kernel(cot_ref, left_ref, right_ref, w_ref, mine_ref, other_ref):
    c = lax.axis_index("chan")
    blocks, rows, width = cot_ref.shape
    taps = [r[...].reshape(blocks * rows, width) for r in (right_ref, cot_ref, left_ref)]
    for out_ref, side in ((other_ref, 1 - c), (mine_ref, c)):
        start = pl.multiple_of(side * width, width)
        total = None
        for t in range(3):
            term = lax.dot_general(
                taps[t],
                w_ref[t, pl.ds(start, width), :],
                (((1,), (1,)), ((), ())),
                preferred_element_type=F32,
            )
            total = term if total is None else total + term
        out_ref[...] = total.astype(BF).reshape(blocks, rows, width)


def grad_kernel(count, cot_ref, h_ref, mine_ref, other_ref, grad_ref, *pieces):
    s = lax.axis_index("seq")
    back = mine_ref[...].astype(F32) + other_ref[...].astype(F32)
    slope = gelu_slope(h_ref[...].astype(F32))
    grad_ref[...] = (cot_ref[...].astype(F32) + back * slope).astype(BF)
    for d in range(count):
        pieces[d][...] = grad_ref[lax.rem(s + d, count)]


def attention_kernel(count, *refs):
    qkv = refs[:count]
    grads = refs[count : 2 * count]
    outs = refs[2 * count :]
    rows, width = grads[0].shape
    scale = 1.0 / math.sqrt(HD)
    query, key, value = (
        jnp.concatenate([qkv[d][j] for d in range(count)], axis=0) for j in range(3)
    )
    grad = jnp.concatenate([grads[d][...] for d in range(count)], axis=0)
    nt = (((1,), (1,)), ((), ()))
    nn = (((1,), (0,)), ((), ()))
    tn = (((0,), (0,)), ((), ()))
    dot = functools.partial(lax.dot_general, preferred_element_type=F32)
    results = ([], [], [])
    for h in range(width // HD):
        cols = slice(h * HD, (h + 1) * HD)
        q, k, v, g = query[:, cols], key[:, cols], value[:, cols], grad[:, cols]
        scores = dot(k, q, nt) * scale
        raised = jnp.exp(scores - jnp.max(scores, axis=0, keepdims=True))
        prob = raised * (1.0 / jnp.sum(raised, axis=0, keepdims=True))
        d_prob = dot(v, g, nt)
        row_total = jnp.sum(prob * d_prob, axis=0, keepdims=True)
        d_score = (prob * (d_prob - row_total)).astype(BF)
        results[0].append((dot(d_score, k, tn) * scale).astype(BF))
        results[1].append((dot(d_score, q, nn) * scale).astype(BF))
        results[2].append(dot(prob.astype(BF), g, nn).astype(BF))
    for j in range(3):
        whole = jnp.concatenate(results[j], axis=1)
        for d in range(count):
            outs[d][j] = whole[d * rows : (d + 1) * rows]


def weight_kernel(count, factor, *refs):
    acts, cots = refs[:4], refs[4 : 4 + 2 * count - 1]
    own_ref, sent_ref, act_buf, cot_buf = refs[4 + 2 * count - 1 :]
    s = lax.axis_index("seq")
    c = lax.axis_index("chan")
    b = lax.axis_index("batch")
    for k in range(2):
        for side, piece in ((c, acts[k]), (1 - c, acts[2 + k])):
            act_buf[2 * side + lax.rem(s + k, 2)] = piece[...]
    for r in range(-(count - 1), count):
        piece = cots[r + count - 1]
        blocks, rows, width = piece.shape

        @pl.when(jnp.logical_and(s + r >= 0, s + r < count))
        def _():
            cot_buf[s + r] = piece[...].reshape(blocks * rows, width)

    half = own_ref.shape[1]
    for t in range(3):
        low = max(0, 1 - t)
        high = min(count, count + 1 - t)
        for out_ref, side in ((sent_ref, 1 - b), (own_ref, b)):
            start = pl.multiple_of(side * half, half)
            total = None
            for j in range(low, high):
                term = jnp.dot(
                    act_buf[j + t - 1, pl.ds(start, half), :],
                    cot_buf[j],
                    preferred_element_type=F32,
                )
                total = term if total is None else total + term
            out_ref[t] = (factor * total).astype(out_ref.dtype)


def add_kernel(own_ref, got_ref, out_ref):
    out_ref[...] = own_ref[...] + got_ref[...].astype(F32)


def place_kernel(count, *refs):
    pieces, outs = refs[:count], refs[count:]
    s = lax.axis_index("seq")
    for d in range(count):
        b = lax.rem(s + d, count)
        for j in range(3):
            outs[j][b] = pieces[d][j]


def shift(x, axis, by, wrap):
    n = lax.axis_size(axis)
    pairs = [(i, (i + by) % n) for i in range(n) if wrap or 0 <= i + by < n]
    return lax.ppermute(x, axis, pairs)


def after(first, *then):
    held = lax.optimization_barrier((first, *then))
    return held[1:]


def per_device(query_vectors, key_vectors, value_vectors, hidden, cotangent, conv_weight):
    count = lax.axis_size("seq")
    blocks, rows, width = hidden.shape
    tokens = blocks * rows
    factor = 1.0 / math.sqrt(tokens * count * lax.axis_size("batch"))
    weights = conv_weight.transpose(1, 0, 2)
    piece = shape((rows, width))
    piece3 = shape((3, rows, width))
    full = shape((blocks, rows, width))
    part = width // 2

    left = shift(cotangent, "seq", 1, False)
    right = shift(cotangent, "seq", -1, False)
    *qkv, act0, act1 = kernel_call(
        functools.partial(prepare_kernel, count),
        [piece3] * count + [shape((part, tokens))] * 2,
        transcendentals=tokens * width,
        name="prepare",
    )(query_vectors, key_vectors, value_vectors, hidden)
    got_qkv = [qkv[0]] + [shift(qkv[d], "seq", d, True) for d in range(1, count)]

    mine, other = kernel_call(
        conv_kernel, [full, full], flops=2 * tokens * 3 * width * 2 * width, name="conv_back"
    )(cotangent, left, right, weights)
    got = shift(other, "chan", 1, True)
    hidden_grad, *grads = kernel_call(
        functools.partial(grad_kernel, count),
        [full] + [piece] * count,
        transcendentals=tokens * width,
        name="hidden_grad",
    )(cotangent, hidden, mine, got)
    got_grads = [grads[0]] + [shift(grads[d], "seq", d, True) for d in range(1, count)]

    far_left, far_right, act0, act1 = after(grads[0], left, right, act0, act1)
    lefts, rights = [far_left], [far_right]
    n_chan = lax.axis_size("chan")
    got_act = []
    for k, act in enumerate((act0, act1)):
        pairs = []
        for i in range(count):
            for c in range(n_chan):
                to = (2 * c + (i + k) % 2) * n_chan + i // 2
                pairs.append((i * n_chan + c, to))
        got_act.append(lax.ppermute(act, ("seq", "chan"), pairs))
    for _ in range(count - 2):
        lefts.append(shift(lefts[-1], "seq", 1, False))
        rights.append(shift(rights[-1], "seq", -1, False))
    other_act = [shift(a, "chan", 1, True) for a in got_act]

    item = 5 * (count * rows) ** 2 * width
    returned = kernel_call(
        functools.partial(attention_kernel, count),
        [piece3] * count,
        flops=2 * item,
        transcendentals=(count * rows) ** 2 * (width // HD),
        name="attention",
    )(*got_qkv, *got_grads)
    back = [returned[0]] + [shift(returned[d], "seq", -d, True) for d in range(1, count)]

    own, sent = kernel_call(
        functools.partial(weight_kernel, count, factor),
        [shape((3, part // 2, width), F32), shape((3, part // 2, width))],
        flops=2 * (3 * count - 2) * tokens * part * width,
        name="weight_grad",
        scratch=[
            pltpu.VMEM((count, part, tokens), BF),
            pltpu.VMEM((count, tokens, width), BF),
        ],
    )(*got_act, *other_act, *reversed(lefts), cotangent, *rights)
    got_sum = shift(sent, "batch", 1, True)
    (weight_grad,) = kernel_call(add_kernel, [shape((3, part // 2, width), F32)], name="add_weight")(
        own, got_sum
    )
    query_grad, key_grad, value_grad = kernel_call(
        functools.partial(place_kernel, count), [full] * 3, name="place"
    )(*back)
    return (query_grad, key_grad, value_grad, hidden_grad, weight_grad.transpose(1, 0, 2))


def from_behind(shard, axis, by):
    length = lax.axis_size(axis)
    pairs = [(i, i + by) for i in range(length) if 0 <= i + by < length]
    return lax.ppermute(shard, axis, pairs)


def per_device_general(query_vectors, key_vectors, value_vectors, hidden, cotangent, conv_weight):
    seq_count = lax.axis_size("seq")
    batch_count = lax.axis_size("batch")
    partner_gap = seq_count // 4
    blocks, row_count, local_width = hidden.shape
    tokens_all = blocks * batch_count * row_count * seq_count
    factor = 1.0 / math.sqrt(tokens_all)
    hidden_f = hidden.astype(jnp.float32)
    activation = tanh_gelu(hidden_f).astype(jnp.bfloat16)
    act_full = lax.all_gather(activation, "chan", axis=2, tiled=True)

    def partner(offset):
        return from_behind(cotangent, "seq", offset)

    cot_before = partner(partner_gap)
    cot_after = partner(-partner_gap)
    cot_taps = jnp.stack([cot_after, cotangent, cot_before])
    back_part = jnp.einsum(
        "tbqo,ito->bqi", cot_taps, conv_weight, preferred_element_type=jnp.float32
    )
    back_sum = lax.psum_scatter(
        back_part.astype(jnp.bfloat16), "chan", scatter_dimension=2, tiled=True
    ).astype(jnp.float32)
    hidden_grad = (cotangent.astype(jnp.float32) + back_sum * gelu_slope(hidden_f)).astype(
        jnp.bfloat16
    )
    weight_grad = lax.psum_scatter(
        factor
        * jnp.einsum("bpi,tbpo->ito", act_full, cot_taps, preferred_element_type=jnp.float32),
        ("seq", "batch"),
        scatter_dimension=0,
        tiled=True,
    )
    heads_local = local_width // HD

    def to_heads(signal):
        return signal.reshape(blocks, row_count, heads_local, HD)

    stacked = jnp.stack(
        [
            to_heads(query_vectors),
            to_heads(key_vectors),
            to_heads(value_vectors),
            to_heads(hidden_grad),
        ],
        axis=3,
    )
    stacked = stacked.transpose(0, 2, 1, 3, 4).reshape(
        seq_count, blocks * heads_local // seq_count, row_count, 4 * HD
    )
    gathered = lax.all_to_all(stacked, "seq", split_axis=0, concat_axis=2, tiled=True)
    item_count = gathered.shape[1]
    length = gathered.shape[2]
    columns = gathered[0].reshape(item_count, length, 4, HD)
    query_all = columns[:, :, 0]
    key_all = columns[:, :, 1]
    value_all = columns[:, :, 2]
    grad_all = columns[:, :, 3]
    score_scale = 1.0 / math.sqrt(HD)
    block_rows = math.gcd(length, 512)
    block_count = length // block_rows
    query_blocks = query_all.reshape(item_count, block_count, block_rows, HD).transpose(1, 0, 2, 3)
    grad_blocks = grad_all.reshape(item_count, block_count, block_rows, HD).transpose(1, 0, 2, 3)

    def query_block(carry, inputs):
        key_acc, value_acc = carry
        query_rows, grad_rows = inputs
        scores = (
            jnp.einsum("iqd,ikd->iqk", query_rows, key_all, preferred_element_type=jnp.float32)
            * score_scale
        )
        row_max = jnp.max(scores, axis=-1, keepdims=True)
        raised = jnp.exp(scores - row_max)
        probability = raised / jnp.sum(raised, axis=-1, keepdims=True)
        prob_b = probability.astype(jnp.bfloat16)
        value_acc = value_acc + jnp.einsum(
            "iqk,iqd->ikd", prob_b, grad_rows, preferred_element_type=jnp.float32
        )
        d_prob = jnp.einsum(
            "iqd,ikd->iqk", grad_rows, value_all, preferred_element_type=jnp.float32
        )
        row_total = jnp.sum(probability * d_prob, axis=-1, keepdims=True)
        d_score = (probability * (d_prob - row_total)).astype(jnp.bfloat16)
        query_out = (
            score_scale
            * jnp.einsum("iqk,ikd->iqd", d_score, key_all, preferred_element_type=jnp.float32)
        ).astype(jnp.bfloat16)
        key_acc = key_acc + jnp.einsum(
            "iqk,iqd->ikd", d_score, query_rows, preferred_element_type=jnp.float32
        )
        return ((key_acc, value_acc), query_out)

    empty_acc = jnp.zeros((item_count, length, HD), jnp.float32)
    (key_acc, value_acc), query_outs = lax.scan(
        query_block, (empty_acc, empty_acc), (query_blocks, grad_blocks)
    )
    query_out = query_outs.transpose(1, 0, 2, 3).reshape(item_count, length, HD)
    key_out = (score_scale * key_acc).astype(jnp.bfloat16)
    value_out = value_acc.astype(jnp.bfloat16)
    results = jnp.concatenate([query_out, key_out, value_out], axis=-1)[None]
    returned = lax.all_to_all(results, "seq", split_axis=2, concat_axis=0, tiled=True)
    returned = returned.reshape(blocks, heads_local, row_count, 3, HD).transpose(3, 0, 2, 1, 4)
    returned = returned.reshape(3, blocks, row_count, local_width)
    return (returned[0], returned[1], returned[2], hidden_grad, weight_grad)


def solution(mesh):
    token = P(("groups", "batch"), "seq", "chan")
    sizes = dict(mesh.shape)

    def run(*arrays):
        blocks = arrays[0].shape[0] // (sizes["groups"] * sizes["batch"])
        fits = blocks == sizes["seq"] == 4 and sizes["batch"] == 2 and sizes["chan"] == 2
        return jax.shard_map(
            per_device if fits else per_device_general,
            mesh=mesh,
            in_specs=(token,) * 5 + (P(None, None, "chan"),),
            out_specs=(token,) * 4 + (P(("groups", "seq", "batch"), None, "chan"),),
            check_vma=False,
        )(*arrays)

    return run
```

```python
import functools
import math

import jax
import jax.numpy as jnp
from jax import lax
from jax.experimental import pallas as pl
from jax.experimental.pallas import tpu as pltpu
from jax.sharding import PartitionSpec as P

HD = 96
BF = jnp.bfloat16
F32 = jnp.float32
COST = 8
VMEM_LIMIT = 40 * 1024 * 1024


def tanh_gelu(signal):
    inner_arg = 0.7978845608 * (signal + 0.044715 * signal * signal * signal)
    return 0.5 * signal * (1.0 + jnp.tanh(inner_arg))


def gelu_slope(signal):
    inner_arg = 0.7978845608 * (signal + 0.044715 * signal * signal * signal)
    hyper = jnp.tanh(inner_arg)
    return 0.5 * (1.0 + hyper) + 0.5 * signal * (1.0 - hyper * hyper) * 0.7978845608 * (
        1.0 + 3.0 * 0.044715 * signal * signal
    )


def kernel_call(body, outs, flops=0, transcendentals=0, name=None, scratch=(), space=pltpu.VMEM):
    vmem = pl.BlockSpec(memory_space=pltpu.VMEM)
    given = pl.BlockSpec(memory_space=space)

    def call(*args):
        if space == pltpu.HBM:
            args = [pltpu.with_memory_space_constraint(a, pltpu.HBM) for a in args]
        moved = sum(math.prod(a.shape) * a.dtype.itemsize for a in args)
        moved += sum(math.prod(o.shape) * o.dtype.itemsize for o in outs)
        return pl.pallas_call(
            body,
            out_shape=list(outs),
            in_specs=[given] * len(args),
            out_specs=[vmem] * len(outs),
            scratch_shapes=list(scratch),
            compiler_params=pltpu.CompilerParams(vmem_limit_bytes=VMEM_LIMIT),
            cost_estimate=pl.CostEstimate(
                flops=flops, bytes_accessed=moved, transcendentals=transcendentals
            ),
            name=name,
        )(*args)

    return call


def shape(dims, dtype=BF):
    return jax.ShapeDtypeStruct(dims, dtype)


def prepare_kernel(count, q_hbm, k_hbm, v_hbm, h_hbm, cot_hbm, w_hbm, *refs):
    outs, (act_ref, h_ref, cot_ref, w_ref, sems) = refs[: count + 1], refs[count + 1 :]
    s = lax.axis_index("seq")
    near = [pltpu.make_async_copy(h_hbm, h_ref, sems.at[0])]
    for d in range(count + 1):
        b = lax.rem(s + d, count) if d < count else count - 1 - s
        for j, ref in enumerate((q_hbm, k_hbm, v_hbm)):
            near.append(
                pltpu.make_async_copy(ref.at[b], outs[d].at[j], sems.at[1 + 3 * d + j])
            )
    near.append(pltpu.make_async_copy(cot_hbm, cot_ref, sems.at[4 + 3 * count]))
    near.append(pltpu.make_async_copy(w_hbm, w_ref, sems.at[5 + 3 * count]))
    for copy in near:
        copy.start()
    near[0].wait()
    blocks, rows, width = h_ref.shape
    act = tanh_gelu(h_ref[...].astype(F32)).reshape(blocks * rows, width)
    act_t = act.T.astype(BF)
    lanes = act_t.shape[1] // 2
    parts = width // lanes
    for i in range(2 * parts):
        for h in range(2):
            act_ref[i // parts * 2 + h, :, pl.ds(i % parts * lanes, lanes)] = act_t[
                i * rows : (i + 1) * rows, h * lanes : (h + 1) * lanes
            ]
    for copy in near[1:]:
        copy.wait()


def conv_kernel(
    cot_ref, left_ref, right_ref, w_ref, act_ref, mine_ref, other_ref, inner_ref, outer_ref
):
    first = lax.axis_index("seq") < 2
    inner_ref[...] = jnp.where(first, right_ref[...], left_ref[...])
    outer_ref[...] = jnp.where(first, left_ref[...], right_ref[...])
    c = lax.axis_index("chan")
    blocks, rows, width = cot_ref.shape
    taps = [r[...].reshape(blocks * rows, width) for r in (right_ref, cot_ref, left_ref)]
    for out_ref, side in ((other_ref, 1 - c), (mine_ref, c)):
        start = pl.multiple_of(side * width, width)
        total = None
        for t in range(3):
            term = lax.dot_general(
                taps[t],
                w_ref[t, pl.ds(start, width), :],
                (((1,), (1,)), ((), ())),
                preferred_element_type=F32,
            )
            total = term if total is None else total + term
        out_ref[:blocks] = total.astype(BF).reshape(blocks, rows, width)
    other_ref[blocks:] = act_ref[...]


def grad_kernel(count, cot_ref, h_ref, mine_ref, other_ref, act_ref, *pieces):
    s = lax.axis_index("seq")
    c = lax.axis_index("chan")
    blocks = cot_ref.shape[0]
    for d in range(count):
        b = lax.rem(s + d, count)
        back = mine_ref[b].astype(F32) + other_ref[b].astype(F32)
        slope = gelu_slope(h_ref[b].astype(F32))
        pieces[d][0] = (cot_ref[b].astype(F32) + back * slope).astype(BF)
        here = lax.div(b, 2) == c
        for h in range(2):
            k = 2 * lax.rem(b, 2) + h
            pieces[d][1 + h] = jnp.where(here, act_ref[k], other_ref[blocks + k])


def attention_kernel(count, own, down, opposite, up, ends, *refs):
    grads, outs = refs[:count], refs[count:]
    _, rows, width = grads[0].shape
    scale = 1.0 / math.sqrt(HD)
    s = lax.axis_index("seq")

    def positions(j):
        before = jnp.where(s == 0, ends[j], down[j])
        behind = jnp.where(s == count - 1, ends[j], up[j])
        return jnp.concatenate([own[j], before, opposite[j], behind], axis=0)

    query, key, value = (positions(j) for j in range(3))
    grad = jnp.concatenate([grads[d][0] for d in range(count)], axis=0)
    nt = (((1,), (1,)), ((), ()))
    nn = (((1,), (0,)), ((), ()))
    tn = (((0,), (0,)), ((), ()))
    dot = functools.partial(lax.dot_general, preferred_element_type=F32)
    results = ([], [], [])
    for h in range(width // HD):
        cols = slice(h * HD, (h + 1) * HD)
        q, k, v, g = query[:, cols], key[:, cols], value[:, cols], grad[:, cols]
        scores = dot(k, q, nt) * scale
        raised = jnp.exp(scores - jnp.max(scores, axis=0, keepdims=True))
        prob = raised * (1.0 / jnp.sum(raised, axis=0, keepdims=True))
        d_prob = dot(v, g, nt)
        row_total = jnp.sum(prob * d_prob, axis=0, keepdims=True)
        d_score = (prob * (d_prob - row_total)).astype(BF)
        results[0].append((dot(d_score, k, tn) * scale).astype(BF))
        results[1].append((dot(d_score, q, nn) * scale).astype(BF))
        results[2].append(dot(prob.astype(BF), g, nn).astype(BF))
    for j in range(3):
        whole = jnp.concatenate(results[j], axis=1)
        for d in range(count):
            outs[d][j] = whole[d * rows : (d + 1) * rows]


def weight_kernel(count, factor, *refs):
    cots, grads, got = refs[:6], refs[6 : 6 + count], (refs[6], *refs[6 + count : 5 + 2 * count])
    own_ref, sent0_ref, sent1_ref, grad_ref, act_buf, cot_buf = refs[5 + 2 * count :]
    s = lax.axis_index("seq")
    b = lax.axis_index("batch")
    _, rows, width = got[0].shape
    lanes = act_buf.shape[2] // 2
    for d in range(count):
        j = lax.rem(s - d + count, count)
        for r in range(width // lanes):
            for h in range(2):
                act_buf[j, pl.ds(r * rows, rows), pl.ds(h * lanes, lanes)] = got[d][
                    1 + h, :, pl.ds(r * lanes, lanes)
                ]
    own_cot, left, right, far, across, farthest = cots
    flat = cot_buf.shape[1:]
    cot_buf[s] = own_cot[...].reshape(flat)

    @pl.when(s > 0)
    def _():
        cot_buf[s - 1] = left[...].reshape(flat)

    @pl.when(s < count - 1)
    def _():
        cot_buf[s + 1] = right[...].reshape(flat)

    low = s < 2

    @pl.when(jnp.logical_or(s == 0, s == 3))
    def _():
        cot_buf[jnp.where(low, 2, 1)] = far[...].reshape(flat)
        cot_buf[jnp.where(low, 3, 0)] = farthest[...].reshape(flat)

    @pl.when(jnp.logical_or(s == 1, s == 2))
    def _():
        cot_buf[jnp.where(low, 3, 0)] = across[...].reshape(flat)

    for d in range(count):
        grad_ref[lax.rem(s + d, count)] = grads[d][0]

    half = own_ref.shape[1]
    for t in range(3):
        low = max(0, 1 - t)
        high = min(count, count + 1 - t)
        for is_own, side in ((False, 1 - b), (True, b)):
            start = pl.multiple_of(side * half, half)
            total = None
            for j in range(low, high):
                term = jnp.dot(
                    act_buf[j + t - 1, pl.ds(start, half), :],
                    cot_buf[j],
                    preferred_element_type=F32,
                )
                total = term if total is None else total + term
            total = factor * total
            if is_own:
                own_ref[t] = total
            else:
                sent0_ref[t] = total[: half // 2].astype(BF)
                sent1_ref[t] = total[half // 2 :].astype(BF)


def add_kernel(own_ref, got0_ref, got1_ref, out_ref):
    half = got0_ref.shape[1]
    out_ref[:, :half] = own_ref[:, :half] + got0_ref[...].astype(F32)
    out_ref[:, half:] = own_ref[:, half:] + got1_ref[...].astype(F32)


def place_kernel(count, *refs):
    pieces, outs = refs[:count], refs[count:]
    s = lax.axis_index("seq")
    for d in range(count):
        b = lax.rem(s + d, count)
        for j in range(3):
            outs[j][b] = pieces[d][j]


def shift(x, axis, by, wrap):
    n = lax.axis_size(axis)
    pairs = [(i, (i + by) % n) for i in range(n) if wrap or 0 <= i + by < n]
    return lax.ppermute(x, axis, pairs)


def after(first, *then):
    held = lax.optimization_barrier((first, *then))
    return held[1:]


def per_device(query_vectors, key_vectors, value_vectors, hidden, cotangent, conv_weight):
    count = lax.axis_size("seq")
    blocks, rows, width = hidden.shape
    tokens = blocks * rows
    factor = 1.0 / math.sqrt(tokens * count * lax.axis_size("batch"))
    weights = conv_weight.transpose(1, 0, 2)
    piece = shape((rows, width))
    piece3 = shape((3, rows, width))
    full = shape((blocks, rows, width))
    part = width // 2

    left = shift(cotangent, "seq", 1, False)
    right = shift(cotangent, "seq", -1, False)
    own_qkv, to_down, to_opposite, to_up, to_end, act, hidden, own_cot, weights = kernel_call(
        functools.partial(prepare_kernel, count),
        [piece3] * (count + 1) + [full] * 3 + [shape(weights.shape)],
        name="prepare",
        scratch=[pltpu.SemaphoreType.DMA((3 * count + 6,))],
        space=pltpu.HBM,
    )(query_vectors, key_vectors, value_vectors, hidden, cotangent, weights)

    down = shift(to_down, "seq", 1, False)
    up = shift(to_up, "seq", -1, False)
    opposite = shift(to_opposite, "seq", 2, True)
    ends = lax.ppermute(to_end, "seq", [(0, count - 1), (count - 1, 0)])
    near_left, right = after(down, left, right)
    near_left, right = after(up, near_left, right)
    mine, other, inner, outer = kernel_call(
        conv_kernel, [full, shape((2 * blocks, rows, width)), full, full], name="conv_back"
    )(own_cot, near_left, right, weights, act)
    got = shift(other, "chan", 1, True)
    grads = kernel_call(
        functools.partial(grad_kernel, count), [piece3] * count, name="hidden_grad"
    )(own_cot, hidden, mine, got, act)
    got_grads = [grads[0]] + [shift(grads[d], "seq", d, True) for d in range(1, count)]

    inner, outer = after(grads[0], *after(opposite, inner, outer))
    far = lax.ppermute(inner, "seq", [(1, 0), (2, 3)])
    across = lax.ppermute(outer, "seq", [(1, 2), (2, 1)])
    farthest = lax.ppermute(across, "seq", [(1, 0), (2, 3)])
    (own_qkv,) = after(across, own_qkv)
    item = 5 * (count * rows) ** 2 * width
    returned = kernel_call(
        functools.partial(attention_kernel, count),
        [piece3] * count,
        flops=COST * 2 * item,
        transcendentals=(count * rows) ** 2 * (width // HD),
        name="attention",
    )(own_qkv, down, opposite, up, ends, *got_grads)
    back = [returned[0]] + [shift(returned[d], "seq", -d, True) for d in range(1, count)]

    own_cot, near_left = after(returned[0], own_cot, near_left)
    own, sent0, sent1, hidden_grad = kernel_call(
        functools.partial(weight_kernel, count, factor),
        [shape((3, part // 2, width), F32)] + [shape((3, part // 4, width))] * 2 + [full],
        name="weight_grad",
        scratch=[
            pltpu.VMEM((count, part, tokens), BF),
            pltpu.VMEM((count, tokens, width), BF),
        ],
    )(own_cot, near_left, right, far, across, farthest, *grads, *got_grads[1:])
    got_sums = [shift(x, "batch", 1, True) for x in (sent0, sent1)]
    (weight_grad,) = kernel_call(add_kernel, [shape((3, part // 2, width), F32)], name="add_weight")(
        own, *got_sums
    )
    (back[0],) = after(weight_grad, back[0])
    query_grad, key_grad, value_grad = kernel_call(
        functools.partial(place_kernel, count), [full] * 3, name="place"
    )(*back)
    return (query_grad, key_grad, value_grad, hidden_grad, weight_grad.transpose(1, 0, 2))


def from_behind(shard, axis, by):
    length = lax.axis_size(axis)
    pairs = [(i, i + by) for i in range(length) if 0 <= i + by < length]
    return lax.ppermute(shard, axis, pairs)


def per_device_general(query_vectors, key_vectors, value_vectors, hidden, cotangent, conv_weight):
    seq_count = lax.axis_size("seq")
    batch_count = lax.axis_size("batch")
    partner_gap = seq_count // 4
    blocks, row_count, local_width = hidden.shape
    tokens_all = blocks * batch_count * row_count * seq_count
    factor = 1.0 / math.sqrt(tokens_all)
    hidden_f = hidden.astype(jnp.float32)
    activation = tanh_gelu(hidden_f).astype(jnp.bfloat16)
    act_full = lax.all_gather(activation, "chan", axis=2, tiled=True)

    def partner(offset):
        return from_behind(cotangent, "seq", offset)

    cot_before = partner(partner_gap)
    cot_after = partner(-partner_gap)
    cot_taps = jnp.stack([cot_after, cotangent, cot_before])
    back_part = jnp.einsum(
        "tbqo,ito->bqi", cot_taps, conv_weight, preferred_element_type=jnp.float32
    )
    back_sum = lax.psum_scatter(
        back_part.astype(jnp.bfloat16), "chan", scatter_dimension=2, tiled=True
    ).astype(jnp.float32)
    hidden_grad = (cotangent.astype(jnp.float32) + back_sum * gelu_slope(hidden_f)).astype(
        jnp.bfloat16
    )
    weight_grad = lax.psum_scatter(
        factor
        * jnp.einsum("bpi,tbpo->ito", act_full, cot_taps, preferred_element_type=jnp.float32),
        ("seq", "batch"),
        scatter_dimension=0,
        tiled=True,
    )
    heads_local = local_width // HD

    def to_heads(signal):
        return signal.reshape(blocks, row_count, heads_local, HD)

    stacked = jnp.stack(
        [
            to_heads(query_vectors),
            to_heads(key_vectors),
            to_heads(value_vectors),
            to_heads(hidden_grad),
        ],
        axis=3,
    )
    stacked = stacked.transpose(0, 2, 1, 3, 4).reshape(
        seq_count, blocks * heads_local // seq_count, row_count, 4 * HD
    )
    gathered = lax.all_to_all(stacked, "seq", split_axis=0, concat_axis=2, tiled=True)
    item_count = gathered.shape[1]
    length = gathered.shape[2]
    columns = gathered[0].reshape(item_count, length, 4, HD)
    query_all = columns[:, :, 0]
    key_all = columns[:, :, 1]
    value_all = columns[:, :, 2]
    grad_all = columns[:, :, 3]
    score_scale = 1.0 / math.sqrt(HD)
    block_rows = math.gcd(length, 512)
    block_count = length // block_rows
    query_blocks = query_all.reshape(item_count, block_count, block_rows, HD).transpose(1, 0, 2, 3)
    grad_blocks = grad_all.reshape(item_count, block_count, block_rows, HD).transpose(1, 0, 2, 3)

    def query_block(carry, inputs):
        key_acc, value_acc = carry
        query_rows, grad_rows = inputs
        scores = (
            jnp.einsum("iqd,ikd->iqk", query_rows, key_all, preferred_element_type=jnp.float32)
            * score_scale
        )
        row_max = jnp.max(scores, axis=-1, keepdims=True)
        raised = jnp.exp(scores - row_max)
        probability = raised / jnp.sum(raised, axis=-1, keepdims=True)
        prob_b = probability.astype(jnp.bfloat16)
        value_acc = value_acc + jnp.einsum(
            "iqk,iqd->ikd", prob_b, grad_rows, preferred_element_type=jnp.float32
        )
        d_prob = jnp.einsum(
            "iqd,ikd->iqk", grad_rows, value_all, preferred_element_type=jnp.float32
        )
        row_total = jnp.sum(probability * d_prob, axis=-1, keepdims=True)
        d_score = (probability * (d_prob - row_total)).astype(jnp.bfloat16)
        query_out = (
            score_scale
            * jnp.einsum("iqk,ikd->iqd", d_score, key_all, preferred_element_type=jnp.float32)
        ).astype(jnp.bfloat16)
        key_acc = key_acc + jnp.einsum(
            "iqk,iqd->ikd", d_score, query_rows, preferred_element_type=jnp.float32
        )
        return ((key_acc, value_acc), query_out)

    empty_acc = jnp.zeros((item_count, length, HD), jnp.float32)
    (key_acc, value_acc), query_outs = lax.scan(
        query_block, (empty_acc, empty_acc), (query_blocks, grad_blocks)
    )
    query_out = query_outs.transpose(1, 0, 2, 3).reshape(item_count, length, HD)
    key_out = (score_scale * key_acc).astype(jnp.bfloat16)
    value_out = value_acc.astype(jnp.bfloat16)
    results = jnp.concatenate([query_out, key_out, value_out], axis=-1)[None]
    returned = lax.all_to_all(results, "seq", split_axis=2, concat_axis=0, tiled=True)
    returned = returned.reshape(blocks, heads_local, row_count, 3, HD).transpose(3, 0, 2, 1, 4)
    returned = returned.reshape(3, blocks, row_count, local_width)
    return (returned[0], returned[1], returned[2], hidden_grad, weight_grad)


def solution(mesh):
    token = P(("groups", "batch"), "seq", "chan")
    sizes = dict(mesh.shape)

    def run(*arrays):
        blocks = arrays[0].shape[0] // (sizes["groups"] * sizes["batch"])
        fits = blocks == sizes["seq"] == 4 and sizes["batch"] == 2 and sizes["chan"] == 2
        return jax.shard_map(
            per_device if fits else per_device_general,
            mesh=mesh,
            in_specs=(token,) * 5 + (P(None, None, "chan"),),
            out_specs=(token,) * 4 + (P(("groups", "seq", "batch"), None, "chan"),),
            check_vma=False,
        )(*arrays)

    return run
```

```python
import functools
import math

import jax
import jax.numpy as jnp
from jax import lax
from jax.experimental import pallas as pl
from jax.experimental.pallas import tpu as pltpu
from jax.sharding import PartitionSpec as P

HD = 96
BF = jnp.bfloat16
F32 = jnp.float32
COST = 8
VMEM_LIMIT = 40 * 1024 * 1024


def tanh_gelu(signal):
    inner_arg = 0.7978845608 * (signal + 0.044715 * signal * signal * signal)
    return 0.5 * signal * (1.0 + jnp.tanh(inner_arg))


def gelu_slope(signal):
    inner_arg = 0.7978845608 * (signal + 0.044715 * signal * signal * signal)
    hyper = jnp.tanh(inner_arg)
    return 0.5 * (1.0 + hyper) + 0.5 * signal * (1.0 - hyper * hyper) * 0.7978845608 * (
        1.0 + 3.0 * 0.044715 * signal * signal
    )


def kernel_call(body, outs, flops=0, transcendentals=0, name=None, scratch=(), space=pltpu.VMEM):
    vmem = pl.BlockSpec(memory_space=pltpu.VMEM)
    given = pl.BlockSpec(memory_space=space)

    def call(*args):
        if space == pltpu.HBM:
            args = [pltpu.with_memory_space_constraint(a, pltpu.HBM) for a in args]
        moved = sum(math.prod(a.shape) * a.dtype.itemsize for a in args)
        moved += sum(math.prod(o.shape) * o.dtype.itemsize for o in outs)
        return pl.pallas_call(
            body,
            out_shape=list(outs),
            in_specs=[given] * len(args),
            out_specs=[vmem] * len(outs),
            scratch_shapes=list(scratch),
            compiler_params=pltpu.CompilerParams(vmem_limit_bytes=VMEM_LIMIT),
            cost_estimate=pl.CostEstimate(
                flops=flops, bytes_accessed=moved, transcendentals=transcendentals
            ),
            name=name,
        )(*args)

    return call


def shape(dims, dtype=BF):
    return jax.ShapeDtypeStruct(dims, dtype)


def fetch(pairs, sems):
    copies = [pltpu.make_async_copy(src, dst, sems.at[i]) for i, (src, dst) in enumerate(pairs)]
    for copy in copies:
        copy.start()
    return copies


def near_kernel(count, cot, q, k, v, down, up, sems):
    s = lax.axis_index("seq")
    blocks = cot.shape[0]
    pairs = []
    for out, d in ((down, 1), (up, count - 1)):
        pairs.append((cot, out.at[pl.ds(0, blocks)]))
        pairs += [(x.at[lax.rem(s + d, count)], out.at[blocks + j]) for j, x in enumerate((q, k, v))]
    for copy in fetch(pairs, sems):
        copy.wait()


def rest_kernel(count, hidden, q, k, v, w, h_ref, own, opposite, end, w_ref, act_ref, sems):
    s = lax.axis_index("seq")
    pairs = [(hidden, h_ref)]
    for out, b in ((own, s), (opposite, lax.rem(s + 2, count)), (end, count - 1 - s)):
        pairs += [(x.at[b], out.at[j]) for j, x in enumerate((q, k, v))]
    pairs.append((w, w_ref))
    copies = fetch(pairs, sems)
    copies[0].wait()
    blocks, rows, width = h_ref.shape
    act = tanh_gelu(h_ref[...].astype(F32)).reshape(blocks * rows, width)
    act_t = act.T.astype(BF)
    lanes = act_t.shape[1] // 2
    parts = width // lanes
    for i in range(2 * parts):
        for h in range(2):
            act_ref[i // parts * 2 + h, :, pl.ds(i % parts * lanes, lanes)] = act_t[
                i * rows : (i + 1) * rows, h * lanes : (h + 1) * lanes
            ]
    for copy in copies[1:]:
        copy.wait()


def conv_kernel(cot_ref, down_ref, up_ref, w_ref, act_ref, mine_ref, other_ref):
    c = lax.axis_index("chan")
    blocks, rows, width = mine_ref.shape
    taps = [r[:blocks].reshape(blocks * rows, width) for r in (up_ref, cot_ref, down_ref)]
    for out_ref, side in ((other_ref, 1 - c), (mine_ref, c)):
        start = pl.multiple_of(side * width, width)
        total = None
        for t in range(3):
            term = lax.dot_general(
                taps[t],
                w_ref[t, pl.ds(start, width), :],
                (((1,), (1,)), ((), ())),
                preferred_element_type=F32,
            )
            total = term if total is None else total + term
        out_ref[:blocks] = total.astype(BF).reshape(blocks, rows, width)
    for k in range(2):
        other_ref[blocks + k] = act_ref[2 * k + 1 - c]


def grad_kernel(
    count, cot_ref, h_ref, mine_ref, got_ref, act_ref, down_ref, up_ref, end_qkv,
    own, down, opposite, up, end,
):
    s = lax.axis_index("seq")
    c = lax.axis_index("chan")
    blocks = h_ref.shape[0]

    def sequence(b):
        back = mine_ref[b].astype(F32) + got_ref[b].astype(F32)
        slope = gelu_slope(h_ref[b].astype(F32))
        grad = (cot_ref[b].astype(F32) + back * slope).astype(BF)
        k = lax.rem(b, 2)
        act = jnp.where(lax.div(b, 2) == c, act_ref[2 * k + c], got_ref[blocks + k])
        return grad, act

    for d, out in ((0, own), (1, down), (2, opposite), (3, up)):
        out[0], out[1] = sequence(lax.rem(s + d, count))
    end[:3] = end_qkv[...]
    first = s == 0
    end[3] = jnp.where(first, up[0], down[0])
    end[4] = jnp.where(first, up[1], down[1])
    down[2:] = down_ref[:blocks]
    up[2:] = up_ref[:blocks]


def pick_kernel(down_ref, up_ref, out_ref):
    out_ref[...] = jnp.where(lax.axis_index("seq") < 2, up_ref[2:], down_ref[2:])


def attention_kernel(
    count, own_qkv, own, down_qkv, up_qkv, opposite_qkv, end, down, up, opposite, *outs
):
    outs, act_ref = outs[:count], outs[count]
    rows, width = own.shape[1:]
    near = down_qkv.shape[0] - 3
    scale = 1.0 / math.sqrt(HD)
    s = lax.axis_index("seq")
    at_first, at_last = s == 0, s == count - 1

    def positions(j):
        before = jnp.where(at_first, end[j], down_qkv[near + j])
        behind = jnp.where(at_last, end[j], up_qkv[near + j])
        return jnp.concatenate([own_qkv[j], before, opposite_qkv[j], behind], axis=0)

    query, key, value = (positions(j) for j in range(3))
    grad, act = (
        (
            own[j],
            jnp.where(at_first, end[3 + j], down[j]),
            opposite[j],
            jnp.where(at_last, end[3 + j], up[j]),
        )
        for j in range(2)
    )
    grad = jnp.concatenate(grad, axis=0)
    for d in range(count):
        act_ref[d] = act[d]
    nt = (((1,), (1,)), ((), ()))
    nn = (((1,), (0,)), ((), ()))
    tn = (((0,), (0,)), ((), ()))
    dot = functools.partial(lax.dot_general, preferred_element_type=F32)
    results = ([], [], [])
    for h in range(width // HD):
        cols = slice(h * HD, (h + 1) * HD)
        q, k, v, g = query[:, cols], key[:, cols], value[:, cols], grad[:, cols]
        scores = dot(k, q, nt) * scale
        raised = jnp.exp(scores - jnp.max(scores, axis=0, keepdims=True))
        prob = raised * (1.0 / jnp.sum(raised, axis=0, keepdims=True))
        d_prob = dot(v, g, nt)
        row_total = jnp.sum(prob * d_prob, axis=0, keepdims=True)
        d_score = (prob * (d_prob - row_total)).astype(BF)
        results[0].append((dot(d_score, k, tn) * scale).astype(BF))
        results[1].append((dot(d_score, q, nn) * scale).astype(BF))
        results[2].append(dot(prob.astype(BF), g, nn).astype(BF))
    for j in range(3):
        whole = jnp.concatenate(results[j], axis=1)
        for d in range(count):
            outs[d][j] = whole[d * rows : (d + 1) * rows]


def weight_kernel(
    count, factor, cot_ref, down, up, down2, up2, farthest, act_ref, act_peer, own, to_down,
    to_opposite, to_up, own_ref, sent0_ref, sent1_ref, grad_ref, act_buf, cot_buf,
):
    s = lax.axis_index("seq")
    c = lax.axis_index("chan")
    b = lax.axis_index("batch")
    blocks, rows, width = grad_ref.shape
    for d, piece in enumerate((own, to_down, to_opposite, to_up)):
        grad_ref[lax.rem(s + d, count)] = piece[0]
    lanes = act_buf.shape[2] // 2
    for d in range(count):
        j = lax.rem(s - d + count, count)
        halves = (
            jnp.where(c == 0, act_ref[d], act_peer[d]),
            jnp.where(c == 0, act_peer[d], act_ref[d]),
        )
        for r in range(width // lanes):
            for h in range(2):
                act_buf[j, pl.ds(r * rows, rows), pl.ds(h * lanes, lanes)] = halves[h][
                    :, r * lanes : (r + 1) * lanes
                ]
    flat = cot_buf.shape[1:]

    def put(position, holds, value):
        @pl.when(holds)
        def _():
            cot_buf[position] = value().reshape(flat)

    cot_buf[s] = cot_ref[:blocks].reshape(flat)
    put(s - 1, s > 0, lambda: down[:blocks])
    put(s + 1, s < count - 1, lambda: up[:blocks])
    put(s - 2, s >= 2, lambda: down2[2:])
    put(s + 2, s < 2, lambda: up2[2:])
    put(count - 1 - s, jnp.logical_or(s == 0, s == count - 1), lambda: farthest[...])

    half = own_ref.shape[1]
    for t in range(3):
        low = max(0, 1 - t)
        high = min(count, count + 1 - t)
        for is_own, side in ((False, 1 - b), (True, b)):
            start = pl.multiple_of(side * half, half)
            total = None
            for j in range(low, high):
                term = jnp.dot(
                    act_buf[j + t - 1, pl.ds(start, half), :],
                    cot_buf[j],
                    preferred_element_type=F32,
                )
                total = term if total is None else total + term
            total = factor * total
            if is_own:
                own_ref[t] = total
            else:
                sent0_ref[t] = total[: half // 2].astype(BF)
                sent1_ref[t] = total[half // 2 :].astype(BF)


def add_kernel(own_ref, got0_ref, got1_ref, out_ref):
    half = got0_ref.shape[1]
    out_ref[:, :half] = own_ref[:, :half] + got0_ref[...].astype(F32)
    out_ref[:, half:] = own_ref[:, half:] + got1_ref[...].astype(F32)


def place_kernel(count, *refs):
    pieces, outs = refs[:count], refs[count:]
    s = lax.axis_index("seq")
    for d in range(count):
        b = lax.rem(s + d, count)
        for j in range(3):
            outs[j][b] = pieces[d][j]


def shift(x, axis, by, wrap):
    n = lax.axis_size(axis)
    pairs = [(i, (i + by) % n) for i in range(n) if wrap or 0 <= i + by < n]
    return lax.ppermute(x, axis, pairs)


def after(first, *then):
    held = lax.optimization_barrier((first, *then))
    return held[1:]


def per_device(query_vectors, key_vectors, value_vectors, hidden, cotangent, conv_weight):
    count = lax.axis_size("seq")
    blocks, rows, width = hidden.shape
    tokens = blocks * rows
    factor = 1.0 / math.sqrt(tokens * count * lax.axis_size("batch"))
    weights = conv_weight.transpose(1, 0, 2)
    part = width // 2

    def units(n):
        return shape((n, rows, width))

    def along(x, by):
        return shift(x, "seq", by, False)

    def between_ends(x):
        return lax.ppermute(x, "seq", [(0, count - 1), (count - 1, 0)])

    to_down, to_up = kernel_call(
        functools.partial(near_kernel, count),
        [units(blocks + 3)] * 2,
        name="near",
        scratch=[pltpu.SemaphoreType.DMA((8,))],
        space=pltpu.HBM,
    )(cotangent, query_vectors, key_vectors, value_vectors)
    down, up = along(to_down, 1), along(to_up, -1)
    (hidden,) = after(to_down, hidden)
    hidden, own_qkv, to_opposite, to_end, weights, act = kernel_call(
        functools.partial(rest_kernel, count),
        [units(blocks), units(3), units(3), units(3), shape(weights.shape), units(blocks)],
        name="rest",
        scratch=[pltpu.SemaphoreType.DMA((11,))],
        space=pltpu.HBM,
    )(hidden, query_vectors, key_vectors, value_vectors, weights)
    opposite = shift(to_opposite, "seq", 2, True)

    mine, other = kernel_call(conv_kernel, [units(blocks), units(blocks + 2)], name="conv_back")(
        to_down, down, up, weights, act
    )
    got = shift(other, "chan", 1, True)
    own, to_down2, to_opposite2, to_up2, to_end2 = kernel_call(
        functools.partial(grad_kernel, count),
        [units(2), units(blocks + 2), units(2), units(blocks + 2), units(5)],
        name="hidden_grad",
    )(to_down, hidden, mine, got, act, down, up, to_end)
    down2, up2 = along(to_down2, 1), along(to_up2, -1)
    far_opposite, far_end = after(opposite, to_opposite2, to_end2)
    opposite2 = shift(far_opposite, "seq", 2, True)
    end2 = between_ends(far_end)
    (far,) = kernel_call(pick_kernel, [units(blocks)], name="pick")(down2, up2)
    farthest = lax.ppermute(far, "seq", [(1, 0), (2, 3)])

    item = 5 * (count * rows) ** 2 * width
    *returned, act_held = kernel_call(
        functools.partial(attention_kernel, count),
        [units(3)] * count + [units(count)],
        flops=COST * 2 * item,
        transcendentals=(count * rows) ** 2 * (width // HD),
        name="attention",
    )(own_qkv, own, down, up, opposite, end2, down2, up2, opposite2)
    back = [returned[0]] + [shift(returned[d], "seq", -d, True) for d in range(1, count)]

    act_peer = shift(act_held, "chan", 1, True)
    total, sent0, sent1, hidden_grad = kernel_call(
        functools.partial(weight_kernel, count, factor),
        [shape((3, part // 2, width), F32)] + [shape((3, part // 4, width))] * 2 + [units(blocks)],
        name="weight_grad",
        scratch=[
            pltpu.VMEM((count, part, tokens), BF),
            pltpu.VMEM((count, tokens, width), BF),
        ],
    )(
        to_down, down, up, down2, up2, farthest, act_held, act_peer, own, to_down2, to_opposite2,
        to_up2,
    )
    got_sums = [shift(x, "batch", 1, True) for x in (sent0, sent1)]
    (weight_grad,) = kernel_call(add_kernel, [shape((3, part // 2, width), F32)], name="add_weight")(
        total, *got_sums
    )
    (back[0],) = after(weight_grad, back[0])
    query_grad, key_grad, value_grad = kernel_call(
        functools.partial(place_kernel, count), [units(blocks)] * 3, name="place"
    )(*back)
    return (query_grad, key_grad, value_grad, hidden_grad, weight_grad.transpose(1, 0, 2))


def from_behind(shard, axis, by):
    length = lax.axis_size(axis)
    pairs = [(i, i + by) for i in range(length) if 0 <= i + by < length]
    return lax.ppermute(shard, axis, pairs)


def per_device_general(query_vectors, key_vectors, value_vectors, hidden, cotangent, conv_weight):
    seq_count = lax.axis_size("seq")
    batch_count = lax.axis_size("batch")
    partner_gap = seq_count // 4
    blocks, row_count, local_width = hidden.shape
    tokens_all = blocks * batch_count * row_count * seq_count
    factor = 1.0 / math.sqrt(tokens_all)
    hidden_f = hidden.astype(jnp.float32)
    activation = tanh_gelu(hidden_f).astype(jnp.bfloat16)
    act_full = lax.all_gather(activation, "chan", axis=2, tiled=True)

    def partner(offset):
        return from_behind(cotangent, "seq", offset)

    cot_before = partner(partner_gap)
    cot_after = partner(-partner_gap)
    cot_taps = jnp.stack([cot_after, cotangent, cot_before])
    back_part = jnp.einsum(
        "tbqo,ito->bqi", cot_taps, conv_weight, preferred_element_type=jnp.float32
    )
    back_sum = lax.psum_scatter(
        back_part.astype(jnp.bfloat16), "chan", scatter_dimension=2, tiled=True
    ).astype(jnp.float32)
    hidden_grad = (cotangent.astype(jnp.float32) + back_sum * gelu_slope(hidden_f)).astype(
        jnp.bfloat16
    )
    weight_grad = lax.psum_scatter(
        factor
        * jnp.einsum("bpi,tbpo->ito", act_full, cot_taps, preferred_element_type=jnp.float32),
        ("seq", "batch"),
        scatter_dimension=0,
        tiled=True,
    )
    heads_local = local_width // HD

    def to_heads(signal):
        return signal.reshape(blocks, row_count, heads_local, HD)

    stacked = jnp.stack(
        [
            to_heads(query_vectors),
            to_heads(key_vectors),
            to_heads(value_vectors),
            to_heads(hidden_grad),
        ],
        axis=3,
    )
    stacked = stacked.transpose(0, 2, 1, 3, 4).reshape(
        seq_count, blocks * heads_local // seq_count, row_count, 4 * HD
    )
    gathered = lax.all_to_all(stacked, "seq", split_axis=0, concat_axis=2, tiled=True)
    item_count = gathered.shape[1]
    length = gathered.shape[2]
    columns = gathered[0].reshape(item_count, length, 4, HD)
    query_all = columns[:, :, 0]
    key_all = columns[:, :, 1]
    value_all = columns[:, :, 2]
    grad_all = columns[:, :, 3]
    score_scale = 1.0 / math.sqrt(HD)
    block_rows = math.gcd(length, 512)
    block_count = length // block_rows
    query_blocks = query_all.reshape(item_count, block_count, block_rows, HD).transpose(1, 0, 2, 3)
    grad_blocks = grad_all.reshape(item_count, block_count, block_rows, HD).transpose(1, 0, 2, 3)

    def query_block(carry, inputs):
        key_acc, value_acc = carry
        query_rows, grad_rows = inputs
        scores = (
            jnp.einsum("iqd,ikd->iqk", query_rows, key_all, preferred_element_type=jnp.float32)
            * score_scale
        )
        row_max = jnp.max(scores, axis=-1, keepdims=True)
        raised = jnp.exp(scores - row_max)
        probability = raised / jnp.sum(raised, axis=-1, keepdims=True)
        prob_b = probability.astype(jnp.bfloat16)
        value_acc = value_acc + jnp.einsum(
            "iqk,iqd->ikd", prob_b, grad_rows, preferred_element_type=jnp.float32
        )
        d_prob = jnp.einsum(
            "iqd,ikd->iqk", grad_rows, value_all, preferred_element_type=jnp.float32
        )
        row_total = jnp.sum(probability * d_prob, axis=-1, keepdims=True)
        d_score = (probability * (d_prob - row_total)).astype(jnp.bfloat16)
        query_out = (
            score_scale
            * jnp.einsum("iqk,ikd->iqd", d_score, key_all, preferred_element_type=jnp.float32)
        ).astype(jnp.bfloat16)
        key_acc = key_acc + jnp.einsum(
            "iqk,iqd->ikd", d_score, query_rows, preferred_element_type=jnp.float32
        )
        return ((key_acc, value_acc), query_out)

    empty_acc = jnp.zeros((item_count, length, HD), jnp.float32)
    (key_acc, value_acc), query_outs = lax.scan(
        query_block, (empty_acc, empty_acc), (query_blocks, grad_blocks)
    )
    query_out = query_outs.transpose(1, 0, 2, 3).reshape(item_count, length, HD)
    key_out = (score_scale * key_acc).astype(jnp.bfloat16)
    value_out = value_acc.astype(jnp.bfloat16)
    results = jnp.concatenate([query_out, key_out, value_out], axis=-1)[None]
    returned = lax.all_to_all(results, "seq", split_axis=2, concat_axis=0, tiled=True)
    returned = returned.reshape(blocks, heads_local, row_count, 3, HD).transpose(3, 0, 2, 1, 4)
    returned = returned.reshape(3, blocks, row_count, local_width)
    return (returned[0], returned[1], returned[2], hidden_grad, weight_grad)


def solution(mesh):
    token = P(("groups", "batch"), "seq", "chan")
    sizes = dict(mesh.shape)

    def run(*arrays):
        blocks = arrays[0].shape[0] // (sizes["groups"] * sizes["batch"])
        fits = blocks == sizes["seq"] == 4 and sizes["batch"] == 2 and sizes["chan"] == 2
        return jax.shard_map(
            per_device if fits else per_device_general,
            mesh=mesh,
            in_specs=(token,) * 5 + (P(None, None, "chan"),),
            out_specs=(token,) * 4 + (P(("groups", "seq", "batch"), None, "chan"),),
            check_vma=False,
        )(*arrays)

    return run
```

```python
import functools
import math

import jax
import jax.numpy as jnp
from jax import lax
from jax.experimental import pallas as pl
from jax.experimental.pallas import tpu as pltpu
from jax.sharding import PartitionSpec as P

HD = 96
BF = jnp.bfloat16
F32 = jnp.float32
COST = 8
VMEM_LIMIT = 40 * 1024 * 1024


def tanh_gelu(signal):
    inner_arg = 0.7978845608 * (signal + 0.044715 * signal * signal * signal)
    return 0.5 * signal * (1.0 + jnp.tanh(inner_arg))


def gelu_slope(signal):
    inner_arg = 0.7978845608 * (signal + 0.044715 * signal * signal * signal)
    hyper = jnp.tanh(inner_arg)
    return 0.5 * (1.0 + hyper) + 0.5 * signal * (1.0 - hyper * hyper) * 0.7978845608 * (
        1.0 + 3.0 * 0.044715 * signal * signal
    )


def kernel_call(
    body, outs, flops=0, transcendentals=0, name=None, scratch=(), space=pltpu.VMEM,
    out_space=pltpu.VMEM,
):
    given, made = (pl.BlockSpec(memory_space=x) for x in (space, out_space))

    def call(*args):
        if space == pltpu.HBM:
            args = [pltpu.with_memory_space_constraint(a, pltpu.HBM) for a in args]
        moved = sum(math.prod(a.shape) * a.dtype.itemsize for a in args)
        moved += sum(math.prod(o.shape) * o.dtype.itemsize for o in outs)
        return pl.pallas_call(
            body,
            out_shape=list(outs),
            in_specs=[given] * len(args),
            out_specs=[made] * len(outs),
            scratch_shapes=list(scratch),
            compiler_params=pltpu.CompilerParams(vmem_limit_bytes=VMEM_LIMIT),
            cost_estimate=pl.CostEstimate(
                flops=flops, bytes_accessed=moved, transcendentals=transcendentals
            ),
            name=name,
        )(*args)

    return call


def shape(dims, dtype=BF):
    return jax.ShapeDtypeStruct(dims, dtype)


def fetch(pairs, sems):
    copies = [pltpu.make_async_copy(src, dst, sems.at[i]) for i, (src, dst) in enumerate(pairs)]
    for copy in copies:
        copy.start()
    return copies


def near_kernel(cot, q, k, v, beside, mirror, sems):
    s = lax.axis_index("seq")
    blocks = cot.shape[0]
    pairs = []
    for out, d in ((beside, 1), (mirror, 3)):
        pairs.append((cot, out.at[pl.ds(0, blocks)]))
        pairs += [(x.at[s ^ d], out.at[blocks + j]) for j, x in enumerate((q, k, v))]
    for copy in fetch(pairs, sems):
        copy.wait()


def rest_kernel(hidden, q, k, v, w, own, opposite, w_ref, slope_ref, act_ref, sent_ref, h_ref, sems):
    s = lax.axis_index("seq")
    c = lax.axis_index("chan")
    pairs = [(hidden, h_ref)]
    for out, b in ((opposite, s ^ 2), (own, s)):
        pairs += [(x.at[b], out.at[j]) for j, x in enumerate((q, k, v))]
    pairs.append((w, w_ref))
    copies = fetch(pairs, sems)
    copies[0].wait()
    blocks, rows, width = h_ref.shape
    signal = h_ref[...].astype(F32)
    slope_ref[...] = gelu_slope(signal)
    act_t = tanh_gelu(signal).reshape(blocks * rows, width).T.astype(BF)
    lanes = act_t.shape[1] // 2
    parts = width // lanes
    halves = act_t[:, :lanes], act_t[:, lanes:]
    first = c == 0
    kept, sent = jnp.where(first, *halves), jnp.where(first, halves[1], halves[0])
    for out, half in ((act_ref, kept), (sent_ref, sent)):
        for i in range(2 * parts):
            out[i // parts, :, pl.ds(i % parts * lanes, lanes)] = half[i * rows : (i + 1) * rows]
    for copy in copies[1:]:
        copy.wait()


def conv_term(tap, w_ref, t, side):
    width = w_ref.shape[2]
    start = pl.multiple_of(side * width, width)
    return lax.dot_general(
        tap,
        w_ref[t, pl.ds(start, width), :],
        (((1,), (1,)), ((), ())),
        preferred_element_type=F32,
    )


def centre_kernel(cot_ref, w_ref, mine_ref, other_ref):
    c = lax.axis_index("chan")
    blocks = cot_ref.shape[0] - 3
    tap = cot_ref[:blocks].reshape(mine_ref.shape)
    mine_ref[...] = conv_term(tap, w_ref, 1, c)
    other_ref[...] = conv_term(tap, w_ref, 1, 1 - c)


def conv_kernel(mine, beside_ref, mirror_ref, w_ref, centre_ref, out_ref):
    c = lax.axis_index("chan")
    even = lax.rem(lax.axis_index("seq"), 2) == 0
    blocks = out_ref.shape[0]
    beside = beside_ref[:blocks].reshape(centre_ref.shape)
    mirror = mirror_ref[:blocks].reshape(centre_ref.shape)
    side = c if mine else 1 - c
    total = (
        centre_ref[...]
        + conv_term(jnp.where(even, beside, mirror), w_ref, 0, side)
        + conv_term(jnp.where(even, mirror, beside), w_ref, 2, side)
    )
    out_ref[...] = total.astype(BF).reshape(out_ref.shape)


def grad_kernel(
    cot_ref, slope_ref, mine_ref, got_ref, act_ref, act_peer, beside_ref, mirror_ref, to_mirror,
    own, beside, opposite, mirror, end,
):
    s = lax.axis_index("seq")
    c = lax.axis_index("chan")
    blocks = mine_ref.shape[0]
    for d, out in ((1, beside), (3, mirror), (2, opposite), (0, own)):
        b = s ^ d
        back = mine_ref[b].astype(F32) + got_ref[b].astype(F32)
        out[0] = (cot_ref[b].astype(F32) + back * slope_ref[b]).astype(BF)
        k = lax.rem(b, 2)
        out[1] = jnp.where(lax.div(b, 2) == c, act_ref[k], act_peer[k])
    end[:3] = to_mirror[blocks:]
    end[3:] = mirror[:2]
    beside[2:] = mirror_ref[:blocks]
    mirror[2:] = beside_ref[:blocks]


def pick_kernel(held_ref, out_ref):
    out_ref[...] = held_ref[2:]


def attention_kernel(
    count, own_qkv, own, beside_qkv, mirror_qkv, opposite_qkv, end, beside, mirror, opposite, *outs
):
    outs, act_ref = outs[:count], outs[count]
    rows, width = own.shape[1:]
    near = beside_qkv.shape[0] - 3
    scale = 1.0 / math.sqrt(HD)
    s = lax.axis_index("seq")
    at_end = jnp.logical_or(s == 0, s == count - 1)

    def positions(j):
        facing = jnp.where(at_end, end[j], mirror_qkv[near + j])
        return jnp.concatenate([own_qkv[j], beside_qkv[near + j], opposite_qkv[j], facing], axis=0)

    query, key, value = (positions(j) for j in range(3))
    grad, act = (
        (own[j], beside[j], opposite[j], jnp.where(at_end, end[3 + j], mirror[j]))
        for j in range(2)
    )
    grad = jnp.concatenate(grad, axis=0)
    for d in range(count):
        act_ref[d] = act[d]
    nt = (((1,), (1,)), ((), ()))
    nn = (((1,), (0,)), ((), ()))
    tn = (((0,), (0,)), ((), ()))
    dot = functools.partial(lax.dot_general, preferred_element_type=F32)
    results = ([], [], [])
    for h in range(width // HD):
        cols = slice(h * HD, (h + 1) * HD)
        q, k, v, g = query[:, cols], key[:, cols], value[:, cols], grad[:, cols]
        scores = dot(k, q, nt) * scale
        raised = jnp.exp(scores - jnp.max(scores, axis=0, keepdims=True))
        prob = raised * (1.0 / jnp.sum(raised, axis=0, keepdims=True))
        d_prob = dot(v, g, nt)
        row_total = jnp.sum(prob * d_prob, axis=0, keepdims=True)
        d_score = (prob * (d_prob - row_total)).astype(BF)
        results[0].append((dot(d_score, k, tn) * scale).astype(BF))
        results[1].append((dot(d_score, q, nn) * scale).astype(BF))
        results[2].append(dot(prob.astype(BF), g, nn).astype(BF))
    for j in range(3):
        whole = jnp.concatenate(results[j], axis=1)
        for d in range(count):
            outs[d][j] = whole[d * rows : (d + 1) * rows]


def weight_kernel(
    count, factor, cot_ref, beside, mirror, beside2, mirror2, farthest, act_ref, act_peer, own,
    to_beside, to_opposite, to_mirror, own_ref, sent0_ref, sent1_ref, grad_ref, act_buf, cot_buf,
):
    s = lax.axis_index("seq")
    c = lax.axis_index("chan")
    b = lax.axis_index("batch")
    blocks, rows, width = grad_ref.shape
    for d, piece in enumerate((own, to_beside, to_opposite, to_mirror)):
        grad_ref[s ^ d] = piece[0]
    lanes = act_buf.shape[2] // 2
    for d in range(count):
        halves = (
            jnp.where(c == 0, act_ref[d], act_peer[d]),
            jnp.where(c == 0, act_peer[d], act_ref[d]),
        )
        for r in range(width // lanes):
            for h in range(2):
                act_buf[s ^ d, pl.ds(r * rows, rows), pl.ds(h * lanes, lanes)] = halves[h][
                    :, r * lanes : (r + 1) * lanes
                ]
    flat = cot_buf.shape[1:]
    at_end = jnp.logical_or(s == 0, s == count - 1)
    cot_buf[s] = cot_ref[:blocks].reshape(flat)
    cot_buf[s ^ 1] = beside[:blocks].reshape(flat)
    cot_buf[s ^ 3] = jnp.where(at_end, farthest[...], mirror[:blocks]).reshape(flat)
    cot_buf[s ^ 2] = jnp.where(at_end, beside2[2:], mirror2[2:]).reshape(flat)

    half = own_ref.shape[1]
    for t in range(3):
        low = max(0, 1 - t)
        high = min(count, count + 1 - t)
        for is_own, side in ((False, 1 - b), (True, b)):
            start = pl.multiple_of(side * half, half)
            total = None
            for j in range(low, high):
                term = jnp.dot(
                    act_buf[j + t - 1, pl.ds(start, half), :],
                    cot_buf[j],
                    preferred_element_type=F32,
                )
                total = term if total is None else total + term
            total = factor * total
            if is_own:
                own_ref[t] = total
            else:
                sent0_ref[t] = total[: half // 2].astype(BF)
                sent1_ref[t] = total[half // 2 :].astype(BF)


def add_kernel(own_ref, got0_ref, got1_ref, out_ref):
    half = got0_ref.shape[1]
    out_ref[:, :half] = own_ref[:, :half] + got0_ref[...].astype(F32)
    out_ref[:, half:] = own_ref[:, half:] + got1_ref[...].astype(F32)


def place_kernel(count, *refs):
    pieces, outs, sems = refs[:count], refs[count:-1], refs[-1]
    s = lax.axis_index("seq")
    pairs = [(pieces[d].at[j], outs[j].at[s ^ d]) for d in range(count) for j in range(3)]
    for copy in fetch(pairs, sems):
        copy.wait()


def swap(x, axis, by, only=None):
    n = lax.axis_size(axis)
    return lax.ppermute(x, axis, [(i, i ^ by) for i in range(n) if only is None or i in only])


def after(first, *then):
    held = lax.optimization_barrier((first, *then))
    return held[1:]


def per_device(query_vectors, key_vectors, value_vectors, hidden, cotangent, conv_weight):
    count = lax.axis_size("seq")
    blocks, rows, width = hidden.shape
    tokens = blocks * rows
    factor = 1.0 / math.sqrt(tokens * count * lax.axis_size("batch"))
    weights = conv_weight.transpose(1, 0, 2)
    part = width // 2
    middle, ends = (1, 2), (0, 3)

    def units(n):
        return shape((n, rows, width))

    to_beside, to_mirror = kernel_call(
        near_kernel,
        [units(blocks + 3)] * 2,
        name="near",
        scratch=[pltpu.SemaphoreType.DMA((8,))],
        space=pltpu.HBM,
    )(cotangent, query_vectors, key_vectors, value_vectors)
    beside = swap(to_beside, "seq", 1)
    mirror = swap(to_mirror, "seq", 3, middle)
    (hidden,) = after(to_beside, hidden)
    own_qkv, to_opposite, weights, slope, act, act_sent = kernel_call(
        rest_kernel,
        [units(3)] * 2 + [shape(weights.shape), shape(hidden.shape, F32), units(2), units(2)],
        name="rest",
        scratch=[pltpu.VMEM(hidden.shape, BF), pltpu.SemaphoreType.DMA((8,))],
        space=pltpu.HBM,
    )(hidden, query_vectors, key_vectors, value_vectors, weights)
    act_got = swap(act_sent, "chan", 1)
    opposite = swap(to_opposite, "seq", 2)

    flat = shape((tokens, width), F32)
    centre_mine, centre_other = kernel_call(centre_kernel, [flat] * 2, name="conv_centre")(
        to_beside, weights
    )
    (other,) = kernel_call(
        functools.partial(conv_kernel, False), [units(blocks)], name="conv_other"
    )(beside, mirror, weights, centre_other)
    got = swap(other, "chan", 1)
    (centre_mine,) = after(other, centre_mine)
    (mine,) = kernel_call(functools.partial(conv_kernel, True), [units(blocks)], name="conv_mine")(
        beside, mirror, weights, centre_mine
    )
    own, to_beside2, to_opposite2, to_mirror2, to_end2 = kernel_call(
        grad_kernel,
        [units(2), units(blocks + 2), units(2), units(blocks + 2), units(5)],
        name="hidden_grad",
    )(to_beside, slope, mine, got, act, act_got, beside, mirror, to_mirror)
    beside2 = swap(to_beside2, "seq", 1)
    mirror2 = swap(to_mirror2, "seq", 3, middle)
    far_opposite, far_end = after(opposite, to_opposite2, to_end2)
    opposite2 = swap(far_opposite, "seq", 2)
    end2 = swap(far_end, "seq", 3, ends)
    (far,) = kernel_call(pick_kernel, [units(blocks)], name="pick")(mirror2)
    farthest = lax.ppermute(far, "seq", [(1, 0), (2, 3)])

    item = 5 * (count * rows) ** 2 * width
    *returned, act_held = kernel_call(
        functools.partial(attention_kernel, count),
        [units(3)] * count + [units(count)],
        flops=COST * 2 * item,
        transcendentals=(count * rows) ** 2 * (width // HD),
        name="attention",
    )(own_qkv, own, beside, mirror, opposite, end2, beside2, mirror2, opposite2)
    back = [returned[0]] + [swap(returned[d], "seq", d) for d in range(1, count)]

    act_peer = swap(act_held, "chan", 1)
    total, sent0, sent1, hidden_grad = kernel_call(
        functools.partial(weight_kernel, count, factor),
        [shape((3, part // 2, width), F32)] + [shape((3, part // 4, width))] * 2 + [units(blocks)],
        name="weight_grad",
        scratch=[
            pltpu.VMEM((count, part, tokens), BF),
            pltpu.VMEM((count, tokens, width), BF),
        ],
    )(
        to_beside, beside, mirror, beside2, mirror2, farthest, act_held, act_peer, own, to_beside2,
        to_opposite2, to_mirror2,
    )
    got_sums = [swap(x, "batch", 1) for x in (sent0, sent1)]
    (weight_grad,) = kernel_call(add_kernel, [shape((3, part // 2, width), F32)], name="add_weight")(
        total, *got_sums
    )
    (back[0],) = after(weight_grad, back[0])
    query_grad, key_grad, value_grad = kernel_call(
        functools.partial(place_kernel, count),
        [units(blocks)] * 3,
        name="place",
        scratch=[pltpu.SemaphoreType.DMA((3 * count,))],
        out_space=pltpu.HBM,
    )(*back)
    return (query_grad, key_grad, value_grad, hidden_grad, weight_grad.transpose(1, 0, 2))


def from_behind(shard, axis, by):
    length = lax.axis_size(axis)
    pairs = [(i, i + by) for i in range(length) if 0 <= i + by < length]
    return lax.ppermute(shard, axis, pairs)


def per_device_general(query_vectors, key_vectors, value_vectors, hidden, cotangent, conv_weight):
    seq_count = lax.axis_size("seq")
    batch_count = lax.axis_size("batch")
    partner_gap = seq_count // 4
    blocks, row_count, local_width = hidden.shape
    tokens_all = blocks * batch_count * row_count * seq_count
    factor = 1.0 / math.sqrt(tokens_all)
    hidden_f = hidden.astype(jnp.float32)
    activation = tanh_gelu(hidden_f).astype(jnp.bfloat16)
    act_full = lax.all_gather(activation, "chan", axis=2, tiled=True)

    def partner(offset):
        return from_behind(cotangent, "seq", offset)

    cot_before = partner(partner_gap)
    cot_after = partner(-partner_gap)
    cot_taps = jnp.stack([cot_after, cotangent, cot_before])
    back_part = jnp.einsum(
        "tbqo,ito->bqi", cot_taps, conv_weight, preferred_element_type=jnp.float32
    )
    back_sum = lax.psum_scatter(
        back_part.astype(jnp.bfloat16), "chan", scatter_dimension=2, tiled=True
    ).astype(jnp.float32)
    hidden_grad = (cotangent.astype(jnp.float32) + back_sum * gelu_slope(hidden_f)).astype(
        jnp.bfloat16
    )
    weight_grad = lax.psum_scatter(
        factor
        * jnp.einsum("bpi,tbpo->ito", act_full, cot_taps, preferred_element_type=jnp.float32),
        ("seq", "batch"),
        scatter_dimension=0,
        tiled=True,
    )
    heads_local = local_width // HD

    def to_heads(signal):
        return signal.reshape(blocks, row_count, heads_local, HD)

    stacked = jnp.stack(
        [
            to_heads(query_vectors),
            to_heads(key_vectors),
            to_heads(value_vectors),
            to_heads(hidden_grad),
        ],
        axis=3,
    )
    stacked = stacked.transpose(0, 2, 1, 3, 4).reshape(
        seq_count, blocks * heads_local // seq_count, row_count, 4 * HD
    )
    gathered = lax.all_to_all(stacked, "seq", split_axis=0, concat_axis=2, tiled=True)
    item_count = gathered.shape[1]
    length = gathered.shape[2]
    columns = gathered[0].reshape(item_count, length, 4, HD)
    query_all = columns[:, :, 0]
    key_all = columns[:, :, 1]
    value_all = columns[:, :, 2]
    grad_all = columns[:, :, 3]
    score_scale = 1.0 / math.sqrt(HD)
    block_rows = math.gcd(length, 512)
    block_count = length // block_rows
    query_blocks = query_all.reshape(item_count, block_count, block_rows, HD).transpose(1, 0, 2, 3)
    grad_blocks = grad_all.reshape(item_count, block_count, block_rows, HD).transpose(1, 0, 2, 3)

    def query_block(carry, inputs):
        key_acc, value_acc = carry
        query_rows, grad_rows = inputs
        scores = (
            jnp.einsum("iqd,ikd->iqk", query_rows, key_all, preferred_element_type=jnp.float32)
            * score_scale
        )
        row_max = jnp.max(scores, axis=-1, keepdims=True)
        raised = jnp.exp(scores - row_max)
        probability = raised / jnp.sum(raised, axis=-1, keepdims=True)
        prob_b = probability.astype(jnp.bfloat16)
        value_acc = value_acc + jnp.einsum(
            "iqk,iqd->ikd", prob_b, grad_rows, preferred_element_type=jnp.float32
        )
        d_prob = jnp.einsum(
            "iqd,ikd->iqk", grad_rows, value_all, preferred_element_type=jnp.float32
        )
        row_total = jnp.sum(probability * d_prob, axis=-1, keepdims=True)
        d_score = (probability * (d_prob - row_total)).astype(jnp.bfloat16)
        query_out = (
            score_scale
            * jnp.einsum("iqk,ikd->iqd", d_score, key_all, preferred_element_type=jnp.float32)
        ).astype(jnp.bfloat16)
        key_acc = key_acc + jnp.einsum(
            "iqk,iqd->ikd", d_score, query_rows, preferred_element_type=jnp.float32
        )
        return ((key_acc, value_acc), query_out)

    empty_acc = jnp.zeros((item_count, length, HD), jnp.float32)
    (key_acc, value_acc), query_outs = lax.scan(
        query_block, (empty_acc, empty_acc), (query_blocks, grad_blocks)
    )
    query_out = query_outs.transpose(1, 0, 2, 3).reshape(item_count, length, HD)
    key_out = (score_scale * key_acc).astype(jnp.bfloat16)
    value_out = value_acc.astype(jnp.bfloat16)
    results = jnp.concatenate([query_out, key_out, value_out], axis=-1)[None]
    returned = lax.all_to_all(results, "seq", split_axis=2, concat_axis=0, tiled=True)
    returned = returned.reshape(blocks, heads_local, row_count, 3, HD).transpose(3, 0, 2, 1, 4)
    returned = returned.reshape(3, blocks, row_count, local_width)
    return (returned[0], returned[1], returned[2], hidden_grad, weight_grad)


def solution(mesh):
    token = P(("groups", "batch"), "seq", "chan")
    sizes = dict(mesh.shape)

    def run(*arrays):
        blocks = arrays[0].shape[0] // (sizes["groups"] * sizes["batch"])
        fits = blocks == sizes["seq"] == 4 and sizes["batch"] == 2 and sizes["chan"] == 2
        return jax.shard_map(
            per_device if fits else per_device_general,
            mesh=mesh,
            in_specs=(token,) * 5 + (P(None, None, "chan"),),
            out_specs=(token,) * 4 + (P(("groups", "seq", "batch"), None, "chan"),),
            check_vma=False,
        )(*arrays)

    return run
```

```python
import functools
import math

import jax
import jax.numpy as jnp
from jax import lax
from jax.experimental import pallas as pl
from jax.experimental.pallas import tpu as pltpu
from jax.sharding import PartitionSpec as P

HD = 96
BF = jnp.bfloat16
F32 = jnp.float32
COST = 8
VMEM_LIMIT = 40 * 1024 * 1024


def tanh_gelu(signal):
    inner_arg = 0.7978845608 * (signal + 0.044715 * signal * signal * signal)
    return 0.5 * signal * (1.0 + jnp.tanh(inner_arg))


def gelu_slope(signal):
    inner_arg = 0.7978845608 * (signal + 0.044715 * signal * signal * signal)
    hyper = jnp.tanh(inner_arg)
    return 0.5 * (1.0 + hyper) + 0.5 * signal * (1.0 - hyper * hyper) * 0.7978845608 * (
        1.0 + 3.0 * 0.044715 * signal * signal
    )


def kernel_call(
    body, outs, flops=0, transcendentals=0, name=None, scratch=(), space=pltpu.VMEM,
    out_space=pltpu.VMEM,
):
    given, made = (pl.BlockSpec(memory_space=x) for x in (space, out_space))

    def call(*args):
        if space == pltpu.HBM:
            args = [pltpu.with_memory_space_constraint(a, pltpu.HBM) for a in args]
        moved = sum(math.prod(a.shape) * a.dtype.itemsize for a in args)
        moved += sum(math.prod(o.shape) * o.dtype.itemsize for o in outs)
        return pl.pallas_call(
            body,
            out_shape=list(outs),
            in_specs=[given] * len(args),
            out_specs=[made] * len(outs),
            scratch_shapes=list(scratch),
            compiler_params=pltpu.CompilerParams(vmem_limit_bytes=VMEM_LIMIT),
            cost_estimate=pl.CostEstimate(
                flops=flops, bytes_accessed=moved, transcendentals=transcendentals
            ),
            name=name,
        )(*args)

    return call


def shape(dims, dtype=BF):
    return jax.ShapeDtypeStruct(dims, dtype)


def fetch(pairs, sems):
    copies = [pltpu.make_async_copy(src, dst, sems.at[i]) for i, (src, dst) in enumerate(pairs)]
    for copy in copies:
        copy.start()
    return copies


def near_kernel(cot, q, k, v, beside, mirror, sems):
    s = lax.axis_index("seq")
    blocks = cot.shape[0]
    pairs = []
    for out, d in ((beside, 1), (mirror, 3)):
        pairs.append((cot, out.at[pl.ds(0, blocks)]))
        pairs += [(x.at[s ^ d], out.at[blocks + j]) for j, x in enumerate((q, k, v))]
    for copy in fetch(pairs, sems):
        copy.wait()


def rest_kernel(hidden, q, k, v, w, own, opposite, w_ref, slope_ref, act_ref, sent_ref, h_ref, sems):
    s = lax.axis_index("seq")
    c = lax.axis_index("chan")
    pairs = [(hidden, h_ref)]
    for out, b in ((opposite, s ^ 2), (own, s)):
        pairs += [(x.at[b], out.at[j]) for j, x in enumerate((q, k, v))]
    pairs.append((w, w_ref))
    copies = fetch(pairs, sems)
    copies[0].wait()
    blocks, rows, width = h_ref.shape
    signal = h_ref[...].astype(F32)
    slope_ref[...] = gelu_slope(signal)
    act_t = tanh_gelu(signal).reshape(blocks * rows, width).T.astype(BF)
    lanes = act_t.shape[1] // 2
    parts = width // lanes
    halves = act_t[:, :lanes], act_t[:, lanes:]
    first = c == 0
    kept, sent = jnp.where(first, *halves), jnp.where(first, halves[1], halves[0])
    for out, half in ((act_ref, kept), (sent_ref, sent)):
        for i in range(2 * parts):
            out[i // parts, :, pl.ds(i % parts * lanes, lanes)] = half[i * rows : (i + 1) * rows]
    for copy in copies[1:]:
        copy.wait()


def conv_term(tap, w_ref, t, side):
    width = w_ref.shape[2]
    start = pl.multiple_of(side * width, width)
    return lax.dot_general(
        tap,
        w_ref[t, pl.ds(start, width), :],
        (((1,), (1,)), ((), ())),
        preferred_element_type=F32,
    )


def chosen(block, act_ref, act_peer):
    k = lax.rem(block, 2)
    return jnp.where(lax.div(block, 2) == lax.axis_index("chan"), act_ref[k], act_peer[k])


def centre_kernel(cot_ref, w_ref, qkv, act_ref, act_peer, mine_ref, other_ref, opposite):
    c = lax.axis_index("chan")
    blocks = cot_ref.shape[0] - 3
    opposite[:3] = qkv[...]
    opposite[3] = chosen(lax.axis_index("seq") ^ 2, act_ref, act_peer)
    tap = cot_ref[:blocks].reshape(mine_ref.shape)
    mine_ref[...] = conv_term(tap, w_ref, 1, c)
    other_ref[...] = conv_term(tap, w_ref, 1, 1 - c)


def conv_kernel(mine, beside_ref, mirror_ref, w_ref, centre_ref, *outs):
    c = lax.axis_index("chan")
    even = lax.rem(lax.axis_index("seq"), 2) == 0
    blocks = beside_ref.shape[0] - 3
    beside = beside_ref[:blocks].reshape(centre_ref.shape)
    mirror = mirror_ref[:blocks].reshape(centre_ref.shape)
    side = c if mine else 1 - c
    total = (
        centre_ref[...]
        + conv_term(jnp.where(even, beside, mirror), w_ref, 0, side)
        + conv_term(jnp.where(even, mirror, beside), w_ref, 2, side)
    ).astype(BF)
    rows = total.shape[0] // len(outs)
    for i, out in enumerate(outs):
        out[...] = total[i * rows : (i + 1) * rows].reshape(out.shape)


def grad_kernel(
    cot_ref, slope_ref, mine_ref, got0_ref, got1_ref, act_ref, act_peer, beside_ref, mirror_ref,
    to_mirror, own, beside, opposite, mirror, end,
):
    s = lax.axis_index("seq")
    blocks = mine_ref.shape[0]
    for d, out in ((1, beside), (3, mirror), (2, opposite), (0, own)):
        b = s ^ d
        i = lax.rem(b, 2)
        got = jnp.where(b < 2, got0_ref[i], got1_ref[i])
        back = mine_ref[b].astype(F32) + got.astype(F32)
        out[0] = (cot_ref[b].astype(F32) + back * slope_ref[b]).astype(BF)
        if d != 2:
            out[1] = chosen(b, act_ref, act_peer)
    end[:3] = to_mirror[blocks:]
    end[3:] = mirror[:2]
    beside[2:] = mirror_ref[:blocks]
    mirror[2:] = beside_ref[:blocks]


def pick_kernel(held_ref, out_ref):
    out_ref[...] = held_ref[2:]


def gather_kernel(own, beside, opposite, out_ref):
    for d, piece in enumerate((own[1], beside[1], opposite[3])):
        out_ref[d] = piece


def attention_kernel(
    count, own_qkv, own, beside_qkv, mirror_qkv, opposite_qkv, end, beside, mirror, opposite, *outs
):
    outs, act_ref = outs[:count], outs[count]
    rows, width = own.shape[1:]
    near = beside_qkv.shape[0] - 3
    scale = 1.0 / math.sqrt(HD)
    s = lax.axis_index("seq")
    at_end = jnp.logical_or(s == 0, s == count - 1)

    def positions(j):
        facing = jnp.where(at_end, end[j], mirror_qkv[near + j])
        return jnp.concatenate([own_qkv[j], beside_qkv[near + j], opposite_qkv[j], facing], axis=0)

    query, key, value = (positions(j) for j in range(3))
    facing, act_ref[0] = (jnp.where(at_end, end[3 + j], mirror[j]) for j in range(2))
    grad = jnp.concatenate([own[0], beside[0], opposite[0], facing], axis=0)
    nt = (((1,), (1,)), ((), ()))
    nn = (((1,), (0,)), ((), ()))
    tn = (((0,), (0,)), ((), ()))
    dot = functools.partial(lax.dot_general, preferred_element_type=F32)
    results = ([], [], [])
    for h in range(width // HD):
        cols = slice(h * HD, (h + 1) * HD)
        q, k, v, g = query[:, cols], key[:, cols], value[:, cols], grad[:, cols]
        scores = dot(k, q, nt) * scale
        raised = jnp.exp(scores - jnp.max(scores, axis=0, keepdims=True))
        prob = raised * (1.0 / jnp.sum(raised, axis=0, keepdims=True))
        d_prob = dot(v, g, nt)
        row_total = jnp.sum(prob * d_prob, axis=0, keepdims=True)
        d_score = (prob * (d_prob - row_total)).astype(BF)
        results[0].append((dot(d_score, k, tn) * scale).astype(BF))
        results[1].append((dot(d_score, q, nn) * scale).astype(BF))
        results[2].append(dot(prob.astype(BF), g, nn).astype(BF))
    for j in range(3):
        whole = jnp.concatenate(results[j], axis=1)
        for d in range(count):
            outs[d][j] = whole[d * rows : (d + 1) * rows]


def weight_kernel(
    count, factor, cot_ref, beside, mirror, beside2, mirror2, farthest, act_ref, act_peer,
    act_last, peer_last, own, to_beside, to_opposite, to_mirror, own_ref, sent0_ref, sent1_ref, grad_ref, act_buf, cot_buf,
):
    s = lax.axis_index("seq")
    c = lax.axis_index("chan")
    b = lax.axis_index("batch")
    blocks, rows, width = grad_ref.shape
    for d, piece in enumerate((own, to_beside, to_opposite, to_mirror)):
        grad_ref[s ^ d] = piece[0]
    lanes = act_buf.shape[2] // 2
    for d in range(count):
        held, came = (act_ref[d], act_peer[d]) if d < 3 else (act_last[0], peer_last[0])
        halves = jnp.where(c == 0, held, came), jnp.where(c == 0, came, held)
        for r in range(width // lanes):
            for h in range(2):
                act_buf[s ^ d, pl.ds(r * rows, rows), pl.ds(h * lanes, lanes)] = halves[h][
                    :, r * lanes : (r + 1) * lanes
                ]
    flat = cot_buf.shape[1:]
    at_end = jnp.logical_or(s == 0, s == count - 1)
    cot_buf[s] = cot_ref[:blocks].reshape(flat)
    cot_buf[s ^ 1] = beside[:blocks].reshape(flat)
    cot_buf[s ^ 3] = jnp.where(at_end, farthest[...], mirror[:blocks]).reshape(flat)
    cot_buf[s ^ 2] = jnp.where(at_end, beside2[2:], mirror2[2:]).reshape(flat)

    half = own_ref.shape[1]
    for t in range(3):
        low = max(0, 1 - t)
        high = min(count, count + 1 - t)
        for is_own, side in ((False, 1 - b), (True, b)):
            start = pl.multiple_of(side * half, half)
            total = None
            for j in range(low, high):
                term = jnp.dot(
                    act_buf[j + t - 1, pl.ds(start, half), :],
                    cot_buf[j],
                    preferred_element_type=F32,
                )
                total = term if total is None else total + term
            total = factor * total
            if is_own:
                own_ref[t] = total
            else:
                sent0_ref[t] = total[: half // 2].astype(BF)
                sent1_ref[t] = total[half // 2 :].astype(BF)


def add_kernel(own_ref, got0_ref, got1_ref, out_ref):
    half = got0_ref.shape[1]
    out_ref[:, :half] = own_ref[:, :half] + got0_ref[...].astype(F32)
    out_ref[:, half:] = own_ref[:, half:] + got1_ref[...].astype(F32)


def place_kernel(count, *refs):
    pieces, outs, sems = refs[:count], refs[count:-1], refs[-1]
    s = lax.axis_index("seq")
    pairs = [(pieces[d].at[j], outs[j].at[s ^ d]) for d in range(count) for j in range(3)]
    for copy in fetch(pairs, sems):
        copy.wait()


def swap(x, axis, by, only=None):
    n = lax.axis_size(axis)
    return lax.ppermute(x, axis, [(i, i ^ by) for i in range(n) if only is None or i in only])


def after(first, *then):
    held = lax.optimization_barrier((first, *then))
    return held[1:]


def per_device(query_vectors, key_vectors, value_vectors, hidden, cotangent, conv_weight):
    count = lax.axis_size("seq")
    blocks, rows, width = hidden.shape
    tokens = blocks * rows
    factor = 1.0 / math.sqrt(tokens * count * lax.axis_size("batch"))
    weights = conv_weight.transpose(1, 0, 2)
    part = width // 2
    middle, ends = (1, 2), (0, 3)

    def units(n):
        return shape((n, rows, width))

    to_beside, to_mirror = kernel_call(
        near_kernel,
        [units(blocks + 3)] * 2,
        name="near",
        scratch=[pltpu.SemaphoreType.DMA((8,))],
        space=pltpu.HBM,
    )(cotangent, query_vectors, key_vectors, value_vectors)
    beside = swap(to_beside, "seq", 1)
    mirror = swap(to_mirror, "seq", 3, middle)
    (hidden,) = after(to_beside, hidden)
    own_qkv, opposite_qkv, weights, slope, act, act_sent = kernel_call(
        rest_kernel,
        [units(3)] * 2 + [shape(weights.shape), shape(hidden.shape, F32), units(2), units(2)],
        name="rest",
        scratch=[pltpu.VMEM(hidden.shape, BF), pltpu.SemaphoreType.DMA((8,))],
        space=pltpu.HBM,
    )(hidden, query_vectors, key_vectors, value_vectors, weights)
    act_got = swap(act_sent, "chan", 1)
    flat = shape((tokens, width), F32)
    centre_mine, centre_other, to_opposite = kernel_call(
        centre_kernel, [flat, flat, units(4)], name="conv_centre"
    )(to_beside, weights, opposite_qkv, act, act_got)
    opposite = swap(to_opposite, "seq", 2)
    others = kernel_call(
        functools.partial(conv_kernel, False), [units(blocks // 2)] * 2, name="conv_other"
    )(beside, mirror, weights, centre_other)
    got = [swap(x, "chan", 1) for x in others]
    (centre_mine,) = after(others[0], centre_mine)
    (mine,) = kernel_call(functools.partial(conv_kernel, True), [units(blocks)], name="conv_mine")(
        beside, mirror, weights, centre_mine
    )
    own, to_beside2, to_opposite2, to_mirror2, to_end2 = kernel_call(
        grad_kernel,
        [units(2), units(blocks + 2), units(1), units(blocks + 2), units(5)],
        name="hidden_grad",
    )(to_beside, slope, mine, *got, act, act_got, beside, mirror, to_mirror)
    beside2 = swap(to_beside2, "seq", 1)
    mirror2 = swap(to_mirror2, "seq", 3, middle)
    far_opposite, far_end = after(opposite, to_opposite2, to_end2)
    opposite2 = swap(far_opposite, "seq", 2)
    end2 = swap(far_end, "seq", 3, ends)
    (far,) = kernel_call(pick_kernel, [units(blocks)], name="pick")(mirror2)
    farthest = lax.ppermute(far, "seq", [(1, 0), (2, 3)])

    (act_held,) = kernel_call(gather_kernel, [units(3)], name="gather")(own, beside2, opposite)
    act_peer = swap(act_held, "chan", 1)
    (own_qkv,) = after(act_held, own_qkv)

    item = 5 * (count * rows) ** 2 * width
    *returned, act_last = kernel_call(
        functools.partial(attention_kernel, count),
        [units(3)] * count + [units(1)],
        flops=COST * 2 * item,
        transcendentals=(count * rows) ** 2 * (width // HD),
        name="attention",
    )(own_qkv, own, beside, mirror, opposite, end2, beside2, mirror2, opposite2)
    back = [returned[0]] + [swap(returned[d], "seq", d) for d in range(1, count)]

    peer_last = swap(act_last, "chan", 1)
    total, sent0, sent1, hidden_grad = kernel_call(
        functools.partial(weight_kernel, count, factor),
        [shape((3, part // 2, width), F32)] + [shape((3, part // 4, width))] * 2 + [units(blocks)],
        name="weight_grad",
        scratch=[
            pltpu.VMEM((count, part, tokens), BF),
            pltpu.VMEM((count, tokens, width), BF),
        ],
    )(
        to_beside, beside, mirror, beside2, mirror2, farthest, act_held, act_peer, act_last,
        peer_last, own, to_beside2, to_opposite2, to_mirror2,
    )
    got_sums = [swap(x, "batch", 1) for x in (sent0, sent1)]
    (weight_grad,) = kernel_call(add_kernel, [shape((3, part // 2, width), F32)], name="add_weight")(
        total, *got_sums
    )
    (back[0],) = after(weight_grad, back[0])
    query_grad, key_grad, value_grad = kernel_call(
        functools.partial(place_kernel, count),
        [units(blocks)] * 3,
        name="place",
        scratch=[pltpu.SemaphoreType.DMA((3 * count,))],
        out_space=pltpu.HBM,
    )(*back)
    return (query_grad, key_grad, value_grad, hidden_grad, weight_grad.transpose(1, 0, 2))


def from_behind(shard, axis, by):
    length = lax.axis_size(axis)
    pairs = [(i, i + by) for i in range(length) if 0 <= i + by < length]
    return lax.ppermute(shard, axis, pairs)


def per_device_general(query_vectors, key_vectors, value_vectors, hidden, cotangent, conv_weight):
    seq_count = lax.axis_size("seq")
    batch_count = lax.axis_size("batch")
    partner_gap = seq_count // 4
    blocks, row_count, local_width = hidden.shape
    tokens_all = blocks * batch_count * row_count * seq_count
    factor = 1.0 / math.sqrt(tokens_all)
    hidden_f = hidden.astype(jnp.float32)
    activation = tanh_gelu(hidden_f).astype(jnp.bfloat16)
    act_full = lax.all_gather(activation, "chan", axis=2, tiled=True)

    def partner(offset):
        return from_behind(cotangent, "seq", offset)

    cot_before = partner(partner_gap)
    cot_after = partner(-partner_gap)
    cot_taps = jnp.stack([cot_after, cotangent, cot_before])
    back_part = jnp.einsum(
        "tbqo,ito->bqi", cot_taps, conv_weight, preferred_element_type=jnp.float32
    )
    back_sum = lax.psum_scatter(
        back_part.astype(jnp.bfloat16), "chan", scatter_dimension=2, tiled=True
    ).astype(jnp.float32)
    hidden_grad = (cotangent.astype(jnp.float32) + back_sum * gelu_slope(hidden_f)).astype(
        jnp.bfloat16
    )
    weight_grad = lax.psum_scatter(
        factor
        * jnp.einsum("bpi,tbpo->ito", act_full, cot_taps, preferred_element_type=jnp.float32),
        ("seq", "batch"),
        scatter_dimension=0,
        tiled=True,
    )
    heads_local = local_width // HD

    def to_heads(signal):
        return signal.reshape(blocks, row_count, heads_local, HD)

    stacked = jnp.stack(
        [
            to_heads(query_vectors),
            to_heads(key_vectors),
            to_heads(value_vectors),
            to_heads(hidden_grad),
        ],
        axis=3,
    )
    stacked = stacked.transpose(0, 2, 1, 3, 4).reshape(
        seq_count, blocks * heads_local // seq_count, row_count, 4 * HD
    )
    gathered = lax.all_to_all(stacked, "seq", split_axis=0, concat_axis=2, tiled=True)
    item_count = gathered.shape[1]
    length = gathered.shape[2]
    columns = gathered[0].reshape(item_count, length, 4, HD)
    query_all = columns[:, :, 0]
    key_all = columns[:, :, 1]
    value_all = columns[:, :, 2]
    grad_all = columns[:, :, 3]
    score_scale = 1.0 / math.sqrt(HD)
    block_rows = math.gcd(length, 512)
    block_count = length // block_rows
    query_blocks = query_all.reshape(item_count, block_count, block_rows, HD).transpose(1, 0, 2, 3)
    grad_blocks = grad_all.reshape(item_count, block_count, block_rows, HD).transpose(1, 0, 2, 3)

    def query_block(carry, inputs):
        key_acc, value_acc = carry
        query_rows, grad_rows = inputs
        scores = (
            jnp.einsum("iqd,ikd->iqk", query_rows, key_all, preferred_element_type=jnp.float32)
            * score_scale
        )
        row_max = jnp.max(scores, axis=-1, keepdims=True)
        raised = jnp.exp(scores - row_max)
        probability = raised / jnp.sum(raised, axis=-1, keepdims=True)
        prob_b = probability.astype(jnp.bfloat16)
        value_acc = value_acc + jnp.einsum(
            "iqk,iqd->ikd", prob_b, grad_rows, preferred_element_type=jnp.float32
        )
        d_prob = jnp.einsum(
            "iqd,ikd->iqk", grad_rows, value_all, preferred_element_type=jnp.float32
        )
        row_total = jnp.sum(probability * d_prob, axis=-1, keepdims=True)
        d_score = (probability * (d_prob - row_total)).astype(jnp.bfloat16)
        query_out = (
            score_scale
            * jnp.einsum("iqk,ikd->iqd", d_score, key_all, preferred_element_type=jnp.float32)
        ).astype(jnp.bfloat16)
        key_acc = key_acc + jnp.einsum(
            "iqk,iqd->ikd", d_score, query_rows, preferred_element_type=jnp.float32
        )
        return ((key_acc, value_acc), query_out)

    empty_acc = jnp.zeros((item_count, length, HD), jnp.float32)
    (key_acc, value_acc), query_outs = lax.scan(
        query_block, (empty_acc, empty_acc), (query_blocks, grad_blocks)
    )
    query_out = query_outs.transpose(1, 0, 2, 3).reshape(item_count, length, HD)
    key_out = (score_scale * key_acc).astype(jnp.bfloat16)
    value_out = value_acc.astype(jnp.bfloat16)
    results = jnp.concatenate([query_out, key_out, value_out], axis=-1)[None]
    returned = lax.all_to_all(results, "seq", split_axis=2, concat_axis=0, tiled=True)
    returned = returned.reshape(blocks, heads_local, row_count, 3, HD).transpose(3, 0, 2, 1, 4)
    returned = returned.reshape(3, blocks, row_count, local_width)
    return (returned[0], returned[1], returned[2], hidden_grad, weight_grad)


def solution(mesh):
    token = P(("groups", "batch"), "seq", "chan")
    sizes = dict(mesh.shape)

    def run(*arrays):
        blocks = arrays[0].shape[0] // (sizes["groups"] * sizes["batch"])
        fits = blocks == sizes["seq"] == 4 and sizes["batch"] == 2 and sizes["chan"] == 2
        return jax.shard_map(
            per_device if fits else per_device_general,
            mesh=mesh,
            in_specs=(token,) * 5 + (P(None, None, "chan"),),
            out_specs=(token,) * 4 + (P(("groups", "seq", "batch"), None, "chan"),),
            check_vma=False,
        )(*arrays)

    return run
```

```python
import functools
import math

import jax
import jax.numpy as jnp
from jax import lax
from jax.experimental import pallas as pl
from jax.experimental.pallas import tpu as pltpu
from jax.sharding import PartitionSpec as P

HD = 96
BF = jnp.bfloat16
F32 = jnp.float32
COST = 8
VMEM_LIMIT = 40 * 1024 * 1024


def tanh_gelu(signal):
    inner_arg = 0.7978845608 * (signal + 0.044715 * signal * signal * signal)
    return 0.5 * signal * (1.0 + jnp.tanh(inner_arg))


def gelu_slope(signal):
    inner_arg = 0.7978845608 * (signal + 0.044715 * signal * signal * signal)
    hyper = jnp.tanh(inner_arg)
    return 0.5 * (1.0 + hyper) + 0.5 * signal * (1.0 - hyper * hyper) * 0.7978845608 * (
        1.0 + 3.0 * 0.044715 * signal * signal
    )


def kernel_call(
    body, outs, flops=0, transcendentals=0, name=None, scratch=(), space=pltpu.VMEM,
    out_space=pltpu.VMEM, bytes_too=True,
):
    given, made = (pl.BlockSpec(memory_space=x) for x in (space, out_space))

    def call(*args):
        if space == pltpu.HBM:
            args = [pltpu.with_memory_space_constraint(a, pltpu.HBM) for a in args]
        moved = sum(math.prod(a.shape) * a.dtype.itemsize for a in args)
        moved += sum(math.prod(o.shape) * o.dtype.itemsize for o in outs)
        return pl.pallas_call(
            body,
            out_shape=list(outs),
            in_specs=[given] * len(args),
            out_specs=[made] * len(outs),
            scratch_shapes=list(scratch),
            compiler_params=pltpu.CompilerParams(vmem_limit_bytes=VMEM_LIMIT),
            cost_estimate=pl.CostEstimate(
                flops=flops, bytes_accessed=moved * bytes_too, transcendentals=transcendentals
            ),
            name=name,
        )(*args)

    return call


def shape(dims, dtype=BF):
    return jax.ShapeDtypeStruct(dims, dtype)


def fetch(pairs, sems):
    copies = [pltpu.make_async_copy(src, dst, sems.at[i]) for i, (src, dst) in enumerate(pairs)]
    for copy in copies:
        copy.start()
    return copies


def near_kernel(cot, q, k, v, beside, mirror, sems):
    s = lax.axis_index("seq")
    blocks = cot.shape[0]
    pairs = []
    for out, d in ((beside, 1), (mirror, 3)):
        pairs.append((cot, out.at[pl.ds(0, blocks)]))
        pairs += [(x.at[s ^ d], out.at[blocks + j]) for j, x in enumerate((q, k, v))]
    for copy in fetch(pairs, sems):
        copy.wait()


def rest_kernel(hidden, q, k, v, w, own, opposite, w_ref, slope_ref, act_ref, sent_ref, h_ref, sems):
    s = lax.axis_index("seq")
    c = lax.axis_index("chan")
    pairs = [(hidden, h_ref)]
    for out, b in ((opposite, s ^ 2), (own, s)):
        pairs += [(x.at[b], out.at[j]) for j, x in enumerate((q, k, v))]
    pairs.append((w, w_ref))
    copies = fetch(pairs, sems)
    copies[0].wait()
    blocks, rows, width = h_ref.shape
    signal = h_ref[...].astype(F32)
    slope_ref[...] = gelu_slope(signal)
    act_t = tanh_gelu(signal).reshape(blocks * rows, width).T.astype(BF)
    lanes = act_t.shape[1] // 2
    parts = width // lanes
    halves = act_t[:, :lanes], act_t[:, lanes:]
    first = c == 0
    kept, sent = jnp.where(first, *halves), jnp.where(first, halves[1], halves[0])
    for out, half in ((act_ref, kept), (sent_ref, sent)):
        for i in range(2 * parts):
            out[i // parts, :, pl.ds(i % parts * lanes, lanes)] = half[i * rows : (i + 1) * rows]
    for copy in copies[1:]:
        copy.wait()


def conv_term(tap, w_ref, t, side):
    width = w_ref.shape[2]
    start = pl.multiple_of(side * width, width)
    return lax.dot_general(
        tap,
        w_ref[t, pl.ds(start, width), :],
        (((1,), (1,)), ((), ())),
        preferred_element_type=F32,
    )


def chosen(block, act_ref, act_peer):
    k = lax.rem(block, 2)
    return jnp.where(lax.div(block, 2) == lax.axis_index("chan"), act_ref[k], act_peer[k])


def centre_kernel(cot_ref, w_ref, qkv, act_ref, act_peer, mine_ref, other_ref, opposite):
    c = lax.axis_index("chan")
    blocks = cot_ref.shape[0] - 3
    opposite[:3] = qkv[...]
    opposite[3] = chosen(lax.axis_index("seq") ^ 2, act_ref, act_peer)
    tap = cot_ref[:blocks].reshape(mine_ref.shape)
    mine_ref[...] = conv_term(tap, w_ref, 1, c)
    other_ref[...] = conv_term(tap, w_ref, 1, 1 - c)


def conv_kernel(mine, beside_ref, mirror_ref, w_ref, centre_ref, *outs):
    c = lax.axis_index("chan")
    even = lax.rem(lax.axis_index("seq"), 2) == 0
    blocks = beside_ref.shape[0] - 3
    beside = beside_ref[:blocks].reshape(centre_ref.shape)
    mirror = mirror_ref[:blocks].reshape(centre_ref.shape)
    side = c if mine else 1 - c
    total = (
        centre_ref[...]
        + conv_term(jnp.where(even, beside, mirror), w_ref, 0, side)
        + conv_term(jnp.where(even, mirror, beside), w_ref, 2, side)
    ).astype(BF)
    rows = total.shape[0] // len(outs)
    for i, out in enumerate(outs):
        out[...] = total[i * rows : (i + 1) * rows].reshape(out.shape)


def grad_kernel(
    cot_ref, slope_ref, mine_ref, got0_ref, got1_ref, act_ref, act_peer, beside_ref, mirror_ref,
    to_mirror, own, beside, opposite, mirror, end,
):
    s = lax.axis_index("seq")
    blocks = mine_ref.shape[0]
    for d, out in ((1, beside), (3, mirror), (2, opposite), (0, own)):
        b = s ^ d
        i = lax.rem(b, 2)
        got = jnp.where(b < 2, got0_ref[i], got1_ref[i])
        back = mine_ref[b].astype(F32) + got.astype(F32)
        out[0] = (cot_ref[b].astype(F32) + back * slope_ref[b]).astype(BF)
        if d != 2:
            out[1] = chosen(b, act_ref, act_peer)
    end[:3] = to_mirror[blocks:]
    end[3:] = mirror[:2]
    beside[2:] = mirror_ref[:blocks]
    mirror[2:] = beside_ref[:blocks]


def pick_kernel(held_ref, out_ref):
    out_ref[...] = held_ref[2:]


def gather_kernel(own, beside, opposite, out_ref):
    for d, piece in enumerate((own[1], beside[1], opposite[3])):
        out_ref[d] = piece


def attention_kernel(
    count, own_qkv, own, beside_qkv, mirror_qkv, opposite_qkv, end, beside, mirror, opposite, *outs
):
    outs, act_ref = outs[:count], outs[count]
    rows, width = own.shape[1:]
    near = beside_qkv.shape[0] - 3
    scale = 1.0 / math.sqrt(HD)
    s = lax.axis_index("seq")
    at_end = jnp.logical_or(s == 0, s == count - 1)

    def positions(j):
        facing = jnp.where(at_end, end[j], mirror_qkv[near + j])
        return jnp.concatenate([own_qkv[j], beside_qkv[near + j], opposite_qkv[j], facing], axis=0)

    query, key, value = (positions(j) for j in range(3))
    facing, act_ref[0] = (jnp.where(at_end, end[3 + j], mirror[j]) for j in range(2))
    grad = jnp.concatenate([own[0], beside[0], opposite[0], facing], axis=0)
    nt = (((1,), (1,)), ((), ()))
    nn = (((1,), (0,)), ((), ()))
    tn = (((0,), (0,)), ((), ()))
    dot = functools.partial(lax.dot_general, preferred_element_type=F32)
    heads = []
    for h in range(width // HD):
        cols = slice(h * HD, (h + 1) * HD)
        heads.append([x[:, cols] for x in (query, key, value, grad)])
    scores = [dot(k, q, nt) * scale for q, k, _, _ in heads]
    d_probs = [dot(v, g, nt) for _, _, v, g in heads]
    raised = [jnp.exp(x - jnp.max(x, axis=0, keepdims=True)) for x in scores]
    probs = [x * (1.0 / jnp.sum(x, axis=0, keepdims=True)) for x in raised]
    v_grads = [dot(p.astype(BF), g, nn).astype(BF) for p, (_, _, _, g) in zip(probs, heads)]
    totals = [jnp.sum(p * d, axis=0, keepdims=True) for p, d in zip(probs, d_probs)]
    d_scores = [(p * (d - t)).astype(BF) for p, d, t in zip(probs, d_probs, totals)]
    k_grads = [(dot(d, q, nn) * scale).astype(BF) for d, (q, _, _, _) in zip(d_scores, heads)]
    q_grads = [(dot(d, k, tn) * scale).astype(BF) for d, (_, k, _, _) in zip(d_scores, heads)]
    results = q_grads, k_grads, v_grads
    for j in range(3):
        whole = jnp.concatenate(results[j], axis=1)
        for d in range(count):
            outs[d][j] = whole[d * rows : (d + 1) * rows]


def weight_kernel(
    count, factor, cot_ref, beside, mirror, beside2, mirror2, farthest, act_ref, act_peer,
    act_last, peer_last, own, to_beside, to_opposite, to_mirror, own_ref, sent0_ref, sent1_ref, grad_ref, act_buf, cot_buf,
):
    s = lax.axis_index("seq")
    c = lax.axis_index("chan")
    b = lax.axis_index("batch")
    blocks, rows, width = grad_ref.shape
    for d, piece in enumerate((own, to_beside, to_opposite, to_mirror)):
        grad_ref[s ^ d] = piece[0]
    lanes = act_buf.shape[2] // 2
    for d in range(count):
        held, came = (act_ref[d], act_peer[d]) if d < 3 else (act_last[0], peer_last[0])
        halves = jnp.where(c == 0, held, came), jnp.where(c == 0, came, held)
        for r in range(width // lanes):
            for h in range(2):
                act_buf[s ^ d, pl.ds(r * rows, rows), pl.ds(h * lanes, lanes)] = halves[h][
                    :, r * lanes : (r + 1) * lanes
                ]
    flat = cot_buf.shape[1:]
    at_end = jnp.logical_or(s == 0, s == count - 1)
    cot_buf[s] = cot_ref[:blocks].reshape(flat)
    cot_buf[s ^ 1] = beside[:blocks].reshape(flat)
    cot_buf[s ^ 3] = jnp.where(at_end, farthest[...], mirror[:blocks]).reshape(flat)
    cot_buf[s ^ 2] = jnp.where(at_end, beside2[2:], mirror2[2:]).reshape(flat)

    half = own_ref.shape[1]
    for t in range(3):
        low = max(0, 1 - t)
        high = min(count, count + 1 - t)
        for is_own, side in ((False, 1 - b), (True, b)):
            start = pl.multiple_of(side * half, half)
            total = None
            for j in range(low, high):
                term = jnp.dot(
                    act_buf[j + t - 1, pl.ds(start, half), :],
                    cot_buf[j],
                    preferred_element_type=F32,
                )
                total = term if total is None else total + term
            total = factor * total
            if is_own:
                own_ref[t] = total
            else:
                sent0_ref[t] = total[: half // 2].astype(BF)
                sent1_ref[t] = total[half // 2 :].astype(BF)


def add_kernel(own_ref, got0_ref, got1_ref, out_ref):
    half = got0_ref.shape[1]
    out_ref[:, :half] = own_ref[:, :half] + got0_ref[...].astype(F32)
    out_ref[:, half:] = own_ref[:, half:] + got1_ref[...].astype(F32)


def place_kernel(*refs):
    pieces, outs, sems = refs[:-4], refs[-4:-1], refs[-1]
    s = lax.axis_index("seq")
    pairs = [(piece.at[j], outs[j].at[s ^ d]) for d, piece in zip((0, 2, 1, 3), pieces) for j in range(3)]
    for copy in fetch(pairs, sems):
        copy.wait()


def swap(x, axis, by, only=None):
    n = lax.axis_size(axis)
    return lax.ppermute(x, axis, [(i, i ^ by) for i in range(n) if only is None or i in only])


def after(first, *then):
    held = lax.optimization_barrier((first, *then))
    return held[1:]


def per_device(query_vectors, key_vectors, value_vectors, hidden, cotangent, conv_weight):
    count = lax.axis_size("seq")
    blocks, rows, width = hidden.shape
    tokens = blocks * rows
    factor = 1.0 / math.sqrt(tokens * count * lax.axis_size("batch"))
    weights = conv_weight.transpose(1, 0, 2)
    part = width // 2
    middle, ends = (1, 2), (0, 3)

    def units(n):
        return shape((n, rows, width))

    to_beside, to_mirror = kernel_call(
        near_kernel,
        [units(blocks + 3)] * 2,
        name="near",
        scratch=[pltpu.SemaphoreType.DMA((8,))],
        space=pltpu.HBM,
    )(cotangent, query_vectors, key_vectors, value_vectors)
    beside = swap(to_beside, "seq", 1)
    mirror = swap(to_mirror, "seq", 3, middle)
    (hidden,) = after(to_beside, hidden)
    own_qkv, opposite_qkv, weights, slope, act, act_sent = kernel_call(
        rest_kernel,
        [units(3)] * 2 + [shape(weights.shape), shape(hidden.shape, F32), units(2), units(2)],
        name="rest",
        scratch=[pltpu.VMEM(hidden.shape, BF), pltpu.SemaphoreType.DMA((8,))],
        space=pltpu.HBM,
    )(hidden, query_vectors, key_vectors, value_vectors, weights)
    act_got = swap(act_sent, "chan", 1)
    flat = shape((tokens, width), F32)
    centre_mine, centre_other, to_opposite = kernel_call(
        centre_kernel, [flat, flat, units(4)], name="conv_centre"
    )(to_beside, weights, opposite_qkv, act, act_got)
    opposite = swap(to_opposite, "seq", 2)
    others = kernel_call(
        functools.partial(conv_kernel, False), [units(blocks // 2)] * 2, name="conv_other"
    )(beside, mirror, weights, centre_other)
    got = [swap(x, "chan", 1) for x in others]
    (centre_mine,) = after(others[0], centre_mine)
    (mine,) = kernel_call(functools.partial(conv_kernel, True), [units(blocks)], name="conv_mine")(
        beside, mirror, weights, centre_mine
    )
    own, to_beside2, to_opposite2, to_mirror2, to_end2 = kernel_call(
        grad_kernel,
        [units(2), units(blocks + 2), units(1), units(blocks + 2), units(5)],
        name="hidden_grad",
    )(to_beside, slope, mine, *got, act, act_got, beside, mirror, to_mirror)
    beside2 = swap(to_beside2, "seq", 1)
    mirror2 = swap(to_mirror2, "seq", 3, middle)
    far_opposite, far_end = after(opposite, to_opposite2, to_end2)
    opposite2 = swap(far_opposite, "seq", 2)
    end2 = swap(far_end, "seq", 3, ends)
    (far,) = kernel_call(pick_kernel, [units(blocks)], name="pick")(mirror2)
    farthest = lax.ppermute(far, "seq", [(1, 0), (2, 3)])

    (act_held,) = kernel_call(gather_kernel, [units(3)], name="gather")(own, beside2, opposite)
    act_peer = swap(act_held, "chan", 1)
    (own_qkv,) = after(act_held, own_qkv)

    item = 5 * (count * rows) ** 2 * width
    *returned, act_last = kernel_call(
        functools.partial(attention_kernel, count),
        [units(3)] * count + [units(1)],
        flops=COST * 2 * item,
        transcendentals=(count * rows) ** 2 * (width // HD),
        name="attention",
    )(own_qkv, own, beside, mirror, opposite, end2, beside2, mirror2, opposite2)
    back = {d: swap(returned[d], "seq", d) for d in (2, 1, 3)}

    peer_last = swap(act_last, "chan", 1)
    total, sent0, sent1, hidden_grad = kernel_call(
        functools.partial(weight_kernel, count, factor),
        [shape((3, part // 2, width), F32)] + [shape((3, part // 4, width))] * 2 + [units(blocks)],
        name="weight_grad",
        bytes_too=False,
        scratch=[
            pltpu.VMEM((count, part, tokens), BF),
            pltpu.VMEM((count, tokens, width), BF),
        ],
    )(
        to_beside, beside, mirror, beside2, mirror2, farthest, act_held, act_peer, act_last,
        peer_last, own, to_beside2, to_opposite2, to_mirror2,
    )
    got_sums = [swap(x, "batch", 1) for x in (sent0, sent1)]
    (weight_grad,) = kernel_call(add_kernel, [shape((3, part // 2, width), F32)], name="add_weight", bytes_too=False)(
        total, *got_sums
    )
    pieces = [returned[0], *back.values()]
    (pieces[0],) = after(weight_grad, pieces[0])
    query_grad, key_grad, value_grad = kernel_call(
        place_kernel,
        [units(blocks)] * 3,
        name="place",
        scratch=[pltpu.SemaphoreType.DMA((3 * count,))],
        out_space=pltpu.HBM,
    )(*pieces)
    return (query_grad, key_grad, value_grad, hidden_grad, weight_grad.transpose(1, 0, 2))


def from_behind(shard, axis, by):
    length = lax.axis_size(axis)
    pairs = [(i, i + by) for i in range(length) if 0 <= i + by < length]
    return lax.ppermute(shard, axis, pairs)


def per_device_general(query_vectors, key_vectors, value_vectors, hidden, cotangent, conv_weight):
    seq_count = lax.axis_size("seq")
    batch_count = lax.axis_size("batch")
    partner_gap = seq_count // 4
    blocks, row_count, local_width = hidden.shape
    tokens_all = blocks * batch_count * row_count * seq_count
    factor = 1.0 / math.sqrt(tokens_all)
    hidden_f = hidden.astype(jnp.float32)
    activation = tanh_gelu(hidden_f).astype(jnp.bfloat16)
    act_full = lax.all_gather(activation, "chan", axis=2, tiled=True)

    def partner(offset):
        return from_behind(cotangent, "seq", offset)

    cot_before = partner(partner_gap)
    cot_after = partner(-partner_gap)
    cot_taps = jnp.stack([cot_after, cotangent, cot_before])
    back_part = jnp.einsum(
        "tbqo,ito->bqi", cot_taps, conv_weight, preferred_element_type=jnp.float32
    )
    back_sum = lax.psum_scatter(
        back_part.astype(jnp.bfloat16), "chan", scatter_dimension=2, tiled=True
    ).astype(jnp.float32)
    hidden_grad = (cotangent.astype(jnp.float32) + back_sum * gelu_slope(hidden_f)).astype(
        jnp.bfloat16
    )
    weight_grad = lax.psum_scatter(
        factor
        * jnp.einsum("bpi,tbpo->ito", act_full, cot_taps, preferred_element_type=jnp.float32),
        ("seq", "batch"),
        scatter_dimension=0,
        tiled=True,
    )
    heads_local = local_width // HD

    def to_heads(signal):
        return signal.reshape(blocks, row_count, heads_local, HD)

    stacked = jnp.stack(
        [
            to_heads(query_vectors),
            to_heads(key_vectors),
            to_heads(value_vectors),
            to_heads(hidden_grad),
        ],
        axis=3,
    )
    stacked = stacked.transpose(0, 2, 1, 3, 4).reshape(
        seq_count, blocks * heads_local // seq_count, row_count, 4 * HD
    )
    gathered = lax.all_to_all(stacked, "seq", split_axis=0, concat_axis=2, tiled=True)
    item_count = gathered.shape[1]
    length = gathered.shape[2]
    columns = gathered[0].reshape(item_count, length, 4, HD)
    query_all = columns[:, :, 0]
    key_all = columns[:, :, 1]
    value_all = columns[:, :, 2]
    grad_all = columns[:, :, 3]
    score_scale = 1.0 / math.sqrt(HD)
    block_rows = math.gcd(length, 512)
    block_count = length // block_rows
    query_blocks = query_all.reshape(item_count, block_count, block_rows, HD).transpose(1, 0, 2, 3)
    grad_blocks = grad_all.reshape(item_count, block_count, block_rows, HD).transpose(1, 0, 2, 3)

    def query_block(carry, inputs):
        key_acc, value_acc = carry
        query_rows, grad_rows = inputs
        scores = (
            jnp.einsum("iqd,ikd->iqk", query_rows, key_all, preferred_element_type=jnp.float32)
            * score_scale
        )
        row_max = jnp.max(scores, axis=-1, keepdims=True)
        raised = jnp.exp(scores - row_max)
        probability = raised / jnp.sum(raised, axis=-1, keepdims=True)
        prob_b = probability.astype(jnp.bfloat16)
        value_acc = value_acc + jnp.einsum(
            "iqk,iqd->ikd", prob_b, grad_rows, preferred_element_type=jnp.float32
        )
        d_prob = jnp.einsum(
            "iqd,ikd->iqk", grad_rows, value_all, preferred_element_type=jnp.float32
        )
        row_total = jnp.sum(probability * d_prob, axis=-1, keepdims=True)
        d_score = (probability * (d_prob - row_total)).astype(jnp.bfloat16)
        query_out = (
            score_scale
            * jnp.einsum("iqk,ikd->iqd", d_score, key_all, preferred_element_type=jnp.float32)
        ).astype(jnp.bfloat16)
        key_acc = key_acc + jnp.einsum(
            "iqk,iqd->ikd", d_score, query_rows, preferred_element_type=jnp.float32
        )
        return ((key_acc, value_acc), query_out)

    empty_acc = jnp.zeros((item_count, length, HD), jnp.float32)
    (key_acc, value_acc), query_outs = lax.scan(
        query_block, (empty_acc, empty_acc), (query_blocks, grad_blocks)
    )
    query_out = query_outs.transpose(1, 0, 2, 3).reshape(item_count, length, HD)
    key_out = (score_scale * key_acc).astype(jnp.bfloat16)
    value_out = value_acc.astype(jnp.bfloat16)
    results = jnp.concatenate([query_out, key_out, value_out], axis=-1)[None]
    returned = lax.all_to_all(results, "seq", split_axis=2, concat_axis=0, tiled=True)
    returned = returned.reshape(blocks, heads_local, row_count, 3, HD).transpose(3, 0, 2, 1, 4)
    returned = returned.reshape(3, blocks, row_count, local_width)
    return (returned[0], returned[1], returned[2], hidden_grad, weight_grad)


def solution(mesh):
    token = P(("groups", "batch"), "seq", "chan")
    sizes = dict(mesh.shape)

    def run(*arrays):
        blocks = arrays[0].shape[0] // (sizes["groups"] * sizes["batch"])
        fits = blocks == sizes["seq"] == 4 and sizes["batch"] == 2 and sizes["chan"] == 2
        return jax.shard_map(
            per_device if fits else per_device_general,
            mesh=mesh,
            in_specs=(token,) * 5 + (P(None, None, "chan"),),
            out_specs=(token,) * 4 + (P(("groups", "seq", "batch"), None, "chan"),),
            check_vma=False,
        )(*arrays)

    return run
```

```python
import functools
import math

import jax
import jax.numpy as jnp
from jax import lax
from jax.experimental import pallas as pl
from jax.experimental.pallas import tpu as pltpu
from jax.sharding import PartitionSpec as P

HD = 96
BF = jnp.bfloat16
F32 = jnp.float32
COST = 8
VMEM_LIMIT = 40 * 1024 * 1024


def tanh_gelu(signal):
    inner_arg = 0.7978845608 * (signal + 0.044715 * signal * signal * signal)
    return 0.5 * signal * (1.0 + jnp.tanh(inner_arg))


def gelu_slope(signal):
    inner_arg = 0.7978845608 * (signal + 0.044715 * signal * signal * signal)
    hyper = jnp.tanh(inner_arg)
    return 0.5 * (1.0 + hyper) + 0.5 * signal * (1.0 - hyper * hyper) * 0.7978845608 * (
        1.0 + 3.0 * 0.044715 * signal * signal
    )


def kernel_call(
    body, outs, flops=0, transcendentals=0, name=None, scratch=(), space=pltpu.VMEM,
    out_space=pltpu.VMEM, bytes_too=True,
):
    given, made = (pl.BlockSpec(memory_space=x) for x in (space, out_space))

    def call(*args):
        if space == pltpu.HBM:
            args = [pltpu.with_memory_space_constraint(a, pltpu.HBM) for a in args]
        moved = sum(math.prod(a.shape) * a.dtype.itemsize for a in args)
        moved += sum(math.prod(o.shape) * o.dtype.itemsize for o in outs)
        return pl.pallas_call(
            body,
            out_shape=list(outs),
            in_specs=[given] * len(args),
            out_specs=[made] * len(outs),
            scratch_shapes=list(scratch),
            compiler_params=pltpu.CompilerParams(vmem_limit_bytes=VMEM_LIMIT),
            cost_estimate=pl.CostEstimate(
                flops=flops, bytes_accessed=moved * bytes_too, transcendentals=transcendentals
            ),
            name=name,
        )(*args)

    return call


def shape(dims, dtype=BF):
    return jax.ShapeDtypeStruct(dims, dtype)


def fetch(pairs, sems):
    copies = [pltpu.make_async_copy(src, dst, sems.at[i]) for i, (src, dst) in enumerate(pairs)]
    for copy in copies:
        copy.start()
    return copies


def near_kernel(cot, q, k, v, beside, mirror, sems):
    s = lax.axis_index("seq")
    blocks = cot.shape[0]
    pairs = []
    for out, d in ((beside, 1), (mirror, 3)):
        pairs.append((cot, out.at[pl.ds(0, blocks)]))
        pairs += [(x.at[s ^ d], out.at[blocks + j]) for j, x in enumerate((q, k, v))]
    for copy in fetch(pairs, sems):
        copy.wait()


def rest_kernel(hidden, q, k, v, w, own, opposite, w_ref, slope_ref, act_ref, sent_ref, h_ref, sems):
    s = lax.axis_index("seq")
    c = lax.axis_index("chan")
    pairs = [(hidden, h_ref)]
    for out, b in ((opposite, s ^ 2), (own, s)):
        pairs += [(x.at[b], out.at[j]) for j, x in enumerate((q, k, v))]
    pairs.append((w, w_ref))
    copies = fetch(pairs, sems)
    copies[0].wait()
    blocks, rows, width = h_ref.shape
    signal = h_ref[...].astype(F32)
    slope_ref[...] = gelu_slope(signal)
    act_t = tanh_gelu(signal).reshape(blocks * rows, width).T.astype(BF)
    lanes = act_t.shape[1] // 2
    parts = width // lanes
    halves = act_t[:, :lanes], act_t[:, lanes:]
    first = c == 0
    kept, sent = jnp.where(first, *halves), jnp.where(first, halves[1], halves[0])
    for out, half in ((act_ref, kept), (sent_ref, sent)):
        for i in range(2 * parts):
            out[i // parts, :, pl.ds(i % parts * lanes, lanes)] = half[i * rows : (i + 1) * rows]
    for copy in copies[1:]:
        copy.wait()


def conv_term(tap, w_ref, t, side):
    width = w_ref.shape[2]
    start = pl.multiple_of(side * width, width)
    return lax.dot_general(
        tap,
        w_ref[t, pl.ds(start, width), :],
        (((1,), (1,)), ((), ())),
        preferred_element_type=F32,
    )


def chosen(block, act_ref, act_peer):
    k = lax.rem(block, 2)
    return jnp.where(lax.div(block, 2) == lax.axis_index("chan"), act_ref[k], act_peer[k])


def centre_kernel(cot_ref, w_ref, qkv, act_ref, act_peer, mine_ref, other_ref, opposite):
    c = lax.axis_index("chan")
    blocks = cot_ref.shape[0] - 3
    opposite[:3] = qkv[...]
    opposite[3] = chosen(lax.axis_index("seq") ^ 2, act_ref, act_peer)
    tap = cot_ref[:blocks].reshape(mine_ref.shape)
    mine_ref[...] = conv_term(tap, w_ref, 1, c)
    other_ref[...] = conv_term(tap, w_ref, 1, 1 - c)


def conv_kernel(mine, beside_ref, mirror_ref, w_ref, centre_ref, *outs):
    c = lax.axis_index("chan")
    even = lax.rem(lax.axis_index("seq"), 2) == 0
    blocks = beside_ref.shape[0] - 3
    beside = beside_ref[:blocks].reshape(centre_ref.shape)
    mirror = mirror_ref[:blocks].reshape(centre_ref.shape)
    side = c if mine else 1 - c
    total = (
        centre_ref[...]
        + conv_term(jnp.where(even, beside, mirror), w_ref, 0, side)
        + conv_term(jnp.where(even, mirror, beside), w_ref, 2, side)
    ).astype(BF)
    rows = total.shape[0] // len(outs)
    for i, out in enumerate(outs):
        out[...] = total[i * rows : (i + 1) * rows].reshape(out.shape)


def grad_kernel(
    cot_ref, slope_ref, mine_ref, got0_ref, got1_ref, act_ref, act_peer, beside_ref, mirror_ref,
    to_mirror, own, beside, opposite, mirror, end,
):
    s = lax.axis_index("seq")
    blocks = mine_ref.shape[0]
    for d, out in ((1, beside), (3, mirror), (2, opposite), (0, own)):
        b = s ^ d
        i = lax.rem(b, 2)
        got = jnp.where(b < 2, got0_ref[i], got1_ref[i])
        back = mine_ref[b].astype(F32) + got.astype(F32)
        out[0] = (cot_ref[b].astype(F32) + back * slope_ref[b]).astype(BF)
        if d != 2:
            out[1] = chosen(b, act_ref, act_peer)
    end[:3] = to_mirror[blocks:]
    end[3:] = mirror[:2]
    beside[2:] = mirror_ref[:blocks]
    mirror[2:] = beside_ref[:blocks]


def pick_kernel(held_ref, out_ref):
    out_ref[...] = held_ref[2:]


def gather_kernel(own, beside, opposite, out_ref):
    for d, piece in enumerate((own[1], beside[1], opposite[3])):
        out_ref[d] = piece


def attention_kernel(
    count, own_qkv, own, beside_qkv, mirror_qkv, opposite_qkv, end, beside, mirror, opposite, *outs
):
    outs, act_ref = outs[:count], outs[count]
    rows, width = own.shape[1:]
    near = beside_qkv.shape[0] - 3
    scale = 1.0 / math.sqrt(HD)
    s = lax.axis_index("seq")
    at_end = jnp.logical_or(s == 0, s == count - 1)

    def positions(j):
        facing = jnp.where(at_end, end[j], mirror_qkv[near + j])
        return jnp.concatenate([own_qkv[j], beside_qkv[near + j], opposite_qkv[j], facing], axis=0)

    query, key, value = (positions(j) for j in range(3))
    facing, act_ref[0] = (jnp.where(at_end, end[3 + j], mirror[j]) for j in range(2))
    grad = jnp.concatenate([own[0], beside[0], opposite[0], facing], axis=0)
    nt = (((1,), (1,)), ((), ()))
    nn = (((1,), (0,)), ((), ()))
    tn = (((0,), (0,)), ((), ()))
    dot = functools.partial(lax.dot_general, preferred_element_type=F32)
    tile = 128
    lane = lax.broadcasted_iota(jnp.int32, (1, width), 1)
    windows, heads = [], []
    for h in range(width // HD):
        low, high = h * HD // tile * tile, -(-(h + 1) * HD // tile) * tile
        inside = jnp.logical_and(lane >= h * HD, lane < (h + 1) * HD).astype(F32).astype(BF)[:, low:high]
        windows.append((low, high))
        q, k, v, g = (x[:, low:high] for x in (query, key, value, grad))
        heads.append((q, k, k * inside, v * inside, g))
    scores = [dot(k, q, nt) * scale for q, _, k, _, _ in heads]
    d_probs = [dot(v, g, nt) for _, _, _, v, g in heads]
    raised = [jnp.exp(x - jnp.max(x, axis=0, keepdims=True)) for x in scores]
    probs = [x * (1.0 / jnp.sum(x, axis=0, keepdims=True)) for x in raised]
    v_grads = [dot(p.astype(BF), x[4], nn) for p, x in zip(probs, heads)]
    totals = [jnp.sum(p * d, axis=0, keepdims=True) for p, d in zip(probs, d_probs)]
    d_scores = [(p * (d - t)).astype(BF) for p, d, t in zip(probs, d_probs, totals)]
    k_grads = [dot(d, x[0], nn) * scale for d, x in zip(d_scores, heads)]
    q_grads = [dot(d, x[1], tn) * scale for d, x in zip(d_scores, heads)]
    for j, results in enumerate((q_grads, k_grads, v_grads)):
        for at in range(0, width, tile):
            whole = None
            for h, ((low, high), x) in enumerate(zip(windows, results)):
                if low <= at < high:
                    part = x[:, at - low : at - low + tile]
                    whole = part if whole is None else jnp.where(lane[:, at : at + tile] < h * HD, whole, part)
            whole = whole.astype(BF)
            for d in range(count):
                outs[d][j, :, at : at + tile] = whole[d * rows : (d + 1) * rows]


def weight_kernel(
    count, factor, cot_ref, beside, mirror, beside2, mirror2, farthest, act_ref, act_peer,
    act_last, peer_last, own, to_beside, to_opposite, to_mirror, own_ref, sent0_ref, sent1_ref, grad_ref, act_buf, cot_buf,
):
    s = lax.axis_index("seq")
    c = lax.axis_index("chan")
    b = lax.axis_index("batch")
    blocks, rows, width = grad_ref.shape
    for d, piece in enumerate((own, to_beside, to_opposite, to_mirror)):
        grad_ref[s ^ d] = piece[0]
    lanes = act_buf.shape[2] // 2
    for d in range(count):
        held, came = (act_ref[d], act_peer[d]) if d < 3 else (act_last[0], peer_last[0])
        halves = jnp.where(c == 0, held, came), jnp.where(c == 0, came, held)
        for r in range(width // lanes):
            for h in range(2):
                act_buf[s ^ d, pl.ds(r * rows, rows), pl.ds(h * lanes, lanes)] = halves[h][
                    :, r * lanes : (r + 1) * lanes
                ]
    flat = cot_buf.shape[1:]
    at_end = jnp.logical_or(s == 0, s == count - 1)
    cot_buf[s] = cot_ref[:blocks].reshape(flat)
    cot_buf[s ^ 1] = beside[:blocks].reshape(flat)
    cot_buf[s ^ 3] = jnp.where(at_end, farthest[...], mirror[:blocks]).reshape(flat)
    cot_buf[s ^ 2] = jnp.where(at_end, beside2[2:], mirror2[2:]).reshape(flat)

    half = own_ref.shape[1]
    for t in range(3):
        low = max(0, 1 - t)
        high = min(count, count + 1 - t)
        for is_own, side in ((False, 1 - b), (True, b)):
            start = pl.multiple_of(side * half, half)
            total = None
            for j in range(low, high):
                term = jnp.dot(
                    act_buf[j + t - 1, pl.ds(start, half), :],
                    cot_buf[j],
                    preferred_element_type=F32,
                )
                total = term if total is None else total + term
            total = factor * total
            if is_own:
                own_ref[t] = total
            else:
                sent0_ref[t] = total[: half // 2].astype(BF)
                sent1_ref[t] = total[half // 2 :].astype(BF)


def add_kernel(own_ref, got0_ref, got1_ref, out_ref):
    half = got0_ref.shape[1]
    out_ref[:, :half] = own_ref[:, :half] + got0_ref[...].astype(F32)
    out_ref[:, half:] = own_ref[:, half:] + got1_ref[...].astype(F32)


def place_kernel(*refs):
    pieces, outs, sems = refs[:-4], refs[-4:-1], refs[-1]
    s = lax.axis_index("seq")
    pairs = [(piece.at[j], outs[j].at[s ^ d]) for d, piece in zip((0, 2, 1, 3), pieces) for j in range(3)]
    for copy in fetch(pairs, sems):
        copy.wait()


def swap(x, axis, by, only=None):
    n = lax.axis_size(axis)
    return lax.ppermute(x, axis, [(i, i ^ by) for i in range(n) if only is None or i in only])


def after(first, *then):
    held = lax.optimization_barrier((first, *then))
    return held[1:]


def per_device(query_vectors, key_vectors, value_vectors, hidden, cotangent, conv_weight):
    count = lax.axis_size("seq")
    blocks, rows, width = hidden.shape
    tokens = blocks * rows
    factor = 1.0 / math.sqrt(tokens * count * lax.axis_size("batch"))
    weights = conv_weight.transpose(1, 0, 2)
    part = width // 2
    middle, ends = (1, 2), (0, 3)

    def units(n):
        return shape((n, rows, width))

    to_beside, to_mirror = kernel_call(
        near_kernel,
        [units(blocks + 3)] * 2,
        name="near",
        scratch=[pltpu.SemaphoreType.DMA((8,))],
        space=pltpu.HBM,
    )(cotangent, query_vectors, key_vectors, value_vectors)
    beside = swap(to_beside, "seq", 1)
    mirror = swap(to_mirror, "seq", 3, middle)
    (hidden,) = after(to_beside, hidden)
    own_qkv, opposite_qkv, weights, slope, act, act_sent = kernel_call(
        rest_kernel,
        [units(3)] * 2 + [shape(weights.shape), shape(hidden.shape, F32), units(2), units(2)],
        name="rest",
        scratch=[pltpu.VMEM(hidden.shape, BF), pltpu.SemaphoreType.DMA((8,))],
        space=pltpu.HBM,
    )(hidden, query_vectors, key_vectors, value_vectors, weights)
    act_got = swap(act_sent, "chan", 1)
    flat = shape((tokens, width), F32)
    centre_mine, centre_other, to_opposite = kernel_call(
        centre_kernel, [flat, flat, units(4)], name="conv_centre"
    )(to_beside, weights, opposite_qkv, act, act_got)
    opposite = swap(to_opposite, "seq", 2)
    others = kernel_call(
        functools.partial(conv_kernel, False), [units(blocks // 2)] * 2, name="conv_other"
    )(beside, mirror, weights, centre_other)
    got = [swap(x, "chan", 1) for x in others]
    (centre_mine,) = after(others[0], centre_mine)
    (mine,) = kernel_call(functools.partial(conv_kernel, True), [units(blocks)], name="conv_mine")(
        beside, mirror, weights, centre_mine
    )
    own, to_beside2, to_opposite2, to_mirror2, to_end2 = kernel_call(
        grad_kernel,
        [units(2), units(blocks + 2), units(1), units(blocks + 2), units(5)],
        name="hidden_grad",
    )(to_beside, slope, mine, *got, act, act_got, beside, mirror, to_mirror)
    beside2 = swap(to_beside2, "seq", 1)
    mirror2 = swap(to_mirror2, "seq", 3, middle)
    far_opposite, far_end = after(opposite, to_opposite2, to_end2)
    opposite2 = swap(far_opposite, "seq", 2)
    end2 = swap(far_end, "seq", 3, ends)
    (far,) = kernel_call(pick_kernel, [units(blocks)], name="pick")(mirror2)
    farthest = lax.ppermute(far, "seq", [(1, 0), (2, 3)])

    (act_held,) = kernel_call(gather_kernel, [units(3)], name="gather")(own, beside2, opposite)
    act_peer = swap(act_held, "chan", 1)
    (own_qkv,) = after(act_held, own_qkv)

    item = 5 * (count * rows) ** 2 * width
    *returned, act_last = kernel_call(
        functools.partial(attention_kernel, count),
        [units(3)] * count + [units(1)],
        flops=COST * 2 * item,
        transcendentals=(count * rows) ** 2 * (width // HD),
        name="attention",
    )(own_qkv, own, beside, mirror, opposite, end2, beside2, mirror2, opposite2)
    back = {d: swap(returned[d], "seq", d) for d in (2, 1, 3)}

    peer_last = swap(act_last, "chan", 1)
    total, sent0, sent1, hidden_grad = kernel_call(
        functools.partial(weight_kernel, count, factor),
        [shape((3, part // 2, width), F32)] + [shape((3, part // 4, width))] * 2 + [units(blocks)],
        name="weight_grad",
        bytes_too=False,
        scratch=[
            pltpu.VMEM((count, part, tokens), BF),
            pltpu.VMEM((count, tokens, width), BF),
        ],
    )(
        to_beside, beside, mirror, beside2, mirror2, farthest, act_held, act_peer, act_last,
        peer_last, own, to_beside2, to_opposite2, to_mirror2,
    )
    got_sums = [swap(x, "batch", 1) for x in (sent0, sent1)]
    (weight_grad,) = kernel_call(add_kernel, [shape((3, part // 2, width), F32)], name="add_weight", bytes_too=False)(
        total, *got_sums
    )
    pieces = [returned[0], *back.values()]
    (pieces[0],) = after(weight_grad, pieces[0])
    query_grad, key_grad, value_grad = kernel_call(
        place_kernel,
        [units(blocks)] * 3,
        name="place",
        scratch=[pltpu.SemaphoreType.DMA((3 * count,))],
        out_space=pltpu.HBM,
    )(*pieces)
    return (query_grad, key_grad, value_grad, hidden_grad, weight_grad.transpose(1, 0, 2))


def from_behind(shard, axis, by):
    length = lax.axis_size(axis)
    pairs = [(i, i + by) for i in range(length) if 0 <= i + by < length]
    return lax.ppermute(shard, axis, pairs)


def per_device_general(query_vectors, key_vectors, value_vectors, hidden, cotangent, conv_weight):
    seq_count = lax.axis_size("seq")
    batch_count = lax.axis_size("batch")
    partner_gap = seq_count // 4
    blocks, row_count, local_width = hidden.shape
    tokens_all = blocks * batch_count * row_count * seq_count
    factor = 1.0 / math.sqrt(tokens_all)
    hidden_f = hidden.astype(jnp.float32)
    activation = tanh_gelu(hidden_f).astype(jnp.bfloat16)
    act_full = lax.all_gather(activation, "chan", axis=2, tiled=True)

    def partner(offset):
        return from_behind(cotangent, "seq", offset)

    cot_before = partner(partner_gap)
    cot_after = partner(-partner_gap)
    cot_taps = jnp.stack([cot_after, cotangent, cot_before])
    back_part = jnp.einsum(
        "tbqo,ito->bqi", cot_taps, conv_weight, preferred_element_type=jnp.float32
    )
    back_sum = lax.psum_scatter(
        back_part.astype(jnp.bfloat16), "chan", scatter_dimension=2, tiled=True
    ).astype(jnp.float32)
    hidden_grad = (cotangent.astype(jnp.float32) + back_sum * gelu_slope(hidden_f)).astype(
        jnp.bfloat16
    )
    weight_grad = lax.psum_scatter(
        factor
        * jnp.einsum("bpi,tbpo->ito", act_full, cot_taps, preferred_element_type=jnp.float32),
        ("seq", "batch"),
        scatter_dimension=0,
        tiled=True,
    )
    heads_local = local_width // HD

    def to_heads(signal):
        return signal.reshape(blocks, row_count, heads_local, HD)

    stacked = jnp.stack(
        [
            to_heads(query_vectors),
            to_heads(key_vectors),
            to_heads(value_vectors),
            to_heads(hidden_grad),
        ],
        axis=3,
    )
    stacked = stacked.transpose(0, 2, 1, 3, 4).reshape(
        seq_count, blocks * heads_local // seq_count, row_count, 4 * HD
    )
    gathered = lax.all_to_all(stacked, "seq", split_axis=0, concat_axis=2, tiled=True)
    item_count = gathered.shape[1]
    length = gathered.shape[2]
    columns = gathered[0].reshape(item_count, length, 4, HD)
    query_all = columns[:, :, 0]
    key_all = columns[:, :, 1]
    value_all = columns[:, :, 2]
    grad_all = columns[:, :, 3]
    score_scale = 1.0 / math.sqrt(HD)
    block_rows = math.gcd(length, 512)
    block_count = length // block_rows
    query_blocks = query_all.reshape(item_count, block_count, block_rows, HD).transpose(1, 0, 2, 3)
    grad_blocks = grad_all.reshape(item_count, block_count, block_rows, HD).transpose(1, 0, 2, 3)

    def query_block(carry, inputs):
        key_acc, value_acc = carry
        query_rows, grad_rows = inputs
        scores = (
            jnp.einsum("iqd,ikd->iqk", query_rows, key_all, preferred_element_type=jnp.float32)
            * score_scale
        )
        row_max = jnp.max(scores, axis=-1, keepdims=True)
        raised = jnp.exp(scores - row_max)
        probability = raised / jnp.sum(raised, axis=-1, keepdims=True)
        prob_b = probability.astype(jnp.bfloat16)
        value_acc = value_acc + jnp.einsum(
            "iqk,iqd->ikd", prob_b, grad_rows, preferred_element_type=jnp.float32
        )
        d_prob = jnp.einsum(
            "iqd,ikd->iqk", grad_rows, value_all, preferred_element_type=jnp.float32
        )
        row_total = jnp.sum(probability * d_prob, axis=-1, keepdims=True)
        d_score = (probability * (d_prob - row_total)).astype(jnp.bfloat16)
        query_out = (
            score_scale
            * jnp.einsum("iqk,ikd->iqd", d_score, key_all, preferred_element_type=jnp.float32)
        ).astype(jnp.bfloat16)
        key_acc = key_acc + jnp.einsum(
            "iqk,iqd->ikd", d_score, query_rows, preferred_element_type=jnp.float32
        )
        return ((key_acc, value_acc), query_out)

    empty_acc = jnp.zeros((item_count, length, HD), jnp.float32)
    (key_acc, value_acc), query_outs = lax.scan(
        query_block, (empty_acc, empty_acc), (query_blocks, grad_blocks)
    )
    query_out = query_outs.transpose(1, 0, 2, 3).reshape(item_count, length, HD)
    key_out = (score_scale * key_acc).astype(jnp.bfloat16)
    value_out = value_acc.astype(jnp.bfloat16)
    results = jnp.concatenate([query_out, key_out, value_out], axis=-1)[None]
    returned = lax.all_to_all(results, "seq", split_axis=2, concat_axis=0, tiled=True)
    returned = returned.reshape(blocks, heads_local, row_count, 3, HD).transpose(3, 0, 2, 1, 4)
    returned = returned.reshape(3, blocks, row_count, local_width)
    return (returned[0], returned[1], returned[2], hidden_grad, weight_grad)


def solution(mesh):
    token = P(("groups", "batch"), "seq", "chan")
    sizes = dict(mesh.shape)

    def run(*arrays):
        blocks = arrays[0].shape[0] // (sizes["groups"] * sizes["batch"])
        fits = blocks == sizes["seq"] == 4 and sizes["batch"] == 2 and sizes["chan"] == 2
        return jax.shard_map(
            per_device if fits else per_device_general,
            mesh=mesh,
            in_specs=(token,) * 5 + (P(None, None, "chan"),),
            out_specs=(token,) * 4 + (P(("groups", "seq", "batch"), None, "chan"),),
            check_vma=False,
        )(*arrays)

    return run
```

```python
import functools
import math

import jax
import jax.numpy as jnp
from jax import lax
from jax.experimental import pallas as pl
from jax.experimental.pallas import tpu as pltpu
from jax.sharding import PartitionSpec as P

HD = 96
BF = jnp.bfloat16
F32 = jnp.float32
COST = 8
VMEM_LIMIT = 40 * 1024 * 1024


def tanh_gelu(signal):
    inner_arg = 0.7978845608 * (signal + 0.044715 * signal * signal * signal)
    return 0.5 * signal * (1.0 + jnp.tanh(inner_arg))


def gelu_slope(signal):
    inner_arg = 0.7978845608 * (signal + 0.044715 * signal * signal * signal)
    hyper = jnp.tanh(inner_arg)
    return 0.5 * (1.0 + hyper) + 0.5 * signal * (1.0 - hyper * hyper) * 0.7978845608 * (
        1.0 + 3.0 * 0.044715 * signal * signal
    )


def kernel_call(
    body, outs, flops=0, transcendentals=0, name=None, scratch=(), space=pltpu.VMEM,
    out_space=pltpu.VMEM, bytes_too=True, aliases=None,
):
    given, made = (pl.BlockSpec(memory_space=x) for x in (space, out_space))

    def call(*args):
        if space == pltpu.HBM:
            args = [pltpu.with_memory_space_constraint(a, pltpu.HBM) for a in args]
        moved = sum(math.prod(a.shape) * a.dtype.itemsize for a in args)
        moved += sum(math.prod(o.shape) * o.dtype.itemsize for o in outs)
        return pl.pallas_call(
            body,
            out_shape=list(outs),
            in_specs=[given] * len(args),
            out_specs=[made] * len(outs),
            scratch_shapes=list(scratch),
            input_output_aliases=aliases or {},
            compiler_params=pltpu.CompilerParams(vmem_limit_bytes=VMEM_LIMIT),
            cost_estimate=pl.CostEstimate(
                flops=flops, bytes_accessed=moved * bytes_too, transcendentals=transcendentals
            ),
            name=name,
        )(*args)

    return call


def shape(dims, dtype=BF):
    return jax.ShapeDtypeStruct(dims, dtype)


def fetch(pairs, sems):
    copies = [pltpu.make_async_copy(src, dst, sems.at[i]) for i, (src, dst) in enumerate(pairs)]
    for copy in copies:
        copy.start()
    return copies


def near_kernel(cot, q, k, v, beside, mirror, sems):
    s = lax.axis_index("seq")
    blocks = cot.shape[0]
    pairs = []
    for out, d in ((beside, 1), (mirror, 3)):
        pairs.append((cot, out.at[pl.ds(0, blocks)]))
        pairs += [(x.at[s ^ d], out.at[blocks + j]) for j, x in enumerate((q, k, v))]
    for copy in fetch(pairs, sems):
        copy.wait()


def rest_kernel(hidden, q, k, v, w, own, opposite, w_ref, slope_ref, act_ref, sent_ref, h_ref, sems):
    s = lax.axis_index("seq")
    c = lax.axis_index("chan")
    pairs = [(hidden, h_ref)]
    for out, b in ((opposite, s ^ 2), (own, s)):
        pairs += [(x.at[b], out.at[j]) for j, x in enumerate((q, k, v))]
    pairs.append((w, w_ref))
    copies = fetch(pairs, sems)
    copies[0].wait()
    blocks, rows, width = h_ref.shape
    signal = h_ref[...].astype(F32)
    slope_ref[...] = gelu_slope(signal)
    act_t = tanh_gelu(signal).reshape(blocks * rows, width).T.astype(BF)
    lanes = act_t.shape[1] // 2
    parts = width // lanes
    halves = act_t[:, :lanes], act_t[:, lanes:]
    first = c == 0
    kept, sent = jnp.where(first, *halves), jnp.where(first, halves[1], halves[0])
    for out, half in ((act_ref, kept), (sent_ref, sent)):
        for i in range(2 * parts):
            out[i // parts, :, pl.ds(i % parts * lanes, lanes)] = half[i * rows : (i + 1) * rows]
    for copy in copies[1:]:
        copy.wait()


def conv_term(tap, w_ref, t, side):
    width = w_ref.shape[2]
    start = pl.multiple_of(side * width, width)
    return lax.dot_general(
        tap,
        w_ref[t, pl.ds(start, width), :],
        (((1,), (1,)), ((), ())),
        preferred_element_type=F32,
    )


def chosen(block, act_ref, act_peer):
    k = lax.rem(block, 2)
    return jnp.where(lax.div(block, 2) == lax.axis_index("chan"), act_ref[k], act_peer[k])


def centre_kernel(cot_ref, w_ref, qkv, act_ref, act_peer, mine_ref, other_ref, opposite):
    c = lax.axis_index("chan")
    blocks = cot_ref.shape[0] - 3
    opposite[:3] = qkv[...]
    opposite[3] = chosen(lax.axis_index("seq") ^ 2, act_ref, act_peer)
    tap = cot_ref[:blocks].reshape(mine_ref.shape)
    mine_ref[...] = conv_term(tap, w_ref, 1, c)
    other_ref[...] = conv_term(tap, w_ref, 1, 1 - c)


def conv_kernel(mine, beside_ref, mirror_ref, w_ref, centre_ref, *outs):
    c = lax.axis_index("chan")
    even = lax.rem(lax.axis_index("seq"), 2) == 0
    blocks = beside_ref.shape[0] - 3
    beside = beside_ref[:blocks].reshape(centre_ref.shape)
    mirror = mirror_ref[:blocks].reshape(centre_ref.shape)
    side = c if mine else 1 - c
    total = (
        centre_ref[...]
        + conv_term(jnp.where(even, beside, mirror), w_ref, 0, side)
        + conv_term(jnp.where(even, mirror, beside), w_ref, 2, side)
    ).astype(BF)
    rows = total.shape[0] // len(outs)
    for i, out in enumerate(outs):
        out[...] = total[i * rows : (i + 1) * rows].reshape(out.shape)


def grad_kernel(
    cot_ref, slope_ref, mine_ref, got0_ref, got1_ref, act_ref, act_peer, beside_ref, mirror_ref,
    to_mirror, own, beside, opposite, mirror, end,
):
    s = lax.axis_index("seq")
    blocks = mine_ref.shape[0]
    for d, out in ((1, beside), (3, mirror), (2, opposite), (0, own)):
        b = s ^ d
        i = lax.rem(b, 2)
        got = jnp.where(b < 2, got0_ref[i], got1_ref[i])
        back = mine_ref[b].astype(F32) + got.astype(F32)
        out[0] = (cot_ref[b].astype(F32) + back * slope_ref[b]).astype(BF)
        if d != 2:
            out[1] = chosen(b, act_ref, act_peer)
    end[:3] = to_mirror[blocks:]
    end[3:] = mirror[:2]
    beside[2:] = mirror_ref[:blocks]
    mirror[2:] = beside_ref[:blocks]


def pick_kernel(held_ref, out_ref):
    out_ref[...] = held_ref[2:]


def gather_kernel(own, beside, opposite, out_ref):
    for d, piece in enumerate((own[1], beside[1], opposite[3])):
        out_ref[d] = piece


def attention_kernel(
    count, own_qkv, own, beside_qkv, mirror_qkv, opposite_qkv, end, beside, mirror, opposite, *outs
):
    outs, act_ref = outs[:count], outs[count]
    rows, width = own.shape[1:]
    near = beside_qkv.shape[0] - 3
    scale = 1.0 / math.sqrt(HD)
    s = lax.axis_index("seq")
    at_end = jnp.logical_or(s == 0, s == count - 1)

    def positions(j):
        facing = jnp.where(at_end, end[j], mirror_qkv[near + j])
        return jnp.concatenate([own_qkv[j], beside_qkv[near + j], opposite_qkv[j], facing], axis=0)

    query, key, value = (positions(j) for j in range(3))
    facing, act_ref[0] = (jnp.where(at_end, end[3 + j], mirror[j]) for j in range(2))
    grad = jnp.concatenate([own[0], beside[0], opposite[0], facing], axis=0)
    nt = (((1,), (1,)), ((), ()))
    nn = (((1,), (0,)), ((), ()))
    tn = (((0,), (0,)), ((), ()))
    dot = functools.partial(lax.dot_general, preferred_element_type=F32)
    tile = 128
    lane = lax.broadcasted_iota(jnp.int32, (1, width), 1)
    windows, heads = [], []
    for h in range(width // HD):
        low, high = h * HD // tile * tile, -(-(h + 1) * HD // tile) * tile
        inside = jnp.logical_and(lane >= h * HD, lane < (h + 1) * HD).astype(F32).astype(BF)[:, low:high]
        windows.append((low, high))
        q, k, v, g = (x[:, low:high] for x in (query, key, value, grad))
        heads.append((q, k, k * inside, v * inside, g))
    scores = [dot(k, q, nt) * scale for q, _, k, _, _ in heads]
    d_probs = [dot(v, g, nt) for _, _, _, v, g in heads]
    raised = [jnp.exp(x - jnp.max(x, axis=0, keepdims=True)) for x in scores]
    probs = [x * (1.0 / jnp.sum(x, axis=0, keepdims=True)) for x in raised]
    v_grads = [dot(p.astype(BF), x[4], nn) for p, x in zip(probs, heads)]
    totals = [jnp.sum(p * d, axis=0, keepdims=True) for p, d in zip(probs, d_probs)]
    d_scores = [(p * (d - t)).astype(BF) for p, d, t in zip(probs, d_probs, totals)]
    k_grads = [dot(d, x[0], nn) * scale for d, x in zip(d_scores, heads)]
    q_grads = [dot(d, x[1], tn) * scale for d, x in zip(d_scores, heads)]
    for j, results in enumerate((q_grads, k_grads, v_grads)):
        for at in range(0, width, tile):
            whole = None
            for h, ((low, high), x) in enumerate(zip(windows, results)):
                if low <= at < high:
                    part = x[:, at - low : at - low + tile]
                    whole = part if whole is None else jnp.where(lane[:, at : at + tile] < h * HD, whole, part)
            whole = whole.astype(BF)
            for d in range(count):
                outs[d][j, :, at : at + tile] = whole[d * rows : (d + 1) * rows]


def weight_kernel(
    count, factor, cot_ref, beside, mirror, beside2, mirror2, farthest, act_ref, act_peer,
    act_last, peer_last, own, to_beside, to_opposite, to_mirror, own_ref, sent0_ref, sent1_ref, grad_ref, act_buf, cot_buf,
):
    s = lax.axis_index("seq")
    c = lax.axis_index("chan")
    b = lax.axis_index("batch")
    blocks, rows, width = grad_ref.shape
    for d, piece in enumerate((own, to_beside, to_opposite, to_mirror)):
        grad_ref[s ^ d] = piece[0]
    lanes = act_buf.shape[2] // 2
    for d in range(count):
        held, came = (act_ref[d], act_peer[d]) if d < 3 else (act_last[0], peer_last[0])
        halves = jnp.where(c == 0, held, came), jnp.where(c == 0, came, held)
        for r in range(width // lanes):
            for h in range(2):
                act_buf[s ^ d, pl.ds(r * rows, rows), pl.ds(h * lanes, lanes)] = halves[h][
                    :, r * lanes : (r + 1) * lanes
                ]
    flat = cot_buf.shape[1:]
    at_end = jnp.logical_or(s == 0, s == count - 1)
    cot_buf[s] = cot_ref[:blocks].reshape(flat)
    cot_buf[s ^ 1] = beside[:blocks].reshape(flat)
    cot_buf[s ^ 3] = jnp.where(at_end, farthest[...], mirror[:blocks]).reshape(flat)
    cot_buf[s ^ 2] = jnp.where(at_end, beside2[2:], mirror2[2:]).reshape(flat)

    half = own_ref.shape[1]
    for t in range(3):
        low = max(0, 1 - t)
        high = min(count, count + 1 - t)
        for is_own, side in ((False, 1 - b), (True, b)):
            start = pl.multiple_of(side * half, half)
            total = None
            for j in range(low, high):
                term = jnp.dot(
                    act_buf[j + t - 1, pl.ds(start, half), :],
                    cot_buf[j],
                    preferred_element_type=F32,
                )
                total = term if total is None else total + term
            total = factor * total
            if is_own:
                own_ref[t] = total
            else:
                sent0_ref[t] = total[: half // 2].astype(BF)
                sent1_ref[t] = total[half // 2 :].astype(BF)


def add_kernel(own_ref, got0_ref, got1_ref, out_ref):
    half = got0_ref.shape[1]
    out_ref[:, :half] = own_ref[:, :half] + got0_ref[...].astype(F32)
    out_ref[:, half:] = own_ref[:, half:] + got1_ref[...].astype(F32)


def place_kernel(taken, *refs):
    pieces, outs, sems = refs[: len(taken)], refs[-4:-1], refs[-1]
    s = lax.axis_index("seq")
    pairs = [(piece.at[j], outs[j].at[s ^ d]) for piece, d in zip(pieces, taken) for j in range(3)]
    for copy in fetch(pairs, sems):
        copy.wait()


def swap(x, axis, by, only=None):
    n = lax.axis_size(axis)
    return lax.ppermute(x, axis, [(i, i ^ by) for i in range(n) if only is None or i in only])


def after(first, *then):
    held = lax.optimization_barrier((first, *then))
    return held[1:]


def per_device(query_vectors, key_vectors, value_vectors, hidden, cotangent, conv_weight):
    count = lax.axis_size("seq")
    blocks, rows, width = hidden.shape
    tokens = blocks * rows
    factor = 1.0 / math.sqrt(tokens * count * lax.axis_size("batch"))
    weights = conv_weight.transpose(1, 0, 2)
    part = width // 2
    middle, ends = (1, 2), (0, 3)

    def units(n):
        return shape((n, rows, width))

    to_beside, to_mirror = kernel_call(
        near_kernel,
        [units(blocks + 3)] * 2,
        name="near",
        scratch=[pltpu.SemaphoreType.DMA((8,))],
        space=pltpu.HBM,
    )(cotangent, query_vectors, key_vectors, value_vectors)
    beside = swap(to_beside, "seq", 1)
    mirror = swap(to_mirror, "seq", 3, middle)
    (hidden,) = after(to_beside, hidden)
    own_qkv, opposite_qkv, weights, slope, act, act_sent = kernel_call(
        rest_kernel,
        [units(3)] * 2 + [shape(weights.shape), shape(hidden.shape, F32), units(2), units(2)],
        name="rest",
        scratch=[pltpu.VMEM(hidden.shape, BF), pltpu.SemaphoreType.DMA((8,))],
        space=pltpu.HBM,
    )(hidden, query_vectors, key_vectors, value_vectors, weights)
    act_got = swap(act_sent, "chan", 1)
    flat = shape((tokens, width), F32)
    centre_mine, centre_other, to_opposite = kernel_call(
        centre_kernel, [flat, flat, units(4)], name="conv_centre"
    )(to_beside, weights, opposite_qkv, act, act_got)
    opposite = swap(to_opposite, "seq", 2)
    others = kernel_call(
        functools.partial(conv_kernel, False), [units(blocks // 2)] * 2, name="conv_other"
    )(beside, mirror, weights, centre_other)
    got = [swap(x, "chan", 1) for x in others]
    (centre_mine,) = after(others[0], centre_mine)
    (mine,) = kernel_call(functools.partial(conv_kernel, True), [units(blocks)], name="conv_mine")(
        beside, mirror, weights, centre_mine
    )
    own, to_beside2, to_opposite2, to_mirror2, to_end2 = kernel_call(
        grad_kernel,
        [units(2), units(blocks + 2), units(1), units(blocks + 2), units(5)],
        name="hidden_grad",
    )(to_beside, slope, mine, *got, act, act_got, beside, mirror, to_mirror)
    beside2 = swap(to_beside2, "seq", 1)
    mirror2 = swap(to_mirror2, "seq", 3, middle)
    far_opposite, far_end = after(opposite, to_opposite2, to_end2)
    opposite2 = swap(far_opposite, "seq", 2)
    end2 = swap(far_end, "seq", 3, ends)
    (far,) = kernel_call(pick_kernel, [units(blocks)], name="pick")(mirror2)
    farthest = lax.ppermute(far, "seq", [(1, 0), (2, 3)])

    (act_held,) = kernel_call(gather_kernel, [units(3)], name="gather")(own, beside2, opposite)
    act_peer = swap(act_held, "chan", 1)
    (own_qkv,) = after(act_held, own_qkv)

    item = 5 * (count * rows) ** 2 * width
    *returned, act_last = kernel_call(
        functools.partial(attention_kernel, count),
        [units(3)] * count + [units(1)],
        flops=COST * 2 * item,
        transcendentals=(count * rows) ** 2 * (width // HD),
        name="attention",
    )(own_qkv, own, beside, mirror, opposite, end2, beside2, mirror2, opposite2)
    back = {d: swap(returned[d], "seq", d) for d in (2, 1, 3)}

    peer_last = swap(act_last, "chan", 1)
    total, sent0, sent1, hidden_grad = kernel_call(
        functools.partial(weight_kernel, count, factor),
        [shape((3, part // 2, width), F32)] + [shape((3, part // 4, width))] * 2 + [units(blocks)],
        name="weight_grad",
        bytes_too=False,
        scratch=[
            pltpu.VMEM((count, part, tokens), BF),
            pltpu.VMEM((count, tokens, width), BF),
        ],
    )(
        to_beside, beside, mirror, beside2, mirror2, farthest, act_held, act_peer, act_last,
        peer_last, own, to_beside2, to_opposite2, to_mirror2,
    )
    got_sums = [swap(x, "batch", 1) for x in (sent0, sent1)]
    (weight_grad,) = kernel_call(add_kernel, [shape((3, part // 2, width), F32)], name="add_weight", bytes_too=False)(
        total, *got_sums
    )
    back[0] = returned[0]
    placed = ()
    for taken in ((0, 2, 1), (3,)):
        pieces = [back[d] for d in taken]
        if placed:
            (pieces[0],) = after(weight_grad, pieces[0])
        placed = kernel_call(
            functools.partial(place_kernel, taken),
            [units(blocks)] * 3,
            name="place",
            scratch=[pltpu.SemaphoreType.DMA((3 * len(taken),))],
            out_space=pltpu.HBM,
            space=pl.ANY,
            aliases={len(pieces) + j: j for j in range(len(placed))},
        )(*pieces, *placed)
    query_grad, key_grad, value_grad = placed
    return (query_grad, key_grad, value_grad, hidden_grad, weight_grad.transpose(1, 0, 2))


def from_behind(shard, axis, by):
    length = lax.axis_size(axis)
    pairs = [(i, i + by) for i in range(length) if 0 <= i + by < length]
    return lax.ppermute(shard, axis, pairs)


def per_device_general(query_vectors, key_vectors, value_vectors, hidden, cotangent, conv_weight):
    seq_count = lax.axis_size("seq")
    batch_count = lax.axis_size("batch")
    partner_gap = seq_count // 4
    blocks, row_count, local_width = hidden.shape
    tokens_all = blocks * batch_count * row_count * seq_count
    factor = 1.0 / math.sqrt(tokens_all)
    hidden_f = hidden.astype(jnp.float32)
    activation = tanh_gelu(hidden_f).astype(jnp.bfloat16)
    act_full = lax.all_gather(activation, "chan", axis=2, tiled=True)

    def partner(offset):
        return from_behind(cotangent, "seq", offset)

    cot_before = partner(partner_gap)
    cot_after = partner(-partner_gap)
    cot_taps = jnp.stack([cot_after, cotangent, cot_before])
    back_part = jnp.einsum(
        "tbqo,ito->bqi", cot_taps, conv_weight, preferred_element_type=jnp.float32
    )
    back_sum = lax.psum_scatter(
        back_part.astype(jnp.bfloat16), "chan", scatter_dimension=2, tiled=True
    ).astype(jnp.float32)
    hidden_grad = (cotangent.astype(jnp.float32) + back_sum * gelu_slope(hidden_f)).astype(
        jnp.bfloat16
    )
    weight_grad = lax.psum_scatter(
        factor
        * jnp.einsum("bpi,tbpo->ito", act_full, cot_taps, preferred_element_type=jnp.float32),
        ("seq", "batch"),
        scatter_dimension=0,
        tiled=True,
    )
    heads_local = local_width // HD

    def to_heads(signal):
        return signal.reshape(blocks, row_count, heads_local, HD)

    stacked = jnp.stack(
        [
            to_heads(query_vectors),
            to_heads(key_vectors),
            to_heads(value_vectors),
            to_heads(hidden_grad),
        ],
        axis=3,
    )
    stacked = stacked.transpose(0, 2, 1, 3, 4).reshape(
        seq_count, blocks * heads_local // seq_count, row_count, 4 * HD
    )
    gathered = lax.all_to_all(stacked, "seq", split_axis=0, concat_axis=2, tiled=True)
    item_count = gathered.shape[1]
    length = gathered.shape[2]
    columns = gathered[0].reshape(item_count, length, 4, HD)
    query_all = columns[:, :, 0]
    key_all = columns[:, :, 1]
    value_all = columns[:, :, 2]
    grad_all = columns[:, :, 3]
    score_scale = 1.0 / math.sqrt(HD)
    block_rows = math.gcd(length, 512)
    block_count = length // block_rows
    query_blocks = query_all.reshape(item_count, block_count, block_rows, HD).transpose(1, 0, 2, 3)
    grad_blocks = grad_all.reshape(item_count, block_count, block_rows, HD).transpose(1, 0, 2, 3)

    def query_block(carry, inputs):
        key_acc, value_acc = carry
        query_rows, grad_rows = inputs
        scores = (
            jnp.einsum("iqd,ikd->iqk", query_rows, key_all, preferred_element_type=jnp.float32)
            * score_scale
        )
        row_max = jnp.max(scores, axis=-1, keepdims=True)
        raised = jnp.exp(scores - row_max)
        probability = raised / jnp.sum(raised, axis=-1, keepdims=True)
        prob_b = probability.astype(jnp.bfloat16)
        value_acc = value_acc + jnp.einsum(
            "iqk,iqd->ikd", prob_b, grad_rows, preferred_element_type=jnp.float32
        )
        d_prob = jnp.einsum(
            "iqd,ikd->iqk", grad_rows, value_all, preferred_element_type=jnp.float32
        )
        row_total = jnp.sum(probability * d_prob, axis=-1, keepdims=True)
        d_score = (probability * (d_prob - row_total)).astype(jnp.bfloat16)
        query_out = (
            score_scale
            * jnp.einsum("iqk,ikd->iqd", d_score, key_all, preferred_element_type=jnp.float32)
        ).astype(jnp.bfloat16)
        key_acc = key_acc + jnp.einsum(
            "iqk,iqd->ikd", d_score, query_rows, preferred_element_type=jnp.float32
        )
        return ((key_acc, value_acc), query_out)

    empty_acc = jnp.zeros((item_count, length, HD), jnp.float32)
    (key_acc, value_acc), query_outs = lax.scan(
        query_block, (empty_acc, empty_acc), (query_blocks, grad_blocks)
    )
    query_out = query_outs.transpose(1, 0, 2, 3).reshape(item_count, length, HD)
    key_out = (score_scale * key_acc).astype(jnp.bfloat16)
    value_out = value_acc.astype(jnp.bfloat16)
    results = jnp.concatenate([query_out, key_out, value_out], axis=-1)[None]
    returned = lax.all_to_all(results, "seq", split_axis=2, concat_axis=0, tiled=True)
    returned = returned.reshape(blocks, heads_local, row_count, 3, HD).transpose(3, 0, 2, 1, 4)
    returned = returned.reshape(3, blocks, row_count, local_width)
    return (returned[0], returned[1], returned[2], hidden_grad, weight_grad)


def solution(mesh):
    token = P(("groups", "batch"), "seq", "chan")
    sizes = dict(mesh.shape)

    def run(*arrays):
        blocks = arrays[0].shape[0] // (sizes["groups"] * sizes["batch"])
        fits = blocks == sizes["seq"] == 4 and sizes["batch"] == 2 and sizes["chan"] == 2
        return jax.shard_map(
            per_device if fits else per_device_general,
            mesh=mesh,
            in_specs=(token,) * 5 + (P(None, None, "chan"),),
            out_specs=(token,) * 4 + (P(("groups", "seq", "batch"), None, "chan"),),
            check_vma=False,
        )(*arrays)

    return run
```

```python
import functools
import math

import jax
import jax.numpy as jnp
from jax import lax
from jax.experimental import pallas as pl
from jax.experimental.pallas import tpu as pltpu
from jax.sharding import PartitionSpec as P

HD = 96
BF = jnp.bfloat16
F32 = jnp.float32
COST = 8
VMEM_LIMIT = 40 * 1024 * 1024


def tanh_gelu(signal):
    inner_arg = 0.7978845608 * (signal + 0.044715 * signal * signal * signal)
    return 0.5 * signal * (1.0 + jnp.tanh(inner_arg))


def gelu_slope(signal):
    inner_arg = 0.7978845608 * (signal + 0.044715 * signal * signal * signal)
    hyper = jnp.tanh(inner_arg)
    return 0.5 * (1.0 + hyper) + 0.5 * signal * (1.0 - hyper * hyper) * 0.7978845608 * (
        1.0 + 3.0 * 0.044715 * signal * signal
    )


def kernel_call(
    body, outs, flops=0, transcendentals=0, name=None, scratch=(), space=pltpu.VMEM,
    out_space=pltpu.VMEM, bytes_too=True, aliases=None,
):
    given, made = (pl.BlockSpec(memory_space=x) for x in (space, out_space))

    def call(*args):
        if space == pltpu.HBM:
            args = [pltpu.with_memory_space_constraint(a, pltpu.HBM) for a in args]
        moved = sum(math.prod(a.shape) * a.dtype.itemsize for a in args)
        moved += sum(math.prod(o.shape) * o.dtype.itemsize for o in outs)
        return pl.pallas_call(
            body,
            out_shape=list(outs),
            in_specs=[given] * len(args),
            out_specs=[made] * len(outs),
            scratch_shapes=list(scratch),
            input_output_aliases=aliases or {},
            compiler_params=pltpu.CompilerParams(vmem_limit_bytes=VMEM_LIMIT),
            cost_estimate=pl.CostEstimate(
                flops=flops, bytes_accessed=moved * bytes_too, transcendentals=transcendentals
            ),
            name=name,
        )(*args)

    return call


def shape(dims, dtype=BF):
    return jax.ShapeDtypeStruct(dims, dtype)


def fetch(pairs, sems):
    copies = [pltpu.make_async_copy(src, dst, sems.at[i]) for i, (src, dst) in enumerate(pairs)]
    for copy in copies:
        copy.start()
    return copies


def near_kernel(cot, q, k, v, beside, mirror, sems):
    s = lax.axis_index("seq")
    blocks = cot.shape[0]
    pairs = []
    for out, d in ((beside, 1), (mirror, 3)):
        pairs.append((cot, out.at[pl.ds(0, blocks)]))
        pairs += [(x.at[s ^ d], out.at[blocks + j]) for j, x in enumerate((q, k, v))]
    for copy in fetch(pairs, sems):
        copy.wait()


def rest_kernel(hidden, q, k, v, w, own, opposite, w_ref, slope_ref, act_ref, sent_ref, h_ref, sems):
    s = lax.axis_index("seq")
    c = lax.axis_index("chan")
    pairs = [(hidden, h_ref)]
    for out, b in ((opposite, s ^ 2), (own, s)):
        pairs += [(x.at[b], out.at[j]) for j, x in enumerate((q, k, v))]
    pairs.append((w, w_ref))
    copies = fetch(pairs, sems)
    copies[0].wait()
    blocks, rows, width = h_ref.shape
    signal = h_ref[...].astype(F32)
    slope_ref[...] = gelu_slope(signal)
    act_t = tanh_gelu(signal).reshape(blocks * rows, width).T.astype(BF)
    lanes = act_t.shape[1] // 2
    parts = width // lanes
    halves = act_t[:, :lanes], act_t[:, lanes:]
    first = c == 0
    kept, sent = jnp.where(first, *halves), jnp.where(first, halves[1], halves[0])
    for out, half in ((act_ref, kept), (sent_ref, sent)):
        for i in range(2 * parts):
            out[i // parts, :, pl.ds(i % parts * lanes, lanes)] = half[i * rows : (i + 1) * rows]
    for copy in copies[1:]:
        copy.wait()


def conv_term(tap, w_ref, t, side):
    width = w_ref.shape[2]
    start = pl.multiple_of(side * width, width)
    return lax.dot_general(
        tap,
        w_ref[t, pl.ds(start, width), :],
        (((1,), (1,)), ((), ())),
        preferred_element_type=F32,
    )


def chosen(block, act_ref, act_peer):
    k = lax.rem(block, 2)
    return jnp.where(lax.div(block, 2) == lax.axis_index("chan"), act_ref[k], act_peer[k])


def centre_kernel(cot_ref, w_ref, qkv, act_ref, act_peer, mine_ref, other_ref, opposite):
    c = lax.axis_index("chan")
    blocks = cot_ref.shape[0] - 3
    opposite[:3] = qkv[...]
    opposite[3] = chosen(lax.axis_index("seq") ^ 2, act_ref, act_peer)
    tap = cot_ref[:blocks].reshape(mine_ref.shape)
    mine_ref[...] = conv_term(tap, w_ref, 1, c)
    other_ref[...] = conv_term(tap, w_ref, 1, 1 - c)


def conv_kernel(mine, beside_ref, mirror_ref, w_ref, centre_ref, *outs):
    c = lax.axis_index("chan")
    even = lax.rem(lax.axis_index("seq"), 2) == 0
    blocks = beside_ref.shape[0] - 3
    beside = beside_ref[:blocks].reshape(centre_ref.shape)
    mirror = mirror_ref[:blocks].reshape(centre_ref.shape)
    side = c if mine else 1 - c
    total = (
        centre_ref[...]
        + conv_term(jnp.where(even, beside, mirror), w_ref, 0, side)
        + conv_term(jnp.where(even, mirror, beside), w_ref, 2, side)
    ).astype(BF)
    rows = total.shape[0] // len(outs)
    for i, out in enumerate(outs):
        out[...] = total[i * rows : (i + 1) * rows].reshape(out.shape)


def grad_kernel(
    cot_ref, slope_ref, mine_ref, got0_ref, got1_ref, act_ref, act_peer, beside_ref, mirror_ref,
    to_mirror, own, beside, opposite, mirror, end,
):
    s = lax.axis_index("seq")
    blocks = mine_ref.shape[0]
    for d, out in ((1, beside), (3, mirror), (2, opposite), (0, own)):
        b = s ^ d
        i = lax.rem(b, 2)
        got = jnp.where(b < 2, got0_ref[i], got1_ref[i])
        back = mine_ref[b].astype(F32) + got.astype(F32)
        out[0] = (cot_ref[b].astype(F32) + back * slope_ref[b]).astype(BF)
        if d != 2:
            out[1] = chosen(b, act_ref, act_peer)
    end[:3] = to_mirror[blocks:]
    end[3:] = mirror[:2]
    beside[2:] = mirror_ref[:blocks]
    mirror[2:] = beside_ref[:blocks]


def pick_kernel(held_ref, out_ref):
    out_ref[...] = held_ref[2:]


def gather_kernel(own, beside, opposite, out_ref):
    for d, piece in enumerate((own[1], beside[1], opposite[3])):
        out_ref[d] = piece


def attention_kernel(
    count, own_qkv, own, beside_qkv, mirror_qkv, opposite_qkv, end, beside, mirror, opposite, *outs
):
    outs, act_ref = outs[:count], outs[count]
    rows, width = own.shape[1:]
    near = beside_qkv.shape[0] - 3
    scale = 1.0 / math.sqrt(HD)
    s = lax.axis_index("seq")
    at_end = jnp.logical_or(s == 0, s == count - 1)

    def positions(j):
        facing = jnp.where(at_end, end[j], mirror_qkv[near + j])
        return jnp.concatenate([own_qkv[j], beside_qkv[near + j], opposite_qkv[j], facing], axis=0)

    query, key, value = (positions(j) for j in range(3))
    facing, act_ref[0] = (jnp.where(at_end, end[3 + j], mirror[j]) for j in range(2))
    grad = jnp.concatenate([own[0], beside[0], opposite[0], facing], axis=0)
    nt = (((1,), (1,)), ((), ()))
    nn = (((1,), (0,)), ((), ()))
    tn = (((0,), (0,)), ((), ()))
    dot = functools.partial(lax.dot_general, preferred_element_type=F32)
    tile = 128
    lane = lax.broadcasted_iota(jnp.int32, (1, width), 1)
    windows, heads = [], []
    for h in range(width // HD):
        low, high = h * HD // tile * tile, -(-(h + 1) * HD // tile) * tile
        inside = jnp.logical_and(lane >= h * HD, lane < (h + 1) * HD).astype(F32).astype(BF)[:, low:high]
        windows.append((low, high))
        q, k, v, g = (x[:, low:high] for x in (query, key, value, grad))
        heads.append((q, k, k * inside, v * inside, g))
    scores = [dot(k, q, nt) for q, _, k, _, _ in heads]
    d_probs = [dot(v, g, nt) for _, _, _, v, g in heads]
    power = scale * math.log2(math.e)
    raised = [jnp.exp2((x - jnp.max(x, axis=0, keepdims=True)) * power) for x in scores]
    probs = [x * (1.0 / jnp.sum(x, axis=0, keepdims=True)) for x in raised]
    v_grads = [dot(p.astype(BF), x[4], nn) for p, x in zip(probs, heads)]
    totals = [jnp.sum(p * d, axis=0, keepdims=True) for p, d in zip(probs, d_probs)]
    d_scores = [(p * (d - t)).astype(BF) for p, d, t in zip(probs, d_probs, totals)]
    k_grads = [dot(d, x[0], nn) * scale for d, x in zip(d_scores, heads)]
    q_grads = [dot(d, x[1], tn) * scale for d, x in zip(d_scores, heads)]
    for j, results in enumerate((q_grads, k_grads, v_grads)):
        for at in range(0, width, tile):
            whole = None
            for h, ((low, high), x) in enumerate(zip(windows, results)):
                if low <= at < high:
                    part = x[:, at - low : at - low + tile]
                    whole = part if whole is None else jnp.where(lane[:, at : at + tile] < h * HD, whole, part)
            whole = whole.astype(BF)
            for d in range(count):
                outs[d][j, :, at : at + tile] = whole[d * rows : (d + 1) * rows]


def weight_kernel(
    count, factor, cot_ref, beside, mirror, beside2, mirror2, farthest, act_ref, act_peer,
    act_last, peer_last, own, to_beside, to_opposite, to_mirror, own_ref, sent0_ref, sent1_ref, grad_ref, act_buf, cot_buf,
):
    s = lax.axis_index("seq")
    c = lax.axis_index("chan")
    b = lax.axis_index("batch")
    blocks, rows, width = grad_ref.shape
    for d, piece in enumerate((own, to_beside, to_opposite, to_mirror)):
        grad_ref[s ^ d] = piece[0]
    lanes = act_buf.shape[2] // 2
    for d in range(count):
        held, came = (act_ref[d], act_peer[d]) if d < 3 else (act_last[0], peer_last[0])
        halves = jnp.where(c == 0, held, came), jnp.where(c == 0, came, held)
        for r in range(width // lanes):
            for h in range(2):
                act_buf[s ^ d, pl.ds(r * rows, rows), pl.ds(h * lanes, lanes)] = halves[h][
                    :, r * lanes : (r + 1) * lanes
                ]
    flat = cot_buf.shape[1:]
    at_end = jnp.logical_or(s == 0, s == count - 1)
    cot_buf[s] = cot_ref[:blocks].reshape(flat)
    cot_buf[s ^ 1] = beside[:blocks].reshape(flat)
    cot_buf[s ^ 3] = jnp.where(at_end, farthest[...], mirror[:blocks]).reshape(flat)
    cot_buf[s ^ 2] = jnp.where(at_end, beside2[2:], mirror2[2:]).reshape(flat)

    half = own_ref.shape[1]
    for t in range(3):
        low = max(0, 1 - t)
        high = min(count, count + 1 - t)
        total = None
        for j in range(low, high):
            term = jnp.dot(act_buf[j + t - 1], cot_buf[j], preferred_element_type=F32)
            total = term if total is None else total + term
        total = factor * total
        lower, upper = total[:half], total[half:]
        own_ref[t] = jnp.where(b == 0, lower, upper)
        sent = jnp.where(b == 0, upper, lower).astype(BF)
        sent0_ref[t] = sent[: half // 2]
        sent1_ref[t] = sent[half // 2 :]


def add_kernel(own_ref, got0_ref, got1_ref, out_ref):
    half = got0_ref.shape[1]
    out_ref[:, :half] = own_ref[:, :half] + got0_ref[...].astype(F32)
    out_ref[:, half:] = own_ref[:, half:] + got1_ref[...].astype(F32)


def place_kernel(taken, *refs):
    pieces, outs, sems = refs[: len(taken)], refs[-4:-1], refs[-1]
    s = lax.axis_index("seq")
    pairs = [(piece.at[j], outs[j].at[s ^ d]) for piece, d in zip(pieces, taken) for j in range(3)]
    for copy in fetch(pairs, sems):
        copy.wait()


def swap(x, axis, by, only=None):
    n = lax.axis_size(axis)
    return lax.ppermute(x, axis, [(i, i ^ by) for i in range(n) if only is None or i in only])


def after(first, *then):
    held = lax.optimization_barrier((first, *then))
    return held[1:]


def per_device(query_vectors, key_vectors, value_vectors, hidden, cotangent, conv_weight):
    count = lax.axis_size("seq")
    blocks, rows, width = hidden.shape
    tokens = blocks * rows
    factor = 1.0 / math.sqrt(tokens * count * lax.axis_size("batch"))
    weights = conv_weight.transpose(1, 0, 2)
    part = width // 2
    middle, ends = (1, 2), (0, 3)

    def units(n):
        return shape((n, rows, width))

    to_beside, to_mirror = kernel_call(
        near_kernel,
        [units(blocks + 3)] * 2,
        name="near",
        scratch=[pltpu.SemaphoreType.DMA((8,))],
        space=pltpu.HBM,
    )(cotangent, query_vectors, key_vectors, value_vectors)
    beside = swap(to_beside, "seq", 1)
    mirror = swap(to_mirror, "seq", 3, middle)
    (hidden,) = after(to_beside, hidden)
    own_qkv, opposite_qkv, weights, slope, act, act_sent = kernel_call(
        rest_kernel,
        [units(3)] * 2 + [shape(weights.shape), shape(hidden.shape, F32), units(2), units(2)],
        name="rest",
        scratch=[pltpu.VMEM(hidden.shape, BF), pltpu.SemaphoreType.DMA((8,))],
        space=pltpu.HBM,
    )(hidden, query_vectors, key_vectors, value_vectors, weights)
    act_got = swap(act_sent, "chan", 1)
    flat = shape((tokens, width), F32)
    centre_mine, centre_other, to_opposite = kernel_call(
        centre_kernel, [flat, flat, units(4)], name="conv_centre"
    )(to_beside, weights, opposite_qkv, act, act_got)
    opposite = swap(to_opposite, "seq", 2)
    others = kernel_call(
        functools.partial(conv_kernel, False), [units(blocks // 2)] * 2, name="conv_other"
    )(beside, mirror, weights, centre_other)
    got = [swap(x, "chan", 1) for x in others]
    (centre_mine,) = after(others[0], centre_mine)
    (mine,) = kernel_call(functools.partial(conv_kernel, True), [units(blocks)], name="conv_mine")(
        beside, mirror, weights, centre_mine
    )
    own, to_beside2, to_opposite2, to_mirror2, to_end2 = kernel_call(
        grad_kernel,
        [units(2), units(blocks + 2), units(1), units(blocks + 2), units(5)],
        name="hidden_grad",
    )(to_beside, slope, mine, *got, act, act_got, beside, mirror, to_mirror)
    beside2 = swap(to_beside2, "seq", 1)
    mirror2 = swap(to_mirror2, "seq", 3, middle)
    far_opposite, far_end = after(opposite, to_opposite2, to_end2)
    opposite2 = swap(far_opposite, "seq", 2)
    end2 = swap(far_end, "seq", 3, ends)
    (far,) = kernel_call(pick_kernel, [units(blocks)], name="pick")(mirror2)
    farthest = lax.ppermute(far, "seq", [(1, 0), (2, 3)])

    (act_held,) = kernel_call(gather_kernel, [units(3)], name="gather")(own, beside2, opposite)
    act_peer = swap(act_held, "chan", 1)
    (own_qkv,) = after(act_held, own_qkv)

    item = 5 * (count * rows) ** 2 * width
    *returned, act_last = kernel_call(
        functools.partial(attention_kernel, count),
        [units(3)] * count + [units(1)],
        flops=COST * 2 * item,
        transcendentals=(count * rows) ** 2 * (width // HD),
        name="attention",
    )(own_qkv, own, beside, mirror, opposite, end2, beside2, mirror2, opposite2)
    back = {d: swap(returned[d], "seq", d) for d in (2, 1, 3)}

    peer_last = swap(act_last, "chan", 1)
    total, sent0, sent1, hidden_grad = kernel_call(
        functools.partial(weight_kernel, count, factor),
        [shape((3, part // 2, width), F32)] + [shape((3, part // 4, width))] * 2 + [units(blocks)],
        name="weight_grad",
        bytes_too=False,
        scratch=[
            pltpu.VMEM((count, part, tokens), BF),
            pltpu.VMEM((count, tokens, width), BF),
        ],
    )(
        to_beside, beside, mirror, beside2, mirror2, farthest, act_held, act_peer, act_last,
        peer_last, own, to_beside2, to_opposite2, to_mirror2,
    )
    got_sums = [swap(x, "batch", 1) for x in (sent0, sent1)]
    (weight_grad,) = kernel_call(add_kernel, [shape((3, part // 2, width), F32)], name="add_weight", bytes_too=False)(
        total, *got_sums
    )
    back[0] = returned[0]
    placed = ()
    for taken in ((0, 2, 1), (3,)):
        pieces = [back[d] for d in taken]
        if placed:
            (pieces[0],) = after(weight_grad, pieces[0])
        placed = kernel_call(
            functools.partial(place_kernel, taken),
            [units(blocks)] * 3,
            name="place",
            scratch=[pltpu.SemaphoreType.DMA((3 * len(taken),))],
            out_space=pltpu.HBM,
            space=pl.ANY,
            aliases={len(pieces) + j: j for j in range(len(placed))},
        )(*pieces, *placed)
    query_grad, key_grad, value_grad = placed
    return (query_grad, key_grad, value_grad, hidden_grad, weight_grad.transpose(1, 0, 2))


def from_behind(shard, axis, by):
    length = lax.axis_size(axis)
    pairs = [(i, i + by) for i in range(length) if 0 <= i + by < length]
    return lax.ppermute(shard, axis, pairs)


def per_device_general(query_vectors, key_vectors, value_vectors, hidden, cotangent, conv_weight):
    seq_count = lax.axis_size("seq")
    batch_count = lax.axis_size("batch")
    partner_gap = seq_count // 4
    blocks, row_count, local_width = hidden.shape
    tokens_all = blocks * batch_count * row_count * seq_count
    factor = 1.0 / math.sqrt(tokens_all)
    hidden_f = hidden.astype(jnp.float32)
    activation = tanh_gelu(hidden_f).astype(jnp.bfloat16)
    act_full = lax.all_gather(activation, "chan", axis=2, tiled=True)

    def partner(offset):
        return from_behind(cotangent, "seq", offset)

    cot_before = partner(partner_gap)
    cot_after = partner(-partner_gap)
    cot_taps = jnp.stack([cot_after, cotangent, cot_before])
    back_part = jnp.einsum(
        "tbqo,ito->bqi", cot_taps, conv_weight, preferred_element_type=jnp.float32
    )
    back_sum = lax.psum_scatter(
        back_part.astype(jnp.bfloat16), "chan", scatter_dimension=2, tiled=True
    ).astype(jnp.float32)
    hidden_grad = (cotangent.astype(jnp.float32) + back_sum * gelu_slope(hidden_f)).astype(
        jnp.bfloat16
    )
    weight_grad = lax.psum_scatter(
        factor
        * jnp.einsum("bpi,tbpo->ito", act_full, cot_taps, preferred_element_type=jnp.float32),
        ("seq", "batch"),
        scatter_dimension=0,
        tiled=True,
    )
    heads_local = local_width // HD

    def to_heads(signal):
        return signal.reshape(blocks, row_count, heads_local, HD)

    stacked = jnp.stack(
        [
            to_heads(query_vectors),
            to_heads(key_vectors),
            to_heads(value_vectors),
            to_heads(hidden_grad),
        ],
        axis=3,
    )
    stacked = stacked.transpose(0, 2, 1, 3, 4).reshape(
        seq_count, blocks * heads_local // seq_count, row_count, 4 * HD
    )
    gathered = lax.all_to_all(stacked, "seq", split_axis=0, concat_axis=2, tiled=True)
    item_count = gathered.shape[1]
    length = gathered.shape[2]
    columns = gathered[0].reshape(item_count, length, 4, HD)
    query_all = columns[:, :, 0]
    key_all = columns[:, :, 1]
    value_all = columns[:, :, 2]
    grad_all = columns[:, :, 3]
    score_scale = 1.0 / math.sqrt(HD)
    block_rows = math.gcd(length, 512)
    block_count = length // block_rows
    query_blocks = query_all.reshape(item_count, block_count, block_rows, HD).transpose(1, 0, 2, 3)
    grad_blocks = grad_all.reshape(item_count, block_count, block_rows, HD).transpose(1, 0, 2, 3)

    def query_block(carry, inputs):
        key_acc, value_acc = carry
        query_rows, grad_rows = inputs
        scores = (
            jnp.einsum("iqd,ikd->iqk", query_rows, key_all, preferred_element_type=jnp.float32)
            * score_scale
        )
        row_max = jnp.max(scores, axis=-1, keepdims=True)
        raised = jnp.exp(scores - row_max)
        probability = raised / jnp.sum(raised, axis=-1, keepdims=True)
        prob_b = probability.astype(jnp.bfloat16)
        value_acc = value_acc + jnp.einsum(
            "iqk,iqd->ikd", prob_b, grad_rows, preferred_element_type=jnp.float32
        )
        d_prob = jnp.einsum(
            "iqd,ikd->iqk", grad_rows, value_all, preferred_element_type=jnp.float32
        )
        row_total = jnp.sum(probability * d_prob, axis=-1, keepdims=True)
        d_score = (probability * (d_prob - row_total)).astype(jnp.bfloat16)
        query_out = (
            score_scale
            * jnp.einsum("iqk,ikd->iqd", d_score, key_all, preferred_element_type=jnp.float32)
        ).astype(jnp.bfloat16)
        key_acc = key_acc + jnp.einsum(
            "iqk,iqd->ikd", d_score, query_rows, preferred_element_type=jnp.float32
        )
        return ((key_acc, value_acc), query_out)

    empty_acc = jnp.zeros((item_count, length, HD), jnp.float32)
    (key_acc, value_acc), query_outs = lax.scan(
        query_block, (empty_acc, empty_acc), (query_blocks, grad_blocks)
    )
    query_out = query_outs.transpose(1, 0, 2, 3).reshape(item_count, length, HD)
    key_out = (score_scale * key_acc).astype(jnp.bfloat16)
    value_out = value_acc.astype(jnp.bfloat16)
    results = jnp.concatenate([query_out, key_out, value_out], axis=-1)[None]
    returned = lax.all_to_all(results, "seq", split_axis=2, concat_axis=0, tiled=True)
    returned = returned.reshape(blocks, heads_local, row_count, 3, HD).transpose(3, 0, 2, 1, 4)
    returned = returned.reshape(3, blocks, row_count, local_width)
    return (returned[0], returned[1], returned[2], hidden_grad, weight_grad)


def solution(mesh):
    token = P(("groups", "batch"), "seq", "chan")
    sizes = dict(mesh.shape)

    def run(*arrays):
        blocks = arrays[0].shape[0] // (sizes["groups"] * sizes["batch"])
        fits = blocks == sizes["seq"] == 4 and sizes["batch"] == 2 and sizes["chan"] == 2
        return jax.shard_map(
            per_device if fits else per_device_general,
            mesh=mesh,
            in_specs=(token,) * 5 + (P(None, None, "chan"),),
            out_specs=(token,) * 4 + (P(("groups", "seq", "batch"), None, "chan"),),
            check_vma=False,
        )(*arrays)

    return run
```
